256 devices in a mesh: tile: 64 (over y, x_hi, z), mem: 4 (over x_lo, core).
Axes of the slice: x: 4 (x_hi: 2, x_lo: 2; x = x_hi * 2 + x_lo), y: 4, z: 8, core: 2. Of those that a mesh axis runs over, the one named last changes fastest.
Arguments:
- prior: float32 [64, 256, 48, 128], P('mem', 'tile'), may hold values from -1 to 1
- base_flow: float32 [256, 48, 128], P('tile'), may hold values from -4 to 4
- base_visc: float32 [256, 48, 128], P('tile'), may hold values from 0.02 to 0.05
- probe_cells: int32 [64, 4], P('tile'), may hold values from 0 to 24575
- obs_slot: int32 [256], replicated, may hold values from 0 to 255, each once
- obs_values: float32 [256], replicated, may hold values from -6 to 6
- obs_var: float32 [256], replicated, may hold values from 0.05 to 0.5
- obs_noise: float32 [64, 256], replicated, may hold values from -5 to 5
Outputs:
- velocity: float32 [64, 256, 48, 128], P('mem', 'tile')
- posterior: float32 [64, 256, 48, 128], P('mem', 'tile')
The draws below stay inside these ranges and needn't reach their ends.
Inputs may be any that keep to these rules, and one draw needn't show every extreme that they name: `obs_slot`: each slot appears once.
All inputs are finite; a program needn't handle non-finite values.
Results may differ from the reference program's by a relative error of at most 0.00095.
The reference program's roundings to bfloat16 on the way (of `weights` and `anomaly`) count: a program that leaves them out, or rounds other values in their place, can miss the bound.
Values may be sent and summed in bfloat16 or wider, within the bound.
No kernel may reach another device: no remote copies, remote signals or barrier semaphores. Data moves between devices by JAX's collectives and lax.ppermute only.
A program may use at most 64 MiB of HBM per device.

```python
import math
import jax
import jax.numpy as jnp
from jax import lax

CX = 4
NZ = 48
NY = 128
P_DEV = 4
ITERS = 4
NX = 256
M = 64
NOBS = 256
N_TILE = 64


def plant(result, stream_key, least, high):
    longest = result.shape.index(max(result.shape))
    spots = []
    for shift in (0, 1):
        where = [jax.random.randint(jax.random.fold_in(stream_key, axis), (), 0, length) for axis, length in enumerate(result.shape)]
        where[longest] = (where[longest] + shift) % result.shape[longest]
        spots.append(tuple(where))
    return result.at[spots[0]].set(least).at[spots[1]].set(high)


def steps_of(stream_key, shape, split, low, largest):
    level = 1.0
    for position, blocks in split:
        heights = jax.random.uniform(jax.random.fold_in(jax.random.fold_in(stream_key, 6), position), (blocks,), jnp.float32, low / len(split), largest / len(split))
        level = level * jnp.repeat(jnp.exp(heights), shape[position] // blocks).reshape((-1,) + (1,) * (len(shape) - 1 - position))
    return level


def gaussian(rng, shape, scale, limit, cuts=(), held_as=jnp.bfloat16):
    drawn = scale * jax.random.normal(rng, shape, jnp.float32)
    if cuts:
        drawn = drawn * steps_of(rng, shape, cuts, -0.22, 0.18)
    return jnp.clip(drawn, -limit, limit).astype(held_as)


def setup_inputs(seed: int = 0) -> dict:
    key_of = jax.random.split(jax.random.key(seed), 9)
    prior = jnp.clip(jax.random.uniform(key_of[0], (M, NX, NZ, NY), jnp.float32, -1.0, 1.0) * steps_of(key_of[0], (M, NX, NZ, NY), ((0, 4), (1, 64)), -0.4, 0.0), -1.0, 1.0)
    base_flow = gaussian(key_of[1], (NX, NZ, NY), 1.0, 4.0, ((0, 64),), jnp.float32)
    base_visc = jnp.clip(0.02 + 0.030000001 * jax.random.uniform(key_of[2], (NX, NZ, NY), jnp.float32) ** steps_of(key_of[2], (NX, NZ, NY), ((0, 64),), -0.2, 0.2), 0.02, 0.05)
    probe_cells = plant(jax.random.randint(key_of[3], (N_TILE, P_DEV), 0, CX * NZ * NY), jax.random.fold_in(key_of[3], 1), 0, (CX * NZ * NY) - 1).astype(jnp.int32)
    obs_slot = jax.random.permutation(key_of[4], NOBS).astype(jnp.int32)
    obs_values = gaussian(key_of[5], (NOBS,), 1.0, 6.0, (), jnp.float32)
    obs_var = jnp.clip(jnp.exp(jax.random.uniform(key_of[6], (NOBS,), jnp.float32, math.log(0.05), math.log(0.5))), 0.05, 0.5)
    obs_noise = gaussian(key_of[7], (M, NOBS), 1.0, 5.0, (), jnp.float32)
    return dict(prior=prior, base_flow=base_flow, base_visc=base_visc, probe_cells=probe_cells, obs_slot=obs_slot, obs_values=obs_values, obs_var=obs_var, obs_noise=obs_noise)


def relax_step(centre, behind, ahead, viscosity):
    spanwise = jnp.roll(centre, 1, -2) + jnp.roll(centre, -1, -2)
    widths = [(0, 0)] * (centre.ndim - 1) + [(1, 1)]
    padded = jnp.pad(centre, widths)
    normal = padded[..., 2:] + padded[..., :-2]
    laplace = behind + ahead + spanwise + normal - 6.0 * centre
    return centre + viscosity * laplace - 0.15 * (centre - behind) + 0.01

def reference(prior, base_flow, base_visc, probe_cells, obs_slot, obs_values, obs_var, obs_noise):

    def one_member(field):
        viscosity = base_visc * jnp.exp(field)
        speed = base_flow
        for sweep in range(ITERS):
            speed = relax_step(speed, jnp.roll(speed, 1, 0), jnp.roll(speed, -1, 0), viscosity)
        return speed
    velocity = lax.map(one_member, prior)
    blocks = velocity.reshape(M, N_TILE, CX * NZ * NY)
    probes = jnp.take_along_axis(blocks, probe_cells[None, :, :], axis=2).reshape(M, NOBS)
    predicted = probes[:, obs_slot]
    spread_obs = predicted - lax.optimization_barrier(jnp.sum(predicted, 0)) / M
    scaled = spread_obs / obs_var[None, :]
    gram = jnp.dot(scaled, spread_obs.T, precision=lax.Precision.HIGHEST) + (M - 1.0) * jnp.eye(M, dtype=jnp.float32)
    innovation = obs_values[None, :] + jnp.sqrt(obs_var)[None, :] * obs_noise - predicted
    rhs = jnp.dot(scaled, innovation.T, precision=lax.Precision.HIGHEST)
    weights = jnp.linalg.solve(gram, rhs).astype(jnp.bfloat16)
    anomaly = (prior - lax.optimization_barrier(jnp.sum(prior, 0)) / M).astype(jnp.bfloat16)
    update = jnp.einsum('km,kxzy->mxzy', weights.astype(jnp.float32), anomaly.astype(jnp.float32))
    return (velocity, prior + update)
```

```python
import functools
import math

import jax
import jax.numpy as jnp
from jax import lax
from jax.experimental import pallas as pl
from jax.experimental.pallas import tpu as pltpu
from jax.sharding import PartitionSpec as P

ITERS = 4
CHUNKS = 2
GROUP = 4
LOG_MID = 0.5 * (math.log(0.02) + math.log(0.05))
LOG_HALF = 0.5 * (math.log(0.05) - math.log(0.02)) + 1.0
NU_SCALE = 124.0 / LOG_HALF
FLOW_SCALE = 31.0
LN2 = math.log(2.0)
VMEM = pl.BlockSpec(memory_space=pltpu.VMEM)
SMEM = pl.BlockSpec(memory_space=pltpu.SMEM)
F32 = jnp.float32
BF16 = jnp.bfloat16


def params(mib=48):
    return pltpu.CompilerParams(vmem_limit_bytes=mib * 1024 * 1024)


def power(x):
    return jnp.exp(x * LN2)


def log2_of(x):
    return jnp.log(x) * (1.0 / LN2)


def encode_kernel(base_slabs, prior_ref, flow_ref, visc_ref, sum_ref, right_ref, left_ref, total_ref, base):
    layers = prior_ref.shape[1]
    base[...] = jnp.log(visc_ref[...]) * NU_SCALE - LOG_MID * NU_SCALE
    if base_slabs:
        for l in range(layers):
            code = power(flow_ref[l] * FLOW_SCALE).astype(BF16)
            right_ref[l] = code
            left_ref[l] = code
    total_ref[...] = sum_ref[...] if sum_ref is not None else jnp.zeros_like(total_ref)

    def member(m, carry):
        for l in range(layers):
            field = prior_ref[m, l]
            total_ref[l] += field
            code = power(field * NU_SCALE + base[l]).astype(BF16)
            if l >= 1:
                right_ref[base_slabs + m * 3 + l - 1] = code
            if l < 3:
                left_ref[base_slabs + m * 3 + l] = code
        return carry

    lax.fori_loop(0, prior_ref.shape[0], member, 0)


def encode(prior, flow, visc, chunk, before):
    members, layers, nz, ny = prior.shape
    part = members // CHUNKS
    base_slabs = layers if chunk == 0 else 0
    slabs = base_slabs + 3 * part
    whole = lambda shape: pl.BlockSpec(shape, lambda i: (0,) * len(shape))
    args = [prior, flow, visc]
    specs = [
        pl.BlockSpec((part, layers, nz, ny), lambda i: (chunk, 0, 0, 0)),
        whole(flow.shape),
        whole(visc.shape),
    ]
    body = functools.partial(encode_kernel, base_slabs)
    if before is None:
        kernel = lambda p, f, v, *rest: body(p, f, v, None, *rest)
    else:
        kernel = body
        args.append(before)
        specs.append(whole(before.shape))
    return pl.pallas_call(
        kernel,
        grid=(1,),
        in_specs=specs,
        out_specs=[whole((slabs, nz, ny)), whole((slabs, nz, ny)), whole((layers, nz, ny))],
        out_shape=[
            jax.ShapeDtypeStruct((slabs, nz, ny), BF16),
            jax.ShapeDtypeStruct((slabs, nz, ny), BF16),
            jax.ShapeDtypeStruct((layers, nz, ny), F32),
        ],
        scratch_shapes=[pltpu.VMEM((layers, nz, ny), F32)],
        compiler_params=params(),
        name=f"encode{chunk}",
    )(*args)


def neighbours(buf, l, centre, nz, ny):
    lane = lax.broadcasted_iota(jnp.int32, centre.shape, 1)
    below = jnp.where(lane == 0, 0.0, pltpu.roll(centre, 1, 1))
    above = jnp.where(lane == ny - 1, 0.0, pltpu.roll(centre, ny - 1, 1))
    return (buf[l, 7 : 7 + nz] + buf[l, 9 : 9 + nz]) + (below + above)


def put(buf, l, value, nz):
    buf[l, 8 : 8 + nz] = value
    buf[l, 7:8] = value[nz - 1 : nz]
    buf[l, 8 + nz : 9 + nz] = value[0:1]


def sweep_kernel(
    chunk, base_slabs, devices, *refs
):
    cells_ref, prior_ref, flow_ref, visc_ref, behind_base, ahead_base, behind_ref, ahead_ref = refs[:8]
    rest = refs[8:]
    if chunk:
        rows_in, _, out_ref, rows_out, buf0, buf1, lap0, adv0, nu, rows = rest
    else:
        out_ref, rows_out, buf0, buf1, lap0, adv0, nu, rows = rest
    step = pl.program_id(0)
    group, layers, nz, ny = prior_ref.shape
    wide = layers + 2 * ITERS

    @pl.when(step == 0)
    def _():
        for l in range(ITERS):
            put(buf0, l, log2_of(behind_base[l].astype(F32)) * (1.0 / FLOW_SCALE), nz)
            put(buf0, ITERS + layers + l, log2_of(ahead_base[l].astype(F32)) * (1.0 / FLOW_SCALE), nz)
        for l in range(layers):
            put(buf0, ITERS + l, flow_ref[l], nz)
        for l in range(1, wide - 1):
            centre, back = buf0[l, 8 : 8 + nz], buf0[l - 1, 8 : 8 + nz]
            sides = back + buf0[l + 1, 8 : 8 + nz] + neighbours(buf0, l, centre, nz, ny)
            lap0[l - 1] = sides - 6.0 * centre
            adv0[l - 1] = centre - 0.15 * (centre - back) + 0.01

    def member(m, carry):
        first = base_slabs + (step * group + m) * 3
        for l in range(3):
            behind = behind_ref[first + l].astype(F32)
            nu[l] = jnp.exp(jnp.log(behind) * (1.0 / (LN2 * NU_SCALE)) + LOG_MID)
            ahead = ahead_ref[first + l].astype(F32)
            nu[3 + layers + l] = jnp.exp(jnp.log(ahead) * (1.0 / (LN2 * NU_SCALE)) + LOG_MID)
        for l in range(layers):
            nu[3 + l] = visc_ref[l] * jnp.exp(prior_ref[m, l])
        for l in range(1, wide - 1):
            put(buf1, l, adv0[l - 1] + nu[l - 1] * lap0[l - 1], nz)
        src, dst = buf1, buf0
        for sweep in range(1, ITERS):
            low, high = sweep + 1, wide - sweep - 1
            back, centre = src[low - 1, 8 : 8 + nz], src[low, 8 : 8 + nz]
            for l in range(low, high):
                front = src[l + 1, 8 : 8 + nz]
                lap = back + front + neighbours(src, l, centre, nz, ny) - 6.0 * centre
                value = centre + nu[l - 1] * lap - 0.15 * (centre - back) + 0.01
                if sweep == ITERS - 1:
                    out_ref[m, l - ITERS] = value
                else:
                    put(dst, l, value, nz)
                back, centre = centre, front
            src, dst = dst, src
        for s in range(4):
            cell = cells_ref[0, s]
            layer, z = cell // (nz * ny), lax.rem(cell, nz * ny) // ny
            rows[pl.ds(s * 16 + chunk * group * pl.num_programs(0) + step * group + m, 1), :] = out_ref[m, layer, pl.ds(z, 1), :]
        return carry

    if chunk:

        @pl.when(step == 0)
        def _():
            rows[...] = rows_in[...]

    lax.fori_loop(0, group, member, 0)

    @pl.when(step == pl.num_programs(0) - 1)
    def _():
        if chunk == 0:
            rows_out[...] = rows[...]
        else:
            lane = lax.broadcasted_iota(jnp.int32, (64, ny), 1)
            row = lax.broadcasted_iota(jnp.int32, (64, ny), 0)
            y = jnp.zeros((64, ny), jnp.int32)
            for s in range(4):
                y = jnp.where(row // 16 == s, lax.rem(cells_ref[0, s], ny), y)
            picked = jnp.sum(jnp.where(lane == y, rows[...], 0.0), axis=1, keepdims=True)
            line = jnp.sum(jnp.where(lane == row, picked, 0.0), axis=0, keepdims=True)
            rows_out[...] = jnp.broadcast_to(line, (devices, ny))


def sweeps(prior, flow, visc, cells, base, halo, chunk, before, devices):
    members, layers, nz, ny = prior.shape
    part = members // CHUNKS
    steps = part // GROUP
    base_slabs = layers if chunk == 0 else 0
    whole = lambda shape: pl.BlockSpec(shape, lambda i: (0,) * len(shape))
    block = pl.BlockSpec((GROUP, layers, nz, ny), lambda i: (chunk * steps + i, 0, 0, 0))
    args = [cells, prior, flow, visc, base[0], base[1], halo[0], halo[1]]
    specs = [SMEM, block, whole(flow.shape), whole(visc.shape)]
    specs += [whole((layers, nz, ny))] * 2 + [whole(halo[0].shape)] * 2
    alias = {}
    rows_shape = (64, ny) if chunk == 0 else (devices, ny)
    if chunk:
        args += [before[1], before[0]]
        specs += [whole((64, ny)), pl.BlockSpec(memory_space=pl.ANY)]
        alias = {len(args) - 1: 0}
    wide = layers + 2 * ITERS
    return pl.pallas_call(
        functools.partial(sweep_kernel, chunk, base_slabs, devices),
        grid=(steps,),
        in_specs=specs,
        out_specs=[block, whole(rows_shape)],
        out_shape=[
            jax.ShapeDtypeStruct(prior.shape, F32),
            jax.ShapeDtypeStruct(rows_shape, F32),
        ],
        input_output_aliases=alias,
        scratch_shapes=[
            pltpu.VMEM((wide, nz + 16, ny), F32),
            pltpu.VMEM((wide, nz + 16, ny), F32),
            pltpu.VMEM((wide - 2, nz, ny), F32),
            pltpu.VMEM((wide - 2, nz, ny), F32),
            pltpu.VMEM((wide - 2, nz, ny), F32),
            pltpu.VMEM((64, ny), F32),
        ],
        compiler_params=params(),
        name=f"sweeps{chunk}",
    )(*args)


def anomaly_kernel(members_all, prior_ref, a_ref, b_ref, c_ref, d_ref, out_ref):
    members, _, nz, ny = prior_ref.shape
    flat = prior_ref.reshape(members * nz, ny)
    mean = (a_ref[0] + b_ref[0] + c_ref[0] + d_ref[0]) / members_all
    for z in range(nz):
        rows = flat[pl.ds(z, members, stride=nz), :]
        out_ref[z] = (rows - mean[z : z + 1]).astype(BF16)


def anomalies(prior, totals, members_all):
    members, layers, nz, ny = prior.shape
    total = pl.BlockSpec((1, nz, ny), lambda l: (l, 0, 0))
    return pl.pallas_call(
        functools.partial(anomaly_kernel, members_all),
        grid=(layers,),
        in_specs=[pl.BlockSpec((members, 1, nz, ny), lambda l: (0, l, 0, 0))] + [total] * 4,
        out_specs=pl.BlockSpec((nz, members, ny), lambda l: (l, 0, 0)),
        out_shape=jax.ShapeDtypeStruct((layers * nz, members, ny), BF16),
        compiler_params=params(),
        name="anomalies",
    )(prior, *totals)


def slots_kernel(probes, slot_ref, value_ref, var_ref, noise_ref, seen_ref, weight_ref, stack):
    members, count = noise_ref.shape
    stack[...] = jnp.zeros_like(stack)
    stack[0:members] = noise_ref[...]
    stack[members : members + 1] = value_ref[...]
    stack[members + 1 : members + 2] = var_ref[...]
    slot = slot_ref[...]
    place = lax.rem(slot, probes) * (count // probes) + slot // probes
    row = lax.broadcasted_iota(jnp.int32, (count, count), 0)
    chosen = jnp.where(row == place, 1.0, 0.0)
    ordered = lax.dot_general(
        chosen, stack[...], (((1,), (1,)), ((), ())), precision=lax.Precision.HIGHEST, preferred_element_type=F32
    )
    value = ordered[:, members : members + 1]
    var = ordered[:, members + 1 : members + 2]
    seen_ref[...] = value + jnp.sqrt(var) * ordered
    weight_ref[...] = jnp.broadcast_to(1.0 / var, weight_ref.shape)


def in_slots(slot, value, var, noise, probes):
    count = slot.shape[0]
    shape = jax.ShapeDtypeStruct((count, 128), F32)
    return pl.pallas_call(
        functools.partial(slots_kernel, probes),
        in_specs=[VMEM] * 4,
        out_specs=[VMEM] * 2,
        out_shape=[shape, shape],
        scratch_shapes=[pltpu.VMEM((128, count), F32)],
        compiler_params=params(),
        name="slots",
    )(slot[None], value[None], var[None], noise)


def dot(a, b, dims):
    return lax.dot_general(a, b, (dims, ((), ())), precision=lax.Precision.HIGHEST, preferred_element_type=F32)


def solve_kernel(members, here, me_ref, vals_ref, seen_ref, weight_ref, out_ref, scr):
    devices, ny = vals_ref.shape
    groups = members // here
    tiles = devices // groups
    probes = 64 // here
    lane = lax.broadcasted_iota(jnp.int32, (tiles, ny), 1)
    parts = [vals_ref[pl.ds(g, tiles, stride=groups), :] for g in range(groups)]
    slabs = []
    for s in range(probes):
        slab = jnp.zeros((tiles, ny), F32)
        for g in range(groups):
            shift = (g - s) * here % ny
            moved = pltpu.roll(parts[g], shift, 1) if shift else parts[g]
            slab = jnp.where((lane >= g * here) & (lane < (g + 1) * here), moved, slab)
        slabs.append(slab)
    predicted = jnp.concatenate(slabs, axis=0)
    lanes = lax.broadcasted_iota(jnp.int32, predicted.shape, 1)
    mean = jnp.sum(predicted, axis=1, keepdims=True) / members
    spread = jnp.where(lanes < members, predicted - mean, 0.0)
    scaled = (spread * weight_ref[...]).T
    gram = dot(scaled, spread, ((1,), (0,)))
    rhs = dot(scaled, seen_ref[...] - predicted, ((1,), (0,)))
    half = 0.5 * jnp.max(jnp.sum(jnp.abs(gram), axis=1))
    alpha = 1.0 / (members - 1.0 + half)
    diagonal = lax.broadcasted_iota(jnp.int32, gram.shape, 0) == lax.broadcasted_iota(jnp.int32, gram.shape, 1)
    error = jnp.where(diagonal, alpha * half, 0.0) - alpha * gram

    def more(state):
        return (state[0] > 1e-9) & (state[1] < 40)

    def double(state):
        size, count, power_of, x = state
        both = dot(power_of, jnp.concatenate([power_of, x], axis=1), ((1,), (0,)))
        return size * size, count + 1, both[:, :ny], x + both[:, ny:]

    x = lax.while_loop(more, double, (half * alpha, 0, error, alpha * rhs))[3]
    me = me_ref[0]
    scr[...] = x
    order = [scr[pl.ds(pl.multiple_of((me ^ g) * here, here), here), :] for g in range(groups)]
    scr[...] = jnp.concatenate(order + [jnp.zeros((ny - members, ny), F32)], axis=0).T
    out_ref[...] = scr[pl.ds(pl.multiple_of(me * here, here), here), :].astype(BF16)[:, :members]


def solve(vals, seen, weight, me, members, here):
    return pl.pallas_call(
        functools.partial(solve_kernel, members, here),
        in_specs=[SMEM] + [VMEM] * 3,
        out_specs=VMEM,
        out_shape=jax.ShapeDtypeStruct((here, members), BF16),
        scratch_shapes=[pltpu.VMEM((128, 128), F32)],
        compiler_params=params(),
        name="solve",
    )(me, vals, seen, weight)


def update_kernel(weights_ref, prior_ref, *refs):
    blocks, out_ref = refs[:-1], refs[-1]
    members, _, nz, ny = prior_ref.shape
    flat = prior_ref.reshape(members * nz, ny)
    out = out_ref.reshape(members * nz, ny)
    weights = weights_ref[...]
    for z in range(0, nz, 2):
        pair = [jnp.concatenate([b[z + i] for b in blocks], axis=0) for i in range(2)]
        update = jnp.dot(weights, jnp.concatenate(pair, axis=1), preferred_element_type=F32)
        for i in range(2):
            where = pl.ds(z + i, members, stride=nz)
            out[where, :] = flat[where, :] + update[:, i * ny : (i + 1) * ny]


def updated(weights, prior, blocks):
    members, layers, nz, ny = prior.shape
    block = pl.BlockSpec((members, 1, nz, ny), lambda l: (0, l, 0, 0))
    part = pl.BlockSpec((nz, members, ny), lambda l: (l, 0, 0))
    return pl.pallas_call(
        update_kernel,
        grid=(layers,),
        in_specs=[pl.BlockSpec(weights.shape, lambda l: (0, 0)), block] + [part] * len(blocks),
        out_specs=block,
        out_shape=jax.ShapeDtypeStruct(prior.shape, F32),
        compiler_params=params(),
        name="update",
    )(weights, prior, *blocks)


def per_device(prior, base_flow, base_visc, probe_cells, obs_slot, obs_values, obs_var, obs_noise):
    here = prior.shape[0]
    tiles, groups = lax.axis_size("tile"), lax.axis_size("mem")
    members = here * groups
    me = lax.axis_index("mem").astype(jnp.int32).reshape(1)

    def along(x, step):
        return lax.ppermute(x, "tile", [(i, (i + step) % tiles) for i in range(tiles)])

    def across(x, bits):
        return lax.ppermute(x, "mem", [(i, i ^ bits) for i in range(groups)])

    halos, total = [], None
    for chunk in range(CHUNKS):
        right, left, total = encode(prior, base_flow, base_visc, chunk, total)
        halos.append((along(right, 1), along(left, -1)))
    totals = [total] + [across(total, bits) for bits in (1, 2, 3)]
    seen, weight = in_slots(obs_slot, obs_values, obs_var, obs_noise, probe_cells.shape[1])
    state = None
    for chunk in range(CHUNKS):
        state = sweeps(prior, base_flow, base_visc, probe_cells, halos[0], halos[chunk], chunk, state, tiles * groups)
    velocity, payload = state
    mine = anomalies(prior, totals, float(members))
    beside = across(mine, 1)
    over = across(mine, 2)
    blocks = [mine, beside, over, across(over, 1)]
    vals = lax.all_to_all(payload, ("tile", "mem"), 0, 0, tiled=True)
    weights = solve(vals, seen, weight, me, members, here)
    return velocity, updated(weights, prior, blocks)


def solution(mesh):
    placed = (
        P("mem", "tile", None, None),
        P("tile", None, None),
        P("tile", None, None),
        P("tile", None),
        P(),
        P(),
        P(),
        P(),
    )
    return jax.shard_map(
        per_device,
        mesh=mesh,
        in_specs=placed,
        out_specs=(P("mem", "tile", None, None), P("mem", "tile", None, None)),
        check_vma=False,
    )
```

```python
import functools
import math

import jax
import jax.numpy as jnp
from jax import lax
from jax.experimental import pallas as pl
from jax.experimental.pallas import tpu as pltpu
from jax.sharding import PartitionSpec as P

ITERS = 4
PARTS = ((8, 0), (4, 2), (4, 3))
CHUNKS = len(PARTS)
AT_ONCE = 4
TOTAL_AFTER, ANOMALY_AFTER = 0, 2
LOG_MID = 0.5 * (math.log(0.02) + math.log(0.05))
LOG_HALF = 0.5 * (math.log(0.05) - math.log(0.02)) + 1.0
NU_SCALE = 124.0 / LOG_HALF
FLOW_SCALE = 31.0
LN2 = math.log(2.0)
VMEM = pl.BlockSpec(memory_space=pltpu.VMEM)
SMEM = pl.BlockSpec(memory_space=pltpu.SMEM)
F32 = jnp.float32
BF16 = jnp.bfloat16


def params(mib=48):
    return pltpu.CompilerParams(vmem_limit_bytes=mib * 1024 * 1024)


def power(x):
    return jnp.exp(x * LN2)


def log2_of(x):
    return jnp.log(x) * (1.0 / LN2)


def encode_kernel(prior_hbm, flow_hbm, visc_hbm, *refs):
    outs, (prior, flow, visc, base, sems) = refs[: 2 * CHUNKS], refs[2 * CHUNKS :]
    layers = prior.shape[1]
    copies = [
        pltpu.make_async_copy(visc_hbm, visc, sems.at[0]),
        pltpu.make_async_copy(flow_hbm, flow, sems.at[1]),
    ]
    for c, (part, place) in enumerate(PARTS):
        span = pl.ds(place * part, part)
        copies.append(pltpu.make_async_copy(prior_hbm.at[span], prior.at[span], sems.at[2 + c]))
    for copy in copies:
        copy.start()
    copies[0].wait()
    base[...] = jnp.log(visc[...]) * NU_SCALE - LOG_MID * NU_SCALE
    copies[1].wait()
    for l in range(layers):
        code = power(flow[l] * FLOW_SCALE).astype(BF16)
        outs[0][l] = code
        outs[1][l] = code
    for c, (part, place) in enumerate(PARTS):
        copies[2 + c].wait()
        right_ref, left_ref = outs[2 * c], outs[2 * c + 1]
        first = layers if c == 0 else 0

        def member(m, carry):
            for l in range(layers):
                code = power(prior[place * part + m, l] * NU_SCALE + base[l]).astype(BF16)
                if l >= 1:
                    right_ref[first + m * 3 + l - 1] = code
                if l < 3:
                    left_ref[first + m * 3 + l] = code
            return carry

        lax.fori_loop(0, part, member, 0)


def encode(prior, flow, visc):
    members, layers, nz, ny = prior.shape
    shapes = []
    for c, (part, _) in enumerate(PARTS):
        slabs = 3 * part + (layers if c == 0 else 0)
        shapes += [jax.ShapeDtypeStruct((slabs, nz, ny), BF16)] * 2
    return pl.pallas_call(
        encode_kernel,
        in_specs=[pl.BlockSpec(memory_space=pltpu.HBM)] * 3,
        out_specs=[VMEM] * len(shapes),
        out_shape=shapes,
        scratch_shapes=[
            pltpu.VMEM(prior.shape, F32),
            pltpu.VMEM(flow.shape, F32),
            pltpu.VMEM(visc.shape, F32),
            pltpu.VMEM(visc.shape, F32),
            pltpu.SemaphoreType.DMA((2 + CHUNKS,)),
        ],
        compiler_params=params(),
        name="encode",
    )(*[pltpu.with_memory_space_constraint(x, pltpu.HBM) for x in (prior, flow, visc)])


def total_kernel(prior_ref, after, out_ref):
    out_ref[...] = prior_ref[0]
    for m in range(1, prior_ref.shape[0]):
        out_ref[...] += prior_ref[m]


def total_of(prior, after):
    return pl.pallas_call(
        total_kernel,
        in_specs=[VMEM, pl.BlockSpec(memory_space=pl.ANY)],
        out_specs=VMEM,
        out_shape=jax.ShapeDtypeStruct(prior.shape[1:], F32),
        compiler_params=params(),
        name="total",
    )(prior, after)


def hold_kernel(*refs):
    pass


def held(value, *after):
    anywhere = pl.BlockSpec(memory_space=pl.ANY)
    return pl.pallas_call(
        hold_kernel,
        in_specs=[anywhere] * (1 + len(after)),
        out_specs=anywhere,
        out_shape=jax.ShapeDtypeStruct(value.shape, value.dtype),
        input_output_aliases={0: 0},
        name="hold",
    )(value, *after)


def neighbours(buf, l, centre, nz, ny):
    lane = lax.broadcasted_iota(jnp.int32, centre.shape, 1)
    below = jnp.where(lane == 0, 0.0, pltpu.roll(centre, 1, 1))
    above = jnp.where(lane == ny - 1, 0.0, pltpu.roll(centre, ny - 1, 1))
    return (buf[l, 7 : 7 + nz] + buf[l, 9 : 9 + nz]) + (below + above)


def put(buf, l, value, nz):
    buf[l, 8 : 8 + nz] = value
    buf[l, 7:8] = value[nz - 1 : nz]
    buf[l, 8 + nz : 9 + nz] = value[0:1]


def sweep_kernel(chunk, devices, cells_ref, prior_ref, flow_ref, visc_ref, behind_ref, ahead_ref, *rest):
    part, layers, nz, ny = prior_ref.shape
    wide = layers + 2 * ITERS
    last = chunk == CHUNKS - 1
    if chunk == 0:
        out_ref, rows, lap0, adv0, buf0, buf1, nu = rest
        for l in range(ITERS):
            put(buf0, l, log2_of(behind_ref[l].astype(F32)) * (1.0 / FLOW_SCALE), nz)
            put(buf0, ITERS + layers + l, log2_of(ahead_ref[l].astype(F32)) * (1.0 / FLOW_SCALE), nz)
        for l in range(layers):
            put(buf0, ITERS + l, flow_ref[l], nz)
        for l in range(1, wide - 1):
            centre, back = buf0[l, 8 : 8 + nz], buf0[l - 1, 8 : 8 + nz]
            sides = back + buf0[l + 1, 8 : 8 + nz] + neighbours(buf0, l, centre, nz, ny)
            lap0[l - 1] = sides - 6.0 * centre
            adv0[l - 1] = centre - 0.15 * (centre - back) + 0.01
        rows[...] = jnp.zeros_like(rows)
    elif not last:
        lap0, adv0, rows_in, _, out_ref, rows, buf0, buf1, nu = rest
        rows[...] = rows_in[...]
    else:
        lap0, adv0, rows_in, _, out_ref, lines_ref, buf0, buf1, nu, rows = rest
        rows[...] = rows_in[...]
    base_slabs = layers if chunk == 0 else 0

    def member(m, carry):
        first = base_slabs + m * 3
        for l in range(3):
            behind = behind_ref[first + l].astype(F32)
            nu[l] = jnp.exp(jnp.log(behind) * (1.0 / (LN2 * NU_SCALE)) + LOG_MID)
            ahead = ahead_ref[first + l].astype(F32)
            nu[3 + layers + l] = jnp.exp(jnp.log(ahead) * (1.0 / (LN2 * NU_SCALE)) + LOG_MID)
        for l in range(layers):
            nu[3 + l] = visc_ref[l] * jnp.exp(prior_ref[m, l])
        for l in range(1, wide - 1):
            put(buf1, l, adv0[l - 1] + nu[l - 1] * lap0[l - 1], nz)
        src, dst = buf1, buf0
        for sweep in range(1, ITERS):
            low, high = sweep + 1, wide - sweep - 1
            back, centre = src[low - 1, 8 : 8 + nz], src[low, 8 : 8 + nz]
            for l in range(low, high):
                front = src[l + 1, 8 : 8 + nz]
                lap = back + front + neighbours(src, l, centre, nz, ny) - 6.0 * centre
                value = centre + nu[l - 1] * lap - 0.15 * (centre - back) + 0.01
                if sweep == ITERS - 1:
                    out_ref[m, l - ITERS] = value
                else:
                    put(dst, l, value, nz)
                back, centre = centre, front
            src, dst = dst, src
        for s in range(4):
            cell = cells_ref[0, s]
            layer, z = cell // (nz * ny), lax.rem(cell, nz * ny) // ny
            rows[pl.ds(s * 16 + PARTS[chunk][1] * part + m, 1), :] = out_ref[m, layer, pl.ds(z, 1), :]
        return carry

    lax.fori_loop(0, part, member, 0)
    if last:
        lane = lax.broadcasted_iota(jnp.int32, rows.shape, 1)
        row = lax.broadcasted_iota(jnp.int32, rows.shape, 0)
        y = jnp.zeros(rows.shape, jnp.int32)
        for s in range(4):
            y = jnp.where(row // 16 == s, lax.rem(cells_ref[0, s], ny), y)
        picked = jnp.sum(jnp.where(lane == y, rows[...], 0.0), axis=1, keepdims=True)
        line = jnp.sum(jnp.where(lane == row, picked, 0.0), axis=0, keepdims=True)
        lines_ref[...] = jnp.broadcast_to(line, (devices, ny))


def sweeps(prior, flow, visc, cells, halo, chunk, before, devices):
    members, layers, nz, ny = prior.shape
    part, place = PARTS[chunk]
    whole = lambda shape: pl.BlockSpec(shape, lambda i: (0,) * len(shape))
    block = pl.BlockSpec((part, layers, nz, ny), lambda i: (place, 0, 0, 0))
    wide = layers + 2 * ITERS
    base_shape = (wide - 2, nz, ny)
    args = [cells, prior, flow, visc, *halo]
    specs = [SMEM, block, whole(flow.shape), whole(visc.shape), whole(halo[0].shape), whole(halo[1].shape)]
    alias = {}
    scratch = [
        pltpu.VMEM((wide, nz + 16, ny), F32),
        pltpu.VMEM((wide, nz + 16, ny), F32),
        pltpu.VMEM(base_shape, F32),
    ]
    if chunk:
        velocity, rows, lap0, adv0 = before
        args += [lap0, adv0, rows, velocity]
        specs += [whole(base_shape)] * 2 + [whole((64, ny)), pl.BlockSpec(memory_space=pl.ANY)]
        alias = {len(args) - 1: 0}
    last = chunk == CHUNKS - 1
    more = [(devices, ny)] if last else [(64, ny)]
    if chunk == 0:
        more += [base_shape] * 2
    if last:
        scratch.append(pltpu.VMEM((64, ny), F32))
    out = pl.pallas_call(
        functools.partial(sweep_kernel, chunk, devices),
        grid=(1,),
        in_specs=specs,
        out_specs=[block] + [whole(shape) for shape in more],
        out_shape=[jax.ShapeDtypeStruct(shape, F32) for shape in [prior.shape] + more],
        input_output_aliases=alias,
        scratch_shapes=scratch,
        compiler_params=params(),
        name=f"sweeps{chunk}",
    )(*args)
    return tuple(out) + (tuple(before[2:]) if chunk else ())


def anomaly_kernel(members_all, prior_ref, a_ref, b_ref, c_ref, d_ref, after, out_ref):
    members, _, nz, ny = prior_ref.shape
    flat = prior_ref.reshape(members * nz, ny)
    mean = (a_ref[0] + b_ref[0] + c_ref[0] + d_ref[0]) / members_all
    for z in range(nz):
        rows = flat[pl.ds(z, members, stride=nz), :]
        out_ref[z] = (rows - mean[z : z + 1]).astype(BF16)


def anomalies(prior, totals, members_all, after):
    members, layers, nz, ny = prior.shape
    total = pl.BlockSpec((1, nz, ny), lambda l: (l, 0, 0))
    return pl.pallas_call(
        functools.partial(anomaly_kernel, members_all),
        grid=(layers,),
        in_specs=[pl.BlockSpec((members, 1, nz, ny), lambda l: (0, l, 0, 0))] + [total] * 4 + [pl.BlockSpec(memory_space=pl.ANY)],
        out_specs=pl.BlockSpec((nz, members, ny), lambda l: (l, 0, 0)),
        out_shape=jax.ShapeDtypeStruct((layers * nz, members, ny), BF16),
        compiler_params=params(),
        name="anomalies",
    )(prior, *totals, after)


def slots_kernel(probes, slot_ref, value_ref, var_ref, noise_ref, after, seen_ref, weight_ref, stack):
    members, count = noise_ref.shape
    stack[...] = jnp.zeros_like(stack)
    stack[0:members] = noise_ref[...]
    stack[members : members + 1] = value_ref[...]
    stack[members + 1 : members + 2] = var_ref[...]
    slot = slot_ref[...]
    place = lax.rem(slot, probes) * (count // probes) + slot // probes
    row = lax.broadcasted_iota(jnp.int32, (count, count), 0)
    chosen = jnp.where(row == place, 1.0, 0.0)
    ordered = lax.dot_general(
        chosen, stack[...], (((1,), (1,)), ((), ())), precision=lax.Precision.HIGHEST, preferred_element_type=F32
    )
    value = ordered[:, members : members + 1]
    var = ordered[:, members + 1 : members + 2]
    seen_ref[...] = value + jnp.sqrt(var) * ordered
    weight_ref[...] = jnp.broadcast_to(1.0 / var, weight_ref.shape)


def in_slots(slot, value, var, noise, probes, after):
    count = slot.shape[0]
    shape = jax.ShapeDtypeStruct((count, 128), F32)
    return pl.pallas_call(
        functools.partial(slots_kernel, probes),
        in_specs=[VMEM] * 4 + [pl.BlockSpec(memory_space=pl.ANY)],
        out_specs=[VMEM] * 2,
        out_shape=[shape, shape],
        scratch_shapes=[pltpu.VMEM((128, count), F32)],
        cost_estimate=pl.CostEstimate(flops=0, bytes_accessed=1 << 26, transcendentals=0),
        compiler_params=params(),
        name="slots",
    )(slot[None], value[None], var[None], noise, after)


def dot(a, b, dims):
    return lax.dot_general(a, b, (dims, ((), ())), precision=lax.Precision.HIGHEST, preferred_element_type=F32)


def solve_kernel(members, here, me_ref, vals_ref, seen_ref, weight_ref, out_ref, scr):
    devices, ny = vals_ref.shape
    groups = members // here
    tiles = devices // groups
    probes = 64 // here
    lane = lax.broadcasted_iota(jnp.int32, (tiles, ny), 1)
    parts = [vals_ref[pl.ds(g, tiles, stride=groups), :] for g in range(groups)]
    slabs = []
    for s in range(probes):
        slab = jnp.zeros((tiles, ny), F32)
        for g in range(groups):
            shift = (g - s) * here % ny
            moved = pltpu.roll(parts[g], shift, 1) if shift else parts[g]
            slab = jnp.where((lane >= g * here) & (lane < (g + 1) * here), moved, slab)
        slabs.append(slab)
    predicted = jnp.concatenate(slabs, axis=0)
    lanes = lax.broadcasted_iota(jnp.int32, predicted.shape, 1)
    mean = jnp.sum(predicted, axis=1, keepdims=True) / members
    spread = jnp.where(lanes < members, predicted - mean, 0.0)
    scaled = (spread * weight_ref[...]).T
    gram = dot(scaled, spread, ((1,), (0,)))
    rhs = dot(scaled, seen_ref[...] - predicted, ((1,), (0,)))
    half = 0.5 * jnp.max(jnp.sum(jnp.abs(gram), axis=1))
    alpha = 1.0 / (members - 1.0 + half)
    diagonal = lax.broadcasted_iota(jnp.int32, gram.shape, 0) == lax.broadcasted_iota(jnp.int32, gram.shape, 1)
    error = jnp.where(diagonal, alpha * half, 0.0) - alpha * gram

    def more(state):
        return (state[0] > 1e-9) & (state[1] < 40)

    def double(state):
        size, count, power_of, x = state
        both = dot(power_of, jnp.concatenate([power_of, x], axis=1), ((1,), (0,)))
        return size * size, count + 1, both[:, :ny], x + both[:, ny:]

    x = lax.while_loop(more, double, (half * alpha, 0, error, alpha * rhs))[3]
    me = me_ref[0]
    scr[...] = x
    order = [scr[pl.ds(pl.multiple_of((me ^ g) * here, here), here), :] for g in range(groups)]
    scr[...] = jnp.concatenate(order + [jnp.zeros((ny - members, ny), F32)], axis=0).T
    mine = scr[pl.ds(pl.multiple_of(me * here, here), here), :]
    copies = out_ref.shape[1] // members
    wide = jnp.concatenate([mine + pltpu.roll(mine, members, 1)] * (copies // 2), axis=1)
    wide = jnp.concatenate([wide] * copies, axis=0)
    row = lax.broadcasted_iota(jnp.int32, wide.shape, 0)
    column = lax.broadcasted_iota(jnp.int32, wide.shape, 1)
    out_ref[...] = jnp.where(row // here == column // members, wide, 0.0).astype(BF16)


def solve(vals, seen, weight, me, members, here):
    return pl.pallas_call(
        functools.partial(solve_kernel, members, here),
        in_specs=[SMEM] + [VMEM] * 3,
        out_specs=VMEM,
        out_shape=jax.ShapeDtypeStruct((AT_ONCE * here, AT_ONCE * members), BF16),
        scratch_shapes=[pltpu.VMEM((128, 128), F32)],
        compiler_params=params(),
        name="solve",
    )(me, vals, seen, weight)


def update_kernel(weights_ref, prior_ref, *refs):
    blocks, out_ref = refs[:-1], refs[-1]
    members, _, nz, ny = prior_ref.shape
    flat = prior_ref.reshape(members * nz, ny)
    out = out_ref.reshape(members * nz, ny)
    weights = weights_ref[...]
    for z in range(0, nz, 2 * AT_ONCE):
        sides = []
        for i in range(2):
            rows = range(z + i * AT_ONCE, z + (i + 1) * AT_ONCE)
            sides.append(jnp.concatenate([b[r] for r in rows for b in blocks], axis=0))
        update = jnp.dot(weights, jnp.concatenate(sides, axis=1), preferred_element_type=F32)
        for i in range(2):
            for r in range(AT_ONCE):
                where = pl.ds(z + i * AT_ONCE + r, members, stride=nz)
                part = update[r * members : (r + 1) * members, i * ny : (i + 1) * ny]
                out[where, :] = flat[where, :] + part


def updated(weights, prior, blocks):
    members, layers, nz, ny = prior.shape
    block = pl.BlockSpec((members, 1, nz, ny), lambda l: (0, l, 0, 0))
    part = pl.BlockSpec((nz, members, ny), lambda l: (l, 0, 0))
    return pl.pallas_call(
        update_kernel,
        grid=(layers,),
        in_specs=[pl.BlockSpec(weights.shape, lambda l: (0, 0)), block] + [part] * len(blocks),
        out_specs=block,
        out_shape=jax.ShapeDtypeStruct(prior.shape, F32),
        compiler_params=params(),
        name="update",
    )(weights, prior, *blocks)


def per_device(prior, base_flow, base_visc, probe_cells, obs_slot, obs_values, obs_var, obs_noise):
    here = prior.shape[0]
    tiles, groups = lax.axis_size("tile"), lax.axis_size("mem")
    members = here * groups
    me = lax.axis_index("mem").astype(jnp.int32).reshape(1)

    def along(x, step):
        return lax.ppermute(x, "tile", [(i, (i + step) % tiles) for i in range(tiles)])

    def across(x, bits):
        return lax.ppermute(x, "mem", [(i, i ^ bits) for i in range(groups)])

    sent = encode(prior, base_flow, base_visc)
    halos = [(along(sent[2 * c], 1), along(sent[2 * c + 1], -1)) for c in range(CHUNKS)]
    state, states = None, []
    for chunk in range(CHUNKS):
        state = sweeps(prior, base_flow, base_visc, probe_cells, halos[chunk], chunk, state, tiles * groups)
        states.append(state)
    velocity, payload = state[:2]
    total = total_of(prior, states[TOTAL_AFTER][1])
    totals = [total] + [across(total, bits) for bits in (1, 2, 3)]
    mine = anomalies(prior, totals, float(members), states[ANOMALY_AFTER][1])
    beside = across(mine, 1)
    over = across(mine, 2)
    vals = lax.all_to_all(payload, ("tile", "mem"), 0, 0, tiled=True)
    seen, weight = in_slots(obs_slot, obs_values, obs_var, obs_noise, probe_cells.shape[1], payload)
    over = held(over, vals, seen)
    blocks = [mine, beside, over, across(over, 1)]
    weights = solve(vals, seen, weight, me, members, here)
    return velocity, updated(weights, prior, blocks)


def solution(mesh):
    placed = (
        P("mem", "tile", None, None),
        P("tile", None, None),
        P("tile", None, None),
        P("tile", None),
        P(),
        P(),
        P(),
        P(),
    )
    return jax.shard_map(
        per_device,
        mesh=mesh,
        in_specs=placed,
        out_specs=(P("mem", "tile", None, None), P("mem", "tile", None, None)),
        check_vma=False,
    )
```

```python
import functools
import math

import jax
import jax.numpy as jnp
from jax import lax
from jax.experimental import pallas as pl
from jax.experimental.pallas import tpu as pltpu
from jax.sharding import PartitionSpec as P

ITERS = 4
PARTS = ((8, 0), (8, 1))
CHUNKS = len(PARTS)
AT_ONCE = 4
TOTAL_AFTER, ANOMALY_AFTER = 0, 1
LOG_MID = 0.5 * (math.log(0.02) + math.log(0.05))
LOG_HALF = 0.5 * (math.log(0.05) - math.log(0.02)) + 1.0
NU_SCALE = 124.0 / LOG_HALF
FLOW_SCALE = 31.0
LN2 = math.log(2.0)
VMEM = pl.BlockSpec(memory_space=pltpu.VMEM)
SMEM = pl.BlockSpec(memory_space=pltpu.SMEM)
F32 = jnp.float32
BF16 = jnp.bfloat16


def params(mib=24):
    return pltpu.CompilerParams(vmem_limit_bytes=mib * 1024 * 1024)


def power(x):
    return jnp.exp(x * LN2)


def log2_of(x):
    return jnp.log(x) * (1.0 / LN2)


def encode_kernel(prior_hbm, flow_hbm, visc_hbm, *refs):
    outs, (prior, flow, visc, base, sems) = refs[: 2 * CHUNKS], refs[2 * CHUNKS :]
    layers = prior.shape[1]
    copies = [
        pltpu.make_async_copy(visc_hbm, visc, sems.at[0]),
        pltpu.make_async_copy(flow_hbm, flow, sems.at[1]),
    ]
    for c, (part, place) in enumerate(PARTS):
        span = pl.ds(place * part, part)
        copies.append(pltpu.make_async_copy(prior_hbm.at[span], prior.at[span], sems.at[2 + c]))
    for copy in copies:
        copy.start()
    copies[0].wait()
    base[...] = jnp.log(visc[...]) * NU_SCALE - LOG_MID * NU_SCALE
    copies[1].wait()
    for l in range(layers):
        code = power(flow[l] * FLOW_SCALE).astype(BF16)
        outs[0][l] = code
        outs[1][l] = code
    for c, (part, place) in enumerate(PARTS):
        copies[2 + c].wait()
        right_ref, left_ref = outs[2 * c], outs[2 * c + 1]
        first = layers if c == 0 else 0

        def member(m, carry):
            for l in range(layers):
                code = power(prior[place * part + m, l] * NU_SCALE + base[l]).astype(BF16)
                if l >= 1:
                    right_ref[first + m * 3 + l - 1] = code
                if l < 3:
                    left_ref[first + m * 3 + l] = code
            return carry

        lax.fori_loop(0, part, member, 0)


def encode(prior, flow, visc):
    members, layers, nz, ny = prior.shape
    shapes = []
    for c, (part, _) in enumerate(PARTS):
        slabs = 3 * part + (layers if c == 0 else 0)
        shapes += [jax.ShapeDtypeStruct((slabs, nz, ny), BF16)] * 2
    return pl.pallas_call(
        encode_kernel,
        in_specs=[pl.BlockSpec(memory_space=pltpu.HBM)] * 3,
        out_specs=[VMEM] * len(shapes),
        out_shape=shapes,
        scratch_shapes=[
            pltpu.VMEM(prior.shape, F32),
            pltpu.VMEM(flow.shape, F32),
            pltpu.VMEM(visc.shape, F32),
            pltpu.VMEM(visc.shape, F32),
            pltpu.SemaphoreType.DMA((2 + CHUNKS,)),
        ],
        compiler_params=params(),
        name="encode",
    )(*[pltpu.with_memory_space_constraint(x, pltpu.HBM) for x in (prior, flow, visc)])


def total_kernel(prior_ref, after, out_ref):
    out_ref[...] = prior_ref[0]
    for m in range(1, prior_ref.shape[0]):
        out_ref[...] += prior_ref[m]


def total_of(prior, after):
    return pl.pallas_call(
        total_kernel,
        in_specs=[VMEM, pl.BlockSpec(memory_space=pl.ANY)],
        out_specs=VMEM,
        out_shape=jax.ShapeDtypeStruct(prior.shape[1:], F32),
        compiler_params=params(),
        name="total",
    )(prior, after)


def hold_kernel(*refs):
    pass


def held(value, *after):
    return pl.pallas_call(
        hold_kernel,
        in_specs=[VMEM] * (1 + len(after)),
        out_specs=VMEM,
        out_shape=jax.ShapeDtypeStruct(value.shape, value.dtype),
        input_output_aliases={0: 0},
        compiler_params=params(),
        name="hold",
    )(value, *after)


def neighbours(buf, l, centre, nz, ny):
    lane = lax.broadcasted_iota(jnp.int32, centre.shape, 1)
    below = jnp.where(lane == 0, 0.0, pltpu.roll(centre, 1, 1))
    above = jnp.where(lane == ny - 1, 0.0, pltpu.roll(centre, ny - 1, 1))
    return (buf[l, 7 : 7 + nz] + buf[l, 9 : 9 + nz]) + (below + above)


def put(buf, l, value, nz):
    buf[l, 8 : 8 + nz] = value
    buf[l, 7:8] = value[nz - 1 : nz]
    buf[l, 8 + nz : 9 + nz] = value[0:1]


def sweep_kernel(chunk, devices, cells_ref, prior_ref, flow_ref, visc_ref, behind_ref, ahead_ref, *rest):
    part, layers, nz, ny = prior_ref.shape
    wide = layers + 2 * ITERS
    last = chunk == CHUNKS - 1
    if chunk == 0:
        out_ref, rows, lap0, adv0, buf0, buf1, nu = rest
        for l in range(ITERS):
            put(buf0, l, log2_of(behind_ref[l].astype(F32)) * (1.0 / FLOW_SCALE), nz)
            put(buf0, ITERS + layers + l, log2_of(ahead_ref[l].astype(F32)) * (1.0 / FLOW_SCALE), nz)
        for l in range(layers):
            put(buf0, ITERS + l, flow_ref[l], nz)
        for l in range(1, wide - 1):
            centre, back = buf0[l, 8 : 8 + nz], buf0[l - 1, 8 : 8 + nz]
            sides = back + buf0[l + 1, 8 : 8 + nz] + neighbours(buf0, l, centre, nz, ny)
            lap0[l - 1] = sides - 6.0 * centre
            adv0[l - 1] = centre - 0.15 * (centre - back) + 0.01
        rows[...] = jnp.zeros_like(rows)
    elif not last:
        lap0, adv0, rows_in, _, out_ref, rows, buf0, buf1, nu = rest
        rows[...] = rows_in[...]
    else:
        lap0, adv0, rows_in, _, out_ref, lines_ref, buf0, buf1, nu, rows = rest
        rows[...] = rows_in[...]
    base_slabs = layers if chunk == 0 else 0

    def member(m, carry):
        first = base_slabs + m * 3
        for l in range(3):
            behind = behind_ref[first + l].astype(F32)
            nu[l] = jnp.exp(jnp.log(behind) * (1.0 / (LN2 * NU_SCALE)) + LOG_MID)
            ahead = ahead_ref[first + l].astype(F32)
            nu[3 + layers + l] = jnp.exp(jnp.log(ahead) * (1.0 / (LN2 * NU_SCALE)) + LOG_MID)
        for l in range(layers):
            nu[3 + l] = visc_ref[l] * jnp.exp(prior_ref[m, l])
        for l in range(1, wide - 1):
            put(buf1, l, adv0[l - 1] + nu[l - 1] * lap0[l - 1], nz)
        src, dst = buf1, buf0
        for sweep in range(1, ITERS):
            low, high = sweep + 1, wide - sweep - 1
            back, centre = src[low - 1, 8 : 8 + nz], src[low, 8 : 8 + nz]
            for l in range(low, high):
                front = src[l + 1, 8 : 8 + nz]
                lap = back + front + neighbours(src, l, centre, nz, ny) - 6.0 * centre
                value = centre + nu[l - 1] * lap - 0.15 * (centre - back) + 0.01
                if sweep == ITERS - 1:
                    out_ref[m, l - ITERS] = value
                else:
                    put(dst, l, value, nz)
                back, centre = centre, front
            src, dst = dst, src
        for s in range(4):
            cell = cells_ref[0, s]
            layer, z = cell // (nz * ny), lax.rem(cell, nz * ny) // ny
            rows[pl.ds(s * 16 + PARTS[chunk][1] * part + m, 1), :] = out_ref[m, layer, pl.ds(z, 1), :]
        return carry

    lax.fori_loop(0, part, member, 0)
    if last:
        lane = lax.broadcasted_iota(jnp.int32, rows.shape, 1)
        row = lax.broadcasted_iota(jnp.int32, rows.shape, 0)
        y = jnp.zeros(rows.shape, jnp.int32)
        for s in range(4):
            y = jnp.where(row // 16 == s, lax.rem(cells_ref[0, s], ny), y)
        picked = jnp.sum(jnp.where(lane == y, rows[...], 0.0), axis=1, keepdims=True)
        line = jnp.sum(jnp.where(lane == row, picked, 0.0), axis=0, keepdims=True)
        lines_ref[...] = jnp.broadcast_to(line, (devices, ny))


def sweeps(prior, flow, visc, cells, halo, chunk, before, devices):
    members, layers, nz, ny = prior.shape
    part, place = PARTS[chunk]
    whole = lambda shape: pl.BlockSpec(shape, lambda i: (0,) * len(shape))
    block = pl.BlockSpec((part, layers, nz, ny), lambda i: (place, 0, 0, 0))
    wide = layers + 2 * ITERS
    base_shape = (wide - 2, nz, ny)
    args = [cells, prior, flow, visc, *halo]
    specs = [SMEM, block, whole(flow.shape), whole(visc.shape), whole(halo[0].shape), whole(halo[1].shape)]
    alias = {}
    scratch = [
        pltpu.VMEM((wide, nz + 16, ny), F32),
        pltpu.VMEM((wide, nz + 16, ny), F32),
        pltpu.VMEM(base_shape, F32),
    ]
    if chunk:
        velocity, rows, lap0, adv0 = before
        args += [lap0, adv0, rows, velocity]
        specs += [whole(base_shape)] * 2 + [whole((64, ny)), pl.BlockSpec(memory_space=pl.ANY)]
        alias = {len(args) - 1: 0}
    last = chunk == CHUNKS - 1
    more = [(devices, ny)] if last else [(64, ny)]
    if chunk == 0:
        more += [base_shape] * 2
    if last:
        scratch.append(pltpu.VMEM((64, ny), F32))
    out = pl.pallas_call(
        functools.partial(sweep_kernel, chunk, devices),
        grid=(1,),
        in_specs=specs,
        out_specs=[block] + [whole(shape) for shape in more],
        out_shape=[jax.ShapeDtypeStruct(shape, F32) for shape in [prior.shape] + more],
        input_output_aliases=alias,
        scratch_shapes=scratch,
        compiler_params=params(),
        name=f"sweeps{chunk}",
    )(*args)
    return tuple(out) + (tuple(before[2:]) if chunk else ())


def anomaly_kernel(members_all, prior_ref, a_ref, b_ref, c_ref, d_ref, after, out_ref):
    members, _, nz, ny = prior_ref.shape
    flat = prior_ref.reshape(members * nz, ny)
    mean = (a_ref[0] + b_ref[0] + c_ref[0] + d_ref[0]) / members_all
    for z in range(nz):
        rows = flat[pl.ds(z, members, stride=nz), :]
        out_ref[z] = (rows - mean[z : z + 1]).astype(BF16)


def anomalies(prior, totals, members_all, after):
    members, layers, nz, ny = prior.shape
    total = pl.BlockSpec((1, nz, ny), lambda l: (l, 0, 0))
    return pl.pallas_call(
        functools.partial(anomaly_kernel, members_all),
        grid=(layers,),
        in_specs=[pl.BlockSpec((members, 1, nz, ny), lambda l: (0, l, 0, 0))] + [total] * 4 + [pl.BlockSpec(memory_space=pl.ANY)],
        out_specs=pl.BlockSpec((nz, members, ny), lambda l: (l, 0, 0)),
        out_shape=jax.ShapeDtypeStruct((layers * nz, members, ny), BF16),
        compiler_params=params(),
        name="anomalies",
    )(prior, *totals, after)


def slots_kernel(probes, slot_ref, value_ref, var_ref, noise_ref, after, seen_ref, weight_ref, stack):
    members, count = noise_ref.shape
    stack[...] = jnp.zeros_like(stack)
    stack[0:members] = noise_ref[...]
    stack[members : members + 1] = value_ref[...]
    stack[members + 1 : members + 2] = var_ref[...]
    slot = slot_ref[...]
    place = lax.rem(slot, probes) * (count // probes) + slot // probes
    row = lax.broadcasted_iota(jnp.int32, (count, count), 0)
    chosen = jnp.where(row == place, 1.0, 0.0)
    ordered = lax.dot_general(
        chosen, stack[...], (((1,), (1,)), ((), ())), precision=lax.Precision.HIGHEST, preferred_element_type=F32
    )
    value = ordered[:, members : members + 1]
    var = ordered[:, members + 1 : members + 2]
    seen_ref[...] = value + jnp.sqrt(var) * ordered
    weight_ref[...] = jnp.broadcast_to(1.0 / var, weight_ref.shape)


def in_slots(slot, value, var, noise, probes, after):
    count = slot.shape[0]
    shape = jax.ShapeDtypeStruct((count, 128), F32)
    return pl.pallas_call(
        functools.partial(slots_kernel, probes),
        in_specs=[VMEM] * 4 + [pl.BlockSpec(memory_space=pl.ANY)],
        out_specs=[VMEM] * 2,
        out_shape=[shape, shape],
        scratch_shapes=[pltpu.VMEM((128, count), F32)],
        cost_estimate=pl.CostEstimate(flops=0, bytes_accessed=1 << 26, transcendentals=0),
        compiler_params=params(),
        name="slots",
    )(slot[None], value[None], var[None], noise, after)


def dot(a, b, dims):
    return lax.dot_general(a, b, (dims, ((), ())), precision=lax.Precision.HIGHEST, preferred_element_type=F32)


def solve_kernel(members, here, me_ref, vals_ref, seen_ref, weight_ref, out_ref, scr):
    devices, ny = vals_ref.shape
    groups = members // here
    tiles = devices // groups
    probes = 64 // here
    lane = lax.broadcasted_iota(jnp.int32, (tiles, ny), 1)
    parts = [vals_ref[pl.ds(g, tiles, stride=groups), :] for g in range(groups)]
    slabs = []
    for s in range(probes):
        slab = jnp.zeros((tiles, ny), F32)
        for g in range(groups):
            shift = (g - s) * here % ny
            moved = pltpu.roll(parts[g], shift, 1) if shift else parts[g]
            slab = jnp.where((lane >= g * here) & (lane < (g + 1) * here), moved, slab)
        slabs.append(slab)
    predicted = jnp.concatenate(slabs, axis=0)
    lanes = lax.broadcasted_iota(jnp.int32, predicted.shape, 1)
    mean = jnp.sum(predicted, axis=1, keepdims=True) / members
    spread = jnp.where(lanes < members, predicted - mean, 0.0)
    scaled = (spread * weight_ref[...]).T
    gram = dot(scaled, spread, ((1,), (0,)))
    rhs = dot(scaled, seen_ref[...] - predicted, ((1,), (0,)))
    half = 0.5 * jnp.max(jnp.sum(jnp.abs(gram), axis=1))
    alpha = 1.0 / (members - 1.0 + half)
    diagonal = lax.broadcasted_iota(jnp.int32, gram.shape, 0) == lax.broadcasted_iota(jnp.int32, gram.shape, 1)
    error = jnp.where(diagonal, alpha * half, 0.0) - alpha * gram

    def more(state):
        return (state[0] > 1e-9) & (state[1] < 40)

    def double(state):
        size, count, power_of, x = state
        both = dot(power_of, jnp.concatenate([power_of, x], axis=1), ((1,), (0,)))
        return size * size, count + 1, both[:, :ny], x + both[:, ny:]

    x = lax.while_loop(more, double, (half * alpha, 0, error, alpha * rhs))[3]
    me = me_ref[0]
    scr[...] = x
    order = [scr[pl.ds(pl.multiple_of((me ^ g) * here, here), here), :] for g in range(groups)]
    scr[...] = jnp.concatenate(order + [jnp.zeros((ny - members, ny), F32)], axis=0).T
    mine = scr[pl.ds(pl.multiple_of(me * here, here), here), :]
    copies = out_ref.shape[1] // members
    wide = jnp.concatenate([mine + pltpu.roll(mine, members, 1)] * (copies // 2), axis=1)
    wide = jnp.concatenate([wide] * copies, axis=0)
    row = lax.broadcasted_iota(jnp.int32, wide.shape, 0)
    column = lax.broadcasted_iota(jnp.int32, wide.shape, 1)
    out_ref[...] = jnp.where(row // here == column // members, wide, 0.0).astype(BF16)


def solve(vals, seen, weight, me, members, here):
    return pl.pallas_call(
        functools.partial(solve_kernel, members, here),
        in_specs=[SMEM] + [VMEM] * 3,
        out_specs=VMEM,
        out_shape=jax.ShapeDtypeStruct((AT_ONCE * here, AT_ONCE * members), BF16),
        scratch_shapes=[pltpu.VMEM((128, 128), F32)],
        compiler_params=params(),
        name="solve",
    )(me, vals, seen, weight)


def update_kernel(weights_ref, prior_ref, *refs):
    blocks, out_ref = refs[:-1], refs[-1]
    members, _, nz, ny = prior_ref.shape
    flat = prior_ref.reshape(members * nz, ny)
    out = out_ref.reshape(members * nz, ny)
    weights = weights_ref[...]
    for z in range(0, nz, 2 * AT_ONCE):
        sides = []
        for i in range(2):
            rows = range(z + i * AT_ONCE, z + (i + 1) * AT_ONCE)
            sides.append(jnp.concatenate([b[r] for r in rows for b in blocks], axis=0))
        update = jnp.dot(weights, jnp.concatenate(sides, axis=1), preferred_element_type=F32)
        for i in range(2):
            for r in range(AT_ONCE):
                where = pl.ds(z + i * AT_ONCE + r, members, stride=nz)
                part = update[r * members : (r + 1) * members, i * ny : (i + 1) * ny]
                out[where, :] = flat[where, :] + part


def updated(weights, prior, blocks):
    members, layers, nz, ny = prior.shape
    block = pl.BlockSpec((members, 1, nz, ny), lambda l: (0, l, 0, 0))
    part = pl.BlockSpec((nz, members, ny), lambda l: (l, 0, 0))
    return pl.pallas_call(
        update_kernel,
        grid=(layers,),
        in_specs=[pl.BlockSpec(weights.shape, lambda l: (0, 0)), block] + [part] * len(blocks),
        out_specs=block,
        out_shape=jax.ShapeDtypeStruct(prior.shape, F32),
        compiler_params=params(),
        name="update",
    )(weights, prior, *blocks)


def per_device(prior, base_flow, base_visc, probe_cells, obs_slot, obs_values, obs_var, obs_noise):
    here = prior.shape[0]
    tiles, groups = lax.axis_size("tile"), lax.axis_size("mem")
    members = here * groups
    me = lax.axis_index("mem").astype(jnp.int32).reshape(1)

    def along(x, step):
        return lax.ppermute(x, "tile", [(i, (i + step) % tiles) for i in range(tiles)])

    def across(x, bits):
        return lax.ppermute(x, "mem", [(i, i ^ bits) for i in range(groups)])

    sent = encode(prior, base_flow, base_visc)
    halos = [(along(sent[2 * c], 1), along(sent[2 * c + 1], -1)) for c in range(CHUNKS)]
    state, states = None, []
    for chunk in range(CHUNKS):
        state = sweeps(prior, base_flow, base_visc, probe_cells, halos[chunk], chunk, state, tiles * groups)
        states.append(state)
    velocity, payload = state[:2]
    total = total_of(prior, states[TOTAL_AFTER][1])
    totals = [total] + [across(total, bits) for bits in (1, 2, 3)]
    mine = anomalies(prior, totals, float(members), states[ANOMALY_AFTER][1])
    beside = across(mine, 1)
    over = across(mine, 2)
    vals = lax.all_to_all(payload, ("tile", "mem"), 0, 0, tiled=True)
    seen, weight = in_slots(obs_slot, obs_values, obs_var, obs_noise, probe_cells.shape[1], payload)
    over = held(over, vals, seen)
    blocks = [mine, beside, over, across(over, 1)]
    weights = solve(vals, seen, weight, me, members, here)
    return velocity, updated(weights, prior, blocks)


def solution(mesh):
    placed = (
        P("mem", "tile", None, None),
        P("tile", None, None),
        P("tile", None, None),
        P("tile", None),
        P(),
        P(),
        P(),
        P(),
    )
    return jax.shard_map(
        per_device,
        mesh=mesh,
        in_specs=placed,
        out_specs=(P("mem", "tile", None, None), P("mem", "tile", None, None)),
        check_vma=False,
    )
```

```python
import functools
import math

import jax
import jax.numpy as jnp
from jax import lax
from jax.experimental import pallas as pl
from jax.experimental.pallas import tpu as pltpu
from jax.sharding import PartitionSpec as P

ITERS = 4
PARTS = ((8, 0), (8, 1))
CHUNKS = len(PARTS)
ROWS = 8
TOTAL_AFTER, ANOMALY_AFTER = 0, 1
LOG_MID = 0.5 * (math.log(0.02) + math.log(0.05))
LOG_HALF = 0.5 * (math.log(0.05) - math.log(0.02)) + 1.0
NU_SCALE = 124.0 / LOG_HALF
FLOW_SCALE = 31.0
LN2 = math.log(2.0)
VMEM = pl.BlockSpec(memory_space=pltpu.VMEM)
SMEM = pl.BlockSpec(memory_space=pltpu.SMEM)
F32 = jnp.float32
BF16 = jnp.bfloat16


def params(mib=24):
    return pltpu.CompilerParams(vmem_limit_bytes=mib * 1024 * 1024)


def power(x):
    return jnp.exp(x * LN2)


def log2_of(x):
    return jnp.log(x) * (1.0 / LN2)


def encode_kernel(prior_hbm, flow_hbm, visc_hbm, *refs):
    outs, (prior, flow, visc, base, sems) = refs[: 2 * CHUNKS], refs[2 * CHUNKS :]
    layers = prior.shape[1]
    copies = [
        pltpu.make_async_copy(visc_hbm, visc, sems.at[0]),
        pltpu.make_async_copy(flow_hbm, flow, sems.at[1]),
    ]
    for c, (part, place) in enumerate(PARTS):
        span = pl.ds(place * part, part)
        copies.append(pltpu.make_async_copy(prior_hbm.at[span], prior.at[span], sems.at[2 + c]))
    for copy in copies:
        copy.start()
    copies[0].wait()
    base[...] = jnp.log(visc[...]) * NU_SCALE - LOG_MID * NU_SCALE
    copies[1].wait()
    for l in range(layers):
        code = power(flow[l] * FLOW_SCALE).astype(BF16)
        outs[0][l] = code
        outs[1][l] = code
    for c, (part, place) in enumerate(PARTS):
        copies[2 + c].wait()
        left_ref, right_ref = outs[2 * c], outs[2 * c + 1]
        first = layers if c == 0 else 0

        def member(m, carry):
            for l in range(layers):
                code = power(prior[place * part + m, l] * NU_SCALE + base[l]).astype(BF16)
                if l >= 1:
                    right_ref[first + m * 3 + l - 1] = code
                if l < 3:
                    left_ref[first + m * 3 + l] = code
            return carry

        lax.fori_loop(0, part, member, 0)


def encode(prior, flow, visc):
    members, layers, nz, ny = prior.shape
    shapes = []
    for c, (part, _) in enumerate(PARTS):
        slabs = 3 * part + (layers if c == 0 else 0)
        shapes += [jax.ShapeDtypeStruct((slabs, nz, ny), BF16)] * 2
    return pl.pallas_call(
        encode_kernel,
        in_specs=[pl.BlockSpec(memory_space=pltpu.HBM)] * 3,
        out_specs=[VMEM] * len(shapes),
        out_shape=shapes,
        scratch_shapes=[
            pltpu.VMEM(prior.shape, F32),
            pltpu.VMEM(flow.shape, F32),
            pltpu.VMEM(visc.shape, F32),
            pltpu.VMEM(visc.shape, F32),
            pltpu.SemaphoreType.DMA((2 + CHUNKS,)),
        ],
        compiler_params=params(),
        name="encode",
    )(*[pltpu.with_memory_space_constraint(x, pltpu.HBM) for x in (prior, flow, visc)])


def total_kernel(prior_ref, after, out_ref):
    out_ref[...] = prior_ref[0]
    for m in range(1, prior_ref.shape[0]):
        out_ref[...] += prior_ref[m]


def total_of(prior, after):
    return pl.pallas_call(
        total_kernel,
        in_specs=[VMEM, pl.BlockSpec(memory_space=pl.ANY)],
        out_specs=VMEM,
        out_shape=jax.ShapeDtypeStruct(prior.shape[1:], F32),
        compiler_params=params(),
        name="total",
    )(prior, after)


def hold_kernel(*refs):
    pass


def held(value, *after):
    return pl.pallas_call(
        hold_kernel,
        in_specs=[VMEM] * (1 + len(after)),
        out_specs=VMEM,
        out_shape=jax.ShapeDtypeStruct(value.shape, value.dtype),
        input_output_aliases={0: 0},
        compiler_params=params(),
        name="hold",
    )(value, *after)


def neighbours(buf, l, centre, nz, ny):
    lane = lax.broadcasted_iota(jnp.int32, centre.shape, 1)
    below = jnp.where(lane == 0, 0.0, pltpu.roll(centre, 1, 1))
    above = jnp.where(lane == ny - 1, 0.0, pltpu.roll(centre, ny - 1, 1))
    return (buf[l, 7 : 7 + nz] + buf[l, 9 : 9 + nz]) + (below + above)


def put(buf, l, value, nz):
    buf[l, 8 : 8 + nz] = value
    buf[l, 7:8] = value[nz - 1 : nz]
    buf[l, 8 + nz : 9 + nz] = value[0:1]


def sweep_kernel(chunk, devices, cells_ref, prior_ref, flow_ref, visc_ref, behind_ref, ahead_ref, *rest):
    _, layers, nz, ny = prior_ref.shape
    part, place = PARTS[chunk]
    wide = layers + 2 * ITERS
    last = chunk == CHUNKS - 1
    if chunk == 0:
        out_hbm, rows, lap0, adv0, buf0, buf1, nu, out_ref, sems = rest
        for l in range(ITERS):
            put(buf0, l, log2_of(behind_ref[l].astype(F32)) * (1.0 / FLOW_SCALE), nz)
            put(buf0, ITERS + layers + l, log2_of(ahead_ref[l].astype(F32)) * (1.0 / FLOW_SCALE), nz)
        for l in range(layers):
            put(buf0, ITERS + l, flow_ref[l], nz)
        for l in range(1, wide - 1):
            centre, back = buf0[l, 8 : 8 + nz], buf0[l - 1, 8 : 8 + nz]
            sides = back + buf0[l + 1, 8 : 8 + nz] + neighbours(buf0, l, centre, nz, ny)
            lap0[l - 1] = sides - 6.0 * centre
            adv0[l - 1] = centre - 0.15 * (centre - back) + 0.01
        rows[...] = jnp.zeros_like(rows)
    elif not last:
        lap0, adv0, rows_in, _, out_hbm, rows, buf0, buf1, nu, out_ref, sems = rest
        rows[...] = rows_in[...]
    else:
        lap0, adv0, rows_in, _, out_hbm, lines_ref, buf0, buf1, nu, out_ref, sems, rows = rest
        rows[...] = rows_in[...]
    base_slabs = layers if chunk == 0 else 0

    def store(m):
        return pltpu.make_async_copy(out_ref.at[m], out_hbm.at[place * part + m], sems.at[m])

    def member(m, carry):
        first = base_slabs + m * 3
        for l in range(3):
            behind = behind_ref[first + l].astype(F32)
            nu[l] = jnp.exp(jnp.log(behind) * (1.0 / (LN2 * NU_SCALE)) + LOG_MID)
            ahead = ahead_ref[first + l].astype(F32)
            nu[3 + layers + l] = jnp.exp(jnp.log(ahead) * (1.0 / (LN2 * NU_SCALE)) + LOG_MID)
        for l in range(layers):
            nu[3 + l] = visc_ref[l] * jnp.exp(prior_ref[place * part + m, l])
        for l in range(1, wide - 1):
            put(buf1, l, adv0[l - 1] + nu[l - 1] * lap0[l - 1], nz)
        src, dst = buf1, buf0
        for sweep in range(1, ITERS):
            low, high = sweep + 1, wide - sweep - 1
            back, centre = src[low - 1, 8 : 8 + nz], src[low, 8 : 8 + nz]
            for l in range(low, high):
                front = src[l + 1, 8 : 8 + nz]
                lap = back + front + neighbours(src, l, centre, nz, ny) - 6.0 * centre
                value = centre + nu[l - 1] * lap - 0.15 * (centre - back) + 0.01
                if sweep == ITERS - 1:
                    out_ref[m, l - ITERS] = value
                else:
                    put(dst, l, value, nz)
                back, centre = centre, front
            src, dst = dst, src
        store(m).start()
        for s in range(4):
            cell = cells_ref[0, s]
            layer, z = cell // (nz * ny), lax.rem(cell, nz * ny) // ny
            rows[pl.ds(s * 16 + place * part + m, 1), :] = out_ref[m, layer, pl.ds(z, 1), :]
        return carry

    lax.fori_loop(0, part, member, 0)
    if last:
        lane = lax.broadcasted_iota(jnp.int32, rows.shape, 1)
        row = lax.broadcasted_iota(jnp.int32, rows.shape, 0)
        y = jnp.zeros(rows.shape, jnp.int32)
        for s in range(4):
            y = jnp.where(row // 16 == s, lax.rem(cells_ref[0, s], ny), y)
        picked = jnp.sum(jnp.where(lane == y, rows[...], 0.0), axis=1, keepdims=True)
        line = jnp.sum(jnp.where(lane == row, picked, 0.0), axis=0, keepdims=True)
        lines_ref[...] = jnp.broadcast_to(line, (devices, ny))
    for m in range(part):
        store(m).wait()


def sweeps(prior, flow, visc, cells, halo, chunk, before, devices):
    _, layers, nz, ny = prior.shape
    part, _ = PARTS[chunk]
    wide = layers + 2 * ITERS
    base_shape = (wide - 2, nz, ny)
    args = [cells, prior, flow, visc, *halo]
    scratch = [
        pltpu.VMEM((wide, nz + 16, ny), F32),
        pltpu.VMEM((wide, nz + 16, ny), F32),
        pltpu.VMEM(base_shape, F32),
        pltpu.VMEM((part, layers, nz, ny), F32),
        pltpu.SemaphoreType.DMA((part,)),
    ]
    alias = {}
    specs = [SMEM] + [VMEM] * (len(args) - 1)
    if chunk:
        args += [before[2], before[3], before[1], before[0]]
        specs += [VMEM] * 3 + [pl.BlockSpec(memory_space=pltpu.HBM)]
        alias = {len(args) - 1: 0}
    last = chunk == CHUNKS - 1
    shapes = [prior.shape, (devices, ny) if last else (64, ny)]
    if chunk == 0:
        shapes += [base_shape] * 2
    if last:
        scratch.append(pltpu.VMEM((64, ny), F32))
    out = pl.pallas_call(
        functools.partial(sweep_kernel, chunk, devices),
        in_specs=specs,
        out_specs=[pl.BlockSpec(memory_space=pltpu.HBM)] + [VMEM] * (len(shapes) - 1),
        out_shape=[jax.ShapeDtypeStruct(shape, F32) for shape in shapes],
        input_output_aliases=alias,
        scratch_shapes=scratch,
        compiler_params=params(),
        name=f"sweeps{chunk}",
    )(*args)
    return tuple(out) + (tuple(before[2:]) if chunk else ())


def anomaly_kernel(members_all, prior_ref, a_ref, b_ref, c_ref, d_ref, after, out_ref):
    members, _, nz, ny = prior_ref.shape
    flat = prior_ref.reshape(members * nz, ny)
    mean = (a_ref[0] + b_ref[0] + c_ref[0] + d_ref[0]) / members_all
    for z in range(nz):
        rows = flat[pl.ds(z, members, stride=nz), :]
        out_ref[z] = (rows - mean[z : z + 1]).astype(BF16)


def anomalies(prior, totals, members_all, after):
    members, layers, nz, ny = prior.shape
    total = pl.BlockSpec((1, nz, ny), lambda l: (l, 0, 0))
    return pl.pallas_call(
        functools.partial(anomaly_kernel, members_all),
        grid=(layers,),
        in_specs=[pl.BlockSpec((members, 1, nz, ny), lambda l: (0, l, 0, 0))] + [total] * 4 + [pl.BlockSpec(memory_space=pl.ANY)],
        out_specs=pl.BlockSpec((nz, members, ny), lambda l: (l, 0, 0)),
        out_shape=jax.ShapeDtypeStruct((layers * nz, members, ny), BF16),
        compiler_params=params(),
        name="anomalies",
    )(prior, *totals, after)


def slots_kernel(probes, slot_ref, value_ref, var_ref, noise_ref, after, seen_ref, weight_ref, stack):
    members, count = noise_ref.shape
    stack[...] = jnp.zeros_like(stack)
    stack[0:members] = noise_ref[...]
    stack[members : members + 1] = value_ref[...]
    stack[members + 1 : members + 2] = var_ref[...]
    slot = slot_ref[...]
    place = lax.rem(slot, probes) * (count // probes) + slot // probes
    row = lax.broadcasted_iota(jnp.int32, (count, count), 0)
    chosen = jnp.where(row == place, 1.0, 0.0)
    ordered = lax.dot_general(
        chosen, stack[...], (((1,), (1,)), ((), ())), precision=lax.Precision.HIGHEST, preferred_element_type=F32
    )
    value = ordered[:, members : members + 1]
    var = ordered[:, members + 1 : members + 2]
    seen_ref[...] = value + jnp.sqrt(var) * ordered
    weight_ref[...] = jnp.broadcast_to(1.0 / var, weight_ref.shape)


def in_slots(slot, value, var, noise, probes, after):
    count = slot.shape[0]
    shape = jax.ShapeDtypeStruct((count, 128), F32)
    return pl.pallas_call(
        functools.partial(slots_kernel, probes),
        in_specs=[VMEM] * 4 + [pl.BlockSpec(memory_space=pl.ANY)],
        out_specs=[VMEM] * 2,
        out_shape=[shape, shape],
        scratch_shapes=[pltpu.VMEM((128, count), F32)],
        cost_estimate=pl.CostEstimate(flops=0, bytes_accessed=1 << 26, transcendentals=0),
        compiler_params=params(),
        name="slots",
    )(slot[None], value[None], var[None], noise, after)


def dot(a, b, dims):
    return lax.dot_general(a, b, (dims, ((), ())), precision=lax.Precision.HIGHEST, preferred_element_type=F32)


def solve_kernel(members, here, me_ref, vals_ref, seen_ref, weight_ref, beside_any, out_ref, beside_ref, scr, sem):
    fetch = pltpu.make_async_copy(beside_any, beside_ref, sem)
    fetch.start()
    devices, ny = vals_ref.shape
    groups = members // here
    tiles = devices // groups
    probes = 64 // here
    lane = lax.broadcasted_iota(jnp.int32, (tiles, ny), 1)
    parts = [vals_ref[pl.ds(g, tiles, stride=groups), :] for g in range(groups)]
    slabs = []
    for s in range(probes):
        slab = jnp.zeros((tiles, ny), F32)
        for g in range(groups):
            shift = (g - s) * here % ny
            moved = pltpu.roll(parts[g], shift, 1) if shift else parts[g]
            slab = jnp.where((lane >= g * here) & (lane < (g + 1) * here), moved, slab)
        slabs.append(slab)
    predicted = jnp.concatenate(slabs, axis=0)
    lanes = lax.broadcasted_iota(jnp.int32, predicted.shape, 1)
    mean = jnp.sum(predicted, axis=1, keepdims=True) / members
    spread = jnp.where(lanes < members, predicted - mean, 0.0)
    scaled = (spread * weight_ref[...]).T
    gram = dot(scaled, spread, ((1,), (0,)))
    rhs = dot(scaled, seen_ref[...] - predicted, ((1,), (0,)))
    half = 0.5 * jnp.max(jnp.sum(jnp.abs(gram), axis=1))
    alpha = 1.0 / (members - 1.0 + half)
    diagonal = lax.broadcasted_iota(jnp.int32, gram.shape, 0) == lax.broadcasted_iota(jnp.int32, gram.shape, 1)
    error = jnp.where(diagonal, alpha * half, 0.0) - alpha * gram

    def more(state):
        return (state[0] > 1e-9) & (state[1] < 40)

    def double(state):
        size, count, power_of, x = state
        both = dot(power_of, jnp.concatenate([power_of, x], axis=1), ((1,), (0,)))
        return size * size, count + 1, both[:, :ny], x + both[:, ny:]

    x = lax.while_loop(more, double, (half * alpha, 0, error, alpha * rhs))[3]
    me = me_ref[0]
    scr[...] = x
    order = [scr[pl.ds(pl.multiple_of((me ^ g) * here, here), here), :] for g in range(groups)]
    scr[...] = jnp.concatenate(order + [jnp.zeros((ny - members, ny), F32)], axis=0).T
    mine = scr[pl.ds(pl.multiple_of(me * here, here), here), :]
    out_ref[...] = mine[:, :members].astype(BF16)
    fetch.wait()


def solve(vals, seen, weight, me, members, here, beside):
    return pl.pallas_call(
        functools.partial(solve_kernel, members, here),
        in_specs=[SMEM] + [VMEM] * 3 + [pl.BlockSpec(memory_space=pl.ANY)],
        out_specs=[VMEM] * 2,
        out_shape=[jax.ShapeDtypeStruct((here, members), BF16), jax.ShapeDtypeStruct(beside.shape, BF16)],
        scratch_shapes=[pltpu.VMEM((128, 128), F32), pltpu.SemaphoreType.DMA],
        compiler_params=params(),
        name="solve",
    )(me, vals, seen, weight, beside)


def update_kernel(weights_ref, prior_ref, mine_ref, beside_ref, over_ref, far_any, out_hbm, far_ref, out_ref, sems):
    here, layers, nz, ny = prior_ref.shape
    members = weights_ref.shape[1]
    fetch = pltpu.make_async_copy(far_any, far_ref, sems.at[layers])
    fetch.start()
    tall = (here * ROWS, here)
    spread = lax.broadcasted_iota(jnp.int32, tall, 0) // ROWS == lax.broadcasted_iota(jnp.int32, tall, 1)
    wide = (members, members * ROWS)
    column = lax.broadcasted_iota(jnp.int32, wide, 1)
    source = column // (here * ROWS) * here + column % here
    repeat = lax.broadcasted_iota(jnp.int32, wide, 0) == source
    lhs = jnp.dot(jnp.where(spread, 1.0, 0.0).astype(BF16), weights_ref[...], preferred_element_type=F32)
    lhs = jnp.dot(lhs.astype(BF16), jnp.where(repeat, 1.0, 0.0).astype(BF16), preferred_element_type=F32)
    row = lax.broadcasted_iota(jnp.int32, lhs.shape, 0)
    column = lax.broadcasted_iota(jnp.int32, lhs.shape, 1)
    lhs = jnp.where(row % ROWS == column // here % ROWS, lhs, 0.0).astype(BF16)
    places = [(l, z) for l in range(layers) for z in range(0, nz, ROWS)]
    stores = []

    def add(blocks, columns, base, done):
        for p in range(0, len(places), 2):
            pair = places[p : p + 2]
            sides = []
            for l, z in pair:
                first = l * nz + z
                sides.append(jnp.concatenate([b[first : first + ROWS].reshape(ROWS * here, ny) for b in blocks], axis=0))
            update = jnp.dot(columns, jnp.concatenate(sides, axis=1), preferred_element_type=F32)
            for i, (l, z) in enumerate(pair):
                part = update[:, i * ny : (i + 1) * ny]
                for m in range(here):
                    out_ref[m, l, z : z + ROWS] = base[m, l, z : z + ROWS] + part[m * ROWS : (m + 1) * ROWS]
                if done and z + ROWS == nz:
                    stores.append(pltpu.make_async_copy(out_ref.at[:, l], out_hbm.at[:, l], sems.at[l]))
                    stores[-1].start()

    split = 3 * here * ROWS
    add((mine_ref, beside_ref, over_ref), lhs[:, :split], prior_ref, False)
    fetch.wait()
    add((far_ref,), lhs[:, split:], out_ref, True)
    for store in stores:
        store.wait()


def updated(weights, prior, mine, beside, over, far):
    layers = prior.shape[1]
    return pl.pallas_call(
        update_kernel,
        in_specs=[VMEM] * 5 + [pl.BlockSpec(memory_space=pl.ANY)],
        out_specs=pl.BlockSpec(memory_space=pltpu.HBM),
        out_shape=jax.ShapeDtypeStruct(prior.shape, F32),
        scratch_shapes=[
            pltpu.VMEM(mine.shape, BF16),
            pltpu.VMEM(prior.shape, F32),
            pltpu.SemaphoreType.DMA((layers + 1,)),
        ],
        compiler_params=params(),
        name="update",
    )(weights, prior, mine, beside, over, far)


def per_device(prior, base_flow, base_visc, probe_cells, obs_slot, obs_values, obs_var, obs_noise):
    here = prior.shape[0]
    tiles, groups = lax.axis_size("tile"), lax.axis_size("mem")
    members = here * groups
    me = lax.axis_index("mem").astype(jnp.int32).reshape(1)

    def along(x, step):
        return lax.ppermute(x, "tile", [(i, (i + step) % tiles) for i in range(tiles)])

    def across(x, bits):
        return lax.ppermute(x, "mem", [(i, i ^ bits) for i in range(groups)])

    sent = encode(prior, base_flow, base_visc)
    halos = []
    for c in range(CHUNKS):
        ahead = along(sent[2 * c], -1)
        halos.append((along(sent[2 * c + 1], 1), ahead))
    state, states = None, []
    for chunk in range(CHUNKS):
        state = sweeps(prior, base_flow, base_visc, probe_cells, halos[chunk], chunk, state, tiles * groups)
        states.append(state)
    velocity, payload = state[:2]
    total = total_of(prior, halos[0][1])
    totals = [total] + [across(total, bits) for bits in (1, 2, 3)]
    mine = anomalies(prior, totals, float(members), states[1][1])
    beside = across(mine, 1)
    over = across(mine, 2)
    vals = lax.all_to_all(payload, ("tile", "mem"), 0, 0, tiled=True)
    seen, weight = in_slots(obs_slot, obs_values, obs_var, obs_noise, probe_cells.shape[1], payload)
    over = held(over, vals, seen)
    far = across(over, 1)
    weights, beside = solve(vals, seen, weight, me, members, here, beside)
    return velocity, updated(weights, prior, mine, beside, over, far)


def solution(mesh):
    placed = (
        P("mem", "tile", None, None),
        P("tile", None, None),
        P("tile", None, None),
        P("tile", None),
        P(),
        P(),
        P(),
        P(),
    )
    return jax.shard_map(
        per_device,
        mesh=mesh,
        in_specs=placed,
        out_specs=(P("mem", "tile", None, None), P("mem", "tile", None, None)),
        check_vma=False,
    )
```

```python
import functools
import math

import jax
import jax.numpy as jnp
from jax import lax
from jax.experimental import pallas as pl
from jax.experimental.pallas import tpu as pltpu
from jax.sharding import PartitionSpec as P

ITERS = 4
PARTS = ((8, 0), (8, 1))
CHUNKS = len(PARTS)
ROWS = 8
TOTAL_AFTER, ANOMALY_AFTER = 0, 1
LOG_MID = 0.5 * (math.log(0.02) + math.log(0.05))
LOG_HALF = 0.5 * (math.log(0.05) - math.log(0.02)) + 1.0
NU_SCALE = 124.0 / LOG_HALF
FLOW_SCALE = 31.0
LN2 = math.log(2.0)
VMEM = pl.BlockSpec(memory_space=pltpu.VMEM)
SMEM = pl.BlockSpec(memory_space=pltpu.SMEM)
F32 = jnp.float32
BF16 = jnp.bfloat16


def params(mib=24):
    return pltpu.CompilerParams(vmem_limit_bytes=mib * 1024 * 1024)


def power(x):
    return jnp.exp(x * LN2)


def log2_of(x):
    return jnp.log(x) * (1.0 / LN2)


def encode_kernel(odd_ref, prior_hbm, flow_hbm, visc_hbm, *refs):
    outs, (prior, flow, visc, base, sems) = refs[: 2 * CHUNKS], refs[2 * CHUNKS :]
    layers = prior.shape[1]
    copies = [
        pltpu.make_async_copy(visc_hbm, visc, sems.at[0]),
        pltpu.make_async_copy(flow_hbm, flow, sems.at[1]),
    ]
    for c, (part, place) in enumerate(PARTS):
        span = pl.ds(place * part, part)
        copies.append(pltpu.make_async_copy(prior_hbm.at[span], prior.at[span], sems.at[2 + c]))
    for copy in copies:
        copy.start()
    copies[0].wait()
    base[...] = jnp.log(visc[...]) * NU_SCALE - LOG_MID * NU_SCALE
    copies[1].wait()
    for l in range(layers):
        code = power(flow[l] * FLOW_SCALE).astype(BF16)
        outs[0][l] = code
        outs[1][l] = code
    for c, (part, place) in enumerate(PARTS):
        copies[2 + c].wait()
        inner_ref, outer_ref = outs[2 * c], outs[2 * c + 1]
        first = layers if c == 0 else 0

        def members(right_ref, left_ref):
            def member(m, carry):
                for l in range(layers):
                    code = power(prior[place * part + m, l] * NU_SCALE + base[l]).astype(BF16)
                    if l >= 1:
                        right_ref[first + m * 3 + l - 1] = code
                    if l < 3:
                        left_ref[first + m * 3 + l] = code
                return carry

            lax.fori_loop(0, part, member, 0)

        @pl.when(odd_ref[0] == 0)
        def _():
            members(inner_ref, outer_ref)

        @pl.when(odd_ref[0] == 1)
        def _():
            members(outer_ref, inner_ref)


def encode(odd, prior, flow, visc):
    members, layers, nz, ny = prior.shape
    shapes = []
    for c, (part, _) in enumerate(PARTS):
        slabs = 3 * part + (layers if c == 0 else 0)
        shapes += [jax.ShapeDtypeStruct((slabs, nz, ny), BF16)] * 2
    return pl.pallas_call(
        encode_kernel,
        in_specs=[SMEM] + [pl.BlockSpec(memory_space=pltpu.HBM)] * 3,
        out_specs=[VMEM] * len(shapes),
        out_shape=shapes,
        scratch_shapes=[
            pltpu.VMEM(prior.shape, F32),
            pltpu.VMEM(flow.shape, F32),
            pltpu.VMEM(visc.shape, F32),
            pltpu.VMEM(visc.shape, F32),
            pltpu.SemaphoreType.DMA((2 + CHUNKS,)),
        ],
        compiler_params=params(),
        name="encode",
    )(odd, *[pltpu.with_memory_space_constraint(x, pltpu.HBM) for x in (prior, flow, visc)])


def total_kernel(prior_ref, after, out_ref):
    out_ref[...] = prior_ref[0]
    for m in range(1, prior_ref.shape[0]):
        out_ref[...] += prior_ref[m]


def total_of(prior, after):
    return pl.pallas_call(
        total_kernel,
        in_specs=[VMEM, pl.BlockSpec(memory_space=pl.ANY)],
        out_specs=VMEM,
        out_shape=jax.ShapeDtypeStruct(prior.shape[1:], F32),
        compiler_params=params(),
        name="total",
    )(prior, after)


def hold_kernel(*refs):
    pass


def held(value, *after):
    return pl.pallas_call(
        hold_kernel,
        in_specs=[VMEM] * (1 + len(after)),
        out_specs=VMEM,
        out_shape=jax.ShapeDtypeStruct(value.shape, value.dtype),
        input_output_aliases={0: 0},
        compiler_params=params(),
        name="hold",
    )(value, *after)


def neighbours(buf, l, centre, nz, ny):
    lane = lax.broadcasted_iota(jnp.int32, centre.shape, 1)
    below = jnp.where(lane == 0, 0.0, pltpu.roll(centre, 1, 1))
    above = jnp.where(lane == ny - 1, 0.0, pltpu.roll(centre, ny - 1, 1))
    return (buf[l, 7 : 7 + nz] + buf[l, 9 : 9 + nz]) + (below + above)


def put(buf, l, value, nz):
    buf[l, 8 : 8 + nz] = value
    buf[l, 7:8] = value[nz - 1 : nz]
    buf[l, 8 + nz : 9 + nz] = value[0:1]


def sweep_kernel(chunk, devices, odd_ref, cells_ref, prior_ref, flow_ref, visc_ref, inner_ref, outer_ref, *rest):
    _, layers, nz, ny = prior_ref.shape
    part, place = PARTS[chunk]
    wide = layers + 2 * ITERS
    last = chunk == CHUNKS - 1
    odd = odd_ref[0]
    partners = ((inner_ref, 1 - odd), (outer_ref, odd))
    if chunk == 0:
        out_hbm, rows, lap0, adv0, buf0, buf1, nu, out_ref, sems = rest
        for l in range(ITERS):
            for side_ref, ahead in partners:
                flow = log2_of(side_ref[l].astype(F32)) * (1.0 / FLOW_SCALE)
                put(buf0, ahead * (ITERS + layers) + l, flow, nz)
        for l in range(layers):
            put(buf0, ITERS + l, flow_ref[l], nz)
        for l in range(1, wide - 1):
            centre, back = buf0[l, 8 : 8 + nz], buf0[l - 1, 8 : 8 + nz]
            sides = back + buf0[l + 1, 8 : 8 + nz] + neighbours(buf0, l, centre, nz, ny)
            lap0[l - 1] = sides - 6.0 * centre
            adv0[l - 1] = centre - 0.15 * (centre - back) + 0.01
        rows[...] = jnp.zeros_like(rows)
    elif not last:
        lap0, adv0, rows_in, _, out_hbm, rows, buf0, buf1, nu, out_ref, sems = rest
        rows[...] = rows_in[...]
    else:
        lap0, adv0, rows_in, _, out_hbm, lines_ref, buf0, buf1, nu, out_ref, sems, rows = rest
        rows[...] = rows_in[...]
    base_slabs = layers if chunk == 0 else 0

    def store(m):
        return pltpu.make_async_copy(out_ref.at[m], out_hbm.at[place * part + m], sems.at[m])

    def member(m, carry):
        first = base_slabs + m * 3
        for l in range(3):
            for side_ref, ahead in partners:
                code = side_ref[first + l].astype(F32)
                nu[ahead * (3 + layers) + l] = jnp.exp(jnp.log(code) * (1.0 / (LN2 * NU_SCALE)) + LOG_MID)
        for l in range(layers):
            nu[3 + l] = visc_ref[l] * jnp.exp(prior_ref[place * part + m, l])
        for l in range(1, wide - 1):
            put(buf1, l, adv0[l - 1] + nu[l - 1] * lap0[l - 1], nz)
        src, dst = buf1, buf0
        for sweep in range(1, ITERS):
            low, high = sweep + 1, wide - sweep - 1
            back, centre = src[low - 1, 8 : 8 + nz], src[low, 8 : 8 + nz]
            for l in range(low, high):
                front = src[l + 1, 8 : 8 + nz]
                lap = back + front + neighbours(src, l, centre, nz, ny) - 6.0 * centre
                value = centre + nu[l - 1] * lap - 0.15 * (centre - back) + 0.01
                if sweep == ITERS - 1:
                    out_ref[m, l - ITERS] = value
                else:
                    put(dst, l, value, nz)
                back, centre = centre, front
            src, dst = dst, src
        store(m).start()
        for s in range(4):
            cell = cells_ref[0, s]
            layer, z = cell // (nz * ny), lax.rem(cell, nz * ny) // ny
            rows[pl.ds(s * 16 + place * part + m, 1), :] = out_ref[m, layer, pl.ds(z, 1), :]
        return carry

    lax.fori_loop(0, part, member, 0)
    if last:
        lane = lax.broadcasted_iota(jnp.int32, rows.shape, 1)
        row = lax.broadcasted_iota(jnp.int32, rows.shape, 0)
        y = jnp.zeros(rows.shape, jnp.int32)
        for s in range(4):
            y = jnp.where(row // 16 == s, lax.rem(cells_ref[0, s], ny), y)
        picked = jnp.sum(jnp.where(lane == y, rows[...], 0.0), axis=1, keepdims=True)
        line = jnp.sum(jnp.where(lane == row, picked, 0.0), axis=0, keepdims=True)
        lines_ref[...] = jnp.broadcast_to(line, (devices, ny))
    for m in range(part):
        store(m).wait()


def sweeps(odd, prior, flow, visc, cells, halo, chunk, before, devices):
    _, layers, nz, ny = prior.shape
    part, _ = PARTS[chunk]
    wide = layers + 2 * ITERS
    base_shape = (wide - 2, nz, ny)
    args = [odd, cells, prior, flow, visc, *halo]
    scratch = [
        pltpu.VMEM((wide, nz + 16, ny), F32),
        pltpu.VMEM((wide, nz + 16, ny), F32),
        pltpu.VMEM(base_shape, F32),
        pltpu.VMEM((part, layers, nz, ny), F32),
        pltpu.SemaphoreType.DMA((part,)),
    ]
    alias = {}
    specs = [SMEM] * 2 + [VMEM] * (len(args) - 2)
    if chunk:
        args += [before[2], before[3], before[1], before[0]]
        specs += [VMEM] * 3 + [pl.BlockSpec(memory_space=pltpu.HBM)]
        alias = {len(args) - 1: 0}
    last = chunk == CHUNKS - 1
    shapes = [prior.shape, (devices, ny) if last else (64, ny)]
    if chunk == 0:
        shapes += [base_shape] * 2
    if last:
        scratch.append(pltpu.VMEM((64, ny), F32))
    out = pl.pallas_call(
        functools.partial(sweep_kernel, chunk, devices),
        in_specs=specs,
        out_specs=[pl.BlockSpec(memory_space=pltpu.HBM)] + [VMEM] * (len(shapes) - 1),
        out_shape=[jax.ShapeDtypeStruct(shape, F32) for shape in shapes],
        input_output_aliases=alias,
        scratch_shapes=scratch,
        compiler_params=params(),
        name=f"sweeps{chunk}",
    )(*args)
    return tuple(out) + (tuple(before[2:]) if chunk else ())


def anomaly_kernel(members_all, prior_ref, a_ref, b_ref, c_ref, d_ref, *refs):
    out_ref = refs[-1]
    members, _, nz, ny = prior_ref.shape
    flat = prior_ref.reshape(members * nz, ny)
    mean = (a_ref[0] + b_ref[0] + c_ref[0] + d_ref[0]) / members_all
    for z in range(nz):
        rows = flat[pl.ds(z, members, stride=nz), :]
        out_ref[z] = (rows - mean[z : z + 1]).astype(BF16)


def anomalies(prior, totals, members_all, *after):
    members, layers, nz, ny = prior.shape
    total = pl.BlockSpec((1, nz, ny), lambda l: (l, 0, 0))
    return pl.pallas_call(
        functools.partial(anomaly_kernel, members_all),
        grid=(layers,),
        in_specs=[pl.BlockSpec((members, 1, nz, ny), lambda l: (0, l, 0, 0))] + [total] * 4 + [pl.BlockSpec(memory_space=pl.ANY)] * len(after),
        out_specs=pl.BlockSpec((nz, members, ny), lambda l: (l, 0, 0)),
        out_shape=jax.ShapeDtypeStruct((layers * nz, members, ny), BF16),
        compiler_params=params(),
        name="anomalies",
    )(prior, *totals, *after)


def slots_kernel(probes, slot_ref, value_ref, var_ref, noise_ref, after, seen_ref, weight_ref, stack):
    members, count = noise_ref.shape
    stack[...] = jnp.zeros_like(stack)
    stack[0:members] = noise_ref[...]
    stack[members : members + 1] = value_ref[...]
    stack[members + 1 : members + 2] = var_ref[...]
    slot = slot_ref[...]
    place = lax.rem(slot, probes) * (count // probes) + slot // probes
    row = lax.broadcasted_iota(jnp.int32, (count, count), 0)
    chosen = jnp.where(row == place, 1.0, 0.0)
    ordered = lax.dot_general(
        chosen, stack[...], (((1,), (1,)), ((), ())), precision=lax.Precision.HIGHEST, preferred_element_type=F32
    )
    value = ordered[:, members : members + 1]
    var = ordered[:, members + 1 : members + 2]
    seen_ref[...] = value + jnp.sqrt(var) * ordered
    weight_ref[...] = jnp.broadcast_to(1.0 / var, weight_ref.shape)


def in_slots(slot, value, var, noise, probes, after):
    count = slot.shape[0]
    shape = jax.ShapeDtypeStruct((count, 128), F32)
    return pl.pallas_call(
        functools.partial(slots_kernel, probes),
        in_specs=[VMEM] * 4 + [pl.BlockSpec(memory_space=pl.ANY)],
        out_specs=[VMEM] * 2,
        out_shape=[shape, shape],
        scratch_shapes=[pltpu.VMEM((128, count), F32)],
        cost_estimate=pl.CostEstimate(flops=0, bytes_accessed=1 << 26, transcendentals=0),
        compiler_params=params(),
        name="slots",
    )(slot[None], value[None], var[None], noise, after)


def dot(a, b, dims):
    return lax.dot_general(a, b, (dims, ((), ())), precision=lax.Precision.HIGHEST, preferred_element_type=F32)


def solve_kernel(members, here, me_ref, vals_ref, seen_ref, weight_ref, beside_any, out_ref, beside_ref, scr, sem):
    fetch = pltpu.make_async_copy(beside_any, beside_ref, sem)
    fetch.start()
    devices, ny = vals_ref.shape
    groups = members // here
    tiles = devices // groups
    probes = 64 // here
    lane = lax.broadcasted_iota(jnp.int32, (tiles, ny), 1)
    parts = [vals_ref[pl.ds(g, tiles, stride=groups), :] for g in range(groups)]
    slabs = []
    for s in range(probes):
        slab = jnp.zeros((tiles, ny), F32)
        for g in range(groups):
            shift = (g - s) * here % ny
            moved = pltpu.roll(parts[g], shift, 1) if shift else parts[g]
            slab = jnp.where((lane >= g * here) & (lane < (g + 1) * here), moved, slab)
        slabs.append(slab)
    predicted = jnp.concatenate(slabs, axis=0)
    lanes = lax.broadcasted_iota(jnp.int32, predicted.shape, 1)
    mean = jnp.sum(predicted, axis=1, keepdims=True) / members
    spread = jnp.where(lanes < members, predicted - mean, 0.0)
    scaled = (spread * weight_ref[...]).T
    gram = dot(scaled, spread, ((1,), (0,)))
    rhs = dot(scaled, seen_ref[...] - predicted, ((1,), (0,)))
    half = 0.5 * jnp.max(jnp.sum(jnp.abs(gram), axis=1))
    alpha = 1.0 / (members - 1.0 + half)
    diagonal = lax.broadcasted_iota(jnp.int32, gram.shape, 0) == lax.broadcasted_iota(jnp.int32, gram.shape, 1)
    error = jnp.where(diagonal, alpha * half, 0.0) - alpha * gram

    def more(state):
        return (state[0] > 1e-9) & (state[1] < 40)

    def double(state):
        size, count, power_of, x = state
        both = dot(power_of, jnp.concatenate([power_of, x], axis=1), ((1,), (0,)))
        return size * size, count + 1, both[:, :ny], x + both[:, ny:]

    x = lax.while_loop(more, double, (half * alpha, 0, error, alpha * rhs))[3]
    me = me_ref[0]
    scr[...] = x
    order = [scr[pl.ds(pl.multiple_of((me ^ g) * here, here), here), :] for g in range(groups)]
    scr[...] = jnp.concatenate(order + [jnp.zeros((ny - members, ny), F32)], axis=0).T
    mine = scr[pl.ds(pl.multiple_of(me * here, here), here), :]
    out_ref[...] = mine[:, :members].astype(BF16)
    fetch.wait()


def solve(vals, seen, weight, me, members, here, beside):
    return pl.pallas_call(
        functools.partial(solve_kernel, members, here),
        in_specs=[SMEM] + [VMEM] * 3 + [pl.BlockSpec(memory_space=pl.ANY)],
        out_specs=[VMEM] * 2,
        out_shape=[jax.ShapeDtypeStruct((here, members), BF16), jax.ShapeDtypeStruct(beside.shape, BF16)],
        scratch_shapes=[pltpu.VMEM((128, 128), F32), pltpu.SemaphoreType.DMA],
        compiler_params=params(),
        name="solve",
    )(me, vals, seen, weight, beside)


def update_kernel(weights_ref, prior_ref, mine_ref, beside_ref, over_ref, far_any, out_hbm, far_ref, out_ref, sems):
    here, layers, nz, ny = prior_ref.shape
    members = weights_ref.shape[1]
    fetch = pltpu.make_async_copy(far_any, far_ref, sems.at[layers])
    fetch.start()
    tall = (here * ROWS, here)
    spread = lax.broadcasted_iota(jnp.int32, tall, 0) // ROWS == lax.broadcasted_iota(jnp.int32, tall, 1)
    wide = (members, members * ROWS)
    column = lax.broadcasted_iota(jnp.int32, wide, 1)
    source = column // (here * ROWS) * here + column % here
    repeat = lax.broadcasted_iota(jnp.int32, wide, 0) == source
    lhs = jnp.dot(jnp.where(spread, 1.0, 0.0).astype(BF16), weights_ref[...], preferred_element_type=F32)
    lhs = jnp.dot(lhs.astype(BF16), jnp.where(repeat, 1.0, 0.0).astype(BF16), preferred_element_type=F32)
    row = lax.broadcasted_iota(jnp.int32, lhs.shape, 0)
    column = lax.broadcasted_iota(jnp.int32, lhs.shape, 1)
    lhs = jnp.where(row % ROWS == column // here % ROWS, lhs, 0.0).astype(BF16)
    places = [(l, z) for l in range(layers) for z in range(0, nz, ROWS)]
    stores = []

    def add(blocks, columns, base, done):
        for p in range(0, len(places), 2):
            pair = places[p : p + 2]
            sides = []
            for l, z in pair:
                first = l * nz + z
                sides.append(jnp.concatenate([b[first : first + ROWS].reshape(ROWS * here, ny) for b in blocks], axis=0))
            update = jnp.dot(columns, jnp.concatenate(sides, axis=1), preferred_element_type=F32)
            for i, (l, z) in enumerate(pair):
                part = update[:, i * ny : (i + 1) * ny]
                for m in range(here):
                    out_ref[m, l, z : z + ROWS] = base[m, l, z : z + ROWS] + part[m * ROWS : (m + 1) * ROWS]
                if done and z + ROWS == nz:
                    stores.append(pltpu.make_async_copy(out_ref.at[:, l], out_hbm.at[:, l], sems.at[l]))
                    stores[-1].start()

    split = 3 * here * ROWS
    add((mine_ref, beside_ref, over_ref), lhs[:, :split], prior_ref, False)
    fetch.wait()
    add((far_ref,), lhs[:, split:], out_ref, True)
    for store in stores:
        store.wait()


def updated(weights, prior, mine, beside, over, far):
    layers = prior.shape[1]
    return pl.pallas_call(
        update_kernel,
        in_specs=[VMEM] * 5 + [pl.BlockSpec(memory_space=pl.ANY)],
        out_specs=pl.BlockSpec(memory_space=pltpu.HBM),
        out_shape=jax.ShapeDtypeStruct(prior.shape, F32),
        scratch_shapes=[
            pltpu.VMEM(mine.shape, BF16),
            pltpu.VMEM(prior.shape, F32),
            pltpu.SemaphoreType.DMA((layers + 1,)),
        ],
        compiler_params=params(),
        name="update",
    )(weights, prior, mine, beside, over, far)


def per_device(prior, base_flow, base_visc, probe_cells, obs_slot, obs_values, obs_var, obs_noise):
    here = prior.shape[0]
    tiles, groups = lax.axis_size("tile"), lax.axis_size("mem")
    members = here * groups
    me = lax.axis_index("mem").astype(jnp.int32).reshape(1)

    odd = (lax.axis_index("tile") & 1).astype(jnp.int32).reshape(1)

    def swap(x, first):
        pairs = [((first + 2 * i) % tiles, (first + 2 * i + 1) % tiles) for i in range(tiles // 2)]
        return lax.ppermute(x, "tile", pairs + [(b, a) for a, b in pairs])

    def across(x, bits):
        return lax.ppermute(x, "mem", [(i, i ^ bits) for i in range(groups)])

    sent = encode(odd, prior, base_flow, base_visc)
    halos = [(swap(sent[2 * c], 0), swap(sent[2 * c + 1], 1)) for c in range(CHUNKS)]
    state, states = None, []
    for chunk in range(CHUNKS):
        state = sweeps(odd, prior, base_flow, base_visc, probe_cells, halos[chunk], chunk, state, tiles * groups)
        states.append(state)
    velocity, payload = state[:2]
    total = total_of(prior, halos[0][0])
    totals = [total] + [across(total, bits) for bits in (1, 2, 3)]
    mine = anomalies(prior, totals, float(members), states[0][1], *halos[1])
    beside = across(mine, 1)
    over = across(mine, 2)
    vals = lax.all_to_all(payload, ("tile", "mem"), 0, 0, tiled=True)
    seen, weight = in_slots(obs_slot, obs_values, obs_var, obs_noise, probe_cells.shape[1], payload)
    over = held(over, vals, seen)
    far = across(over, 1)
    weights, beside = solve(vals, seen, weight, me, members, here, beside)
    return velocity, updated(weights, prior, mine, beside, over, far)


def solution(mesh):
    placed = (
        P("mem", "tile", None, None),
        P("tile", None, None),
        P("tile", None, None),
        P("tile", None),
        P(),
        P(),
        P(),
        P(),
    )
    return jax.shard_map(
        per_device,
        mesh=mesh,
        in_specs=placed,
        out_specs=(P("mem", "tile", None, None), P("mem", "tile", None, None)),
        check_vma=False,
    )
```

```python
import functools
import math

import jax
import jax.numpy as jnp
from jax import lax
from jax.experimental import pallas as pl
from jax.experimental.pallas import tpu as pltpu
from jax.sharding import PartitionSpec as P

ITERS = 4
PARTS = ((8, 0), (8, 1))
CHUNKS = len(PARTS)
ROWS = 8
STEPS = 1
LOG_MID = 0.5 * (math.log(0.02) + math.log(0.05))
LOG_HALF = 0.5 * (math.log(0.05) - math.log(0.02)) + 1.0
NU_SCALE = 124.0 / LOG_HALF
FLOW_SCALE = 31.0
LN2 = math.log(2.0)
VMEM = pl.BlockSpec(memory_space=pltpu.VMEM)
SMEM = pl.BlockSpec(memory_space=pltpu.SMEM)
F32 = jnp.float32
BF16 = jnp.bfloat16


def params(mib=24):
    return pltpu.CompilerParams(vmem_limit_bytes=mib * 1024 * 1024)


def power(x):
    return jnp.exp(x * LN2)


def log2_of(x):
    return jnp.log(x) * (1.0 / LN2)


def encode_kernel(odd_ref, prior_hbm, flow_hbm, visc_hbm, *refs):
    outs, (prior, flow, visc, base, sems) = refs[: 2 * CHUNKS], refs[2 * CHUNKS :]
    layers = prior.shape[1]
    copies = [
        pltpu.make_async_copy(visc_hbm, visc, sems.at[0]),
        pltpu.make_async_copy(flow_hbm, flow, sems.at[1]),
    ]
    for c, (part, place) in enumerate(PARTS):
        span = pl.ds(place * part, part)
        copies.append(pltpu.make_async_copy(prior_hbm.at[span], prior.at[span], sems.at[2 + c]))
    for copy in copies:
        copy.start()
    copies[0].wait()
    base[...] = jnp.log(visc[...]) * NU_SCALE - LOG_MID * NU_SCALE
    copies[1].wait()
    for l in range(layers):
        code = power(flow[l] * FLOW_SCALE).astype(BF16)
        outs[0][l] = code
        outs[1][l] = code
    for c, (part, place) in enumerate(PARTS):
        copies[2 + c].wait()
        inner_ref, outer_ref = outs[2 * c], outs[2 * c + 1]
        first = layers if c == 0 else 0

        def members(right_ref, left_ref):
            def member(m, carry):
                for l in range(layers):
                    code = power(prior[place * part + m, l] * NU_SCALE + base[l]).astype(BF16)
                    if l >= 1:
                        right_ref[first + m * 3 + l - 1] = code
                    if l < 3:
                        left_ref[first + m * 3 + l] = code
                return carry

            lax.fori_loop(0, part, member, 0)

        @pl.when(odd_ref[0] == 0)
        def _():
            members(inner_ref, outer_ref)

        @pl.when(odd_ref[0] == 1)
        def _():
            members(outer_ref, inner_ref)


def encode(odd, prior, flow, visc):
    members, layers, nz, ny = prior.shape
    shapes = []
    for c, (part, _) in enumerate(PARTS):
        slabs = 3 * part + (layers if c == 0 else 0)
        shapes += [jax.ShapeDtypeStruct((slabs, nz, ny), BF16)] * 2
    return pl.pallas_call(
        encode_kernel,
        in_specs=[SMEM] + [pl.BlockSpec(memory_space=pltpu.HBM)] * 3,
        out_specs=[VMEM] * len(shapes),
        out_shape=shapes,
        scratch_shapes=[
            pltpu.VMEM(prior.shape, F32),
            pltpu.VMEM(flow.shape, F32),
            pltpu.VMEM(visc.shape, F32),
            pltpu.VMEM(visc.shape, F32),
            pltpu.SemaphoreType.DMA((2 + CHUNKS,)),
        ],
        compiler_params=params(),
        name="encode",
    )(odd, *[pltpu.with_memory_space_constraint(x, pltpu.HBM) for x in (prior, flow, visc)])


def total_kernel(prior_ref, after, out_ref):
    out_ref[...] = prior_ref[0]
    for m in range(1, prior_ref.shape[0]):
        out_ref[...] += prior_ref[m]


def total_of(prior, after):
    return pl.pallas_call(
        total_kernel,
        in_specs=[VMEM, pl.BlockSpec(memory_space=pl.ANY)],
        out_specs=VMEM,
        out_shape=jax.ShapeDtypeStruct(prior.shape[1:], F32),
        compiler_params=params(),
        name="total",
    )(prior, after)


def pair_sum_kernel(a_ref, b_ref, out_ref):
    out_ref[...] = a_ref[...] + b_ref[...]


def pair_sum(a, b):
    return pl.pallas_call(
        pair_sum_kernel,
        in_specs=[VMEM] * 2,
        out_specs=VMEM,
        out_shape=jax.ShapeDtypeStruct(a.shape, F32),
        compiler_params=params(),
        name="pair_sum",
    )(a, b)


def hold_kernel(*refs):
    pass


def held(value, *after):
    return pl.pallas_call(
        hold_kernel,
        in_specs=[VMEM] * (1 + len(after)),
        out_specs=VMEM,
        out_shape=jax.ShapeDtypeStruct(value.shape, value.dtype),
        input_output_aliases={0: 0},
        compiler_params=params(),
        name="hold",
    )(value, *after)


def neighbours(buf, l, centre, nz, ny):
    lane = lax.broadcasted_iota(jnp.int32, centre.shape, 1)
    below = jnp.where(lane == 0, 0.0, pltpu.roll(centre, 1, 1))
    above = jnp.where(lane == ny - 1, 0.0, pltpu.roll(centre, ny - 1, 1))
    return (buf[l, 7 : 7 + nz] + buf[l, 9 : 9 + nz]) + (below + above)


def put(buf, l, value, nz):
    buf[l, 8 : 8 + nz] = value
    buf[l, 7:8] = value[nz - 1 : nz]
    buf[l, 8 + nz : 9 + nz] = value[0:1]


def sweep_kernel(chunk, devices, odd_ref, cells_ref, prior_ref, flow_ref, visc_ref, inner_ref, outer_ref, *rest):
    _, layers, nz, ny = prior_ref.shape
    part, place = PARTS[chunk]
    group = part // STEPS
    step = pl.program_id(0)
    wide = layers + 2 * ITERS
    last = chunk == CHUNKS - 1
    odd = odd_ref[0]
    partners = ((inner_ref, 1 - odd), (outer_ref, odd))
    if chunk == 0:
        out_ref, rows, lap0, adv0, buf0, buf1, nu = rest

        @pl.when(step == 0)
        def _():
            for l in range(ITERS):
                for side_ref, ahead in partners:
                    flow = log2_of(side_ref[l].astype(F32)) * (1.0 / FLOW_SCALE)
                    put(buf0, ahead * (ITERS + layers) + l, flow, nz)
            for l in range(layers):
                put(buf0, ITERS + l, flow_ref[l], nz)
            for l in range(1, wide - 1):
                centre, back = buf0[l, 8 : 8 + nz], buf0[l - 1, 8 : 8 + nz]
                sides = back + buf0[l + 1, 8 : 8 + nz] + neighbours(buf0, l, centre, nz, ny)
                lap0[l - 1] = sides - 6.0 * centre
                adv0[l - 1] = centre - 0.15 * (centre - back) + 0.01
            rows[...] = jnp.zeros_like(rows)

    elif not last:
        lap0, adv0, rows_in, _, out_ref, rows, buf0, buf1, nu = rest

        @pl.when(step == 0)
        def _():
            rows[...] = rows_in[...]

    else:
        lap0, adv0, rows_in, _, out_ref, lines_ref, buf0, buf1, nu, rows = rest

        @pl.when(step == 0)
        def _():
            rows[...] = rows_in[...]

    base_slabs = layers if chunk == 0 else 0

    def member(m, carry):
        index = step * group + m
        first = base_slabs + index * 3
        for l in range(3):
            for side_ref, ahead in partners:
                code = side_ref[first + l].astype(F32)
                nu[ahead * (3 + layers) + l] = jnp.exp(jnp.log(code) * (1.0 / (LN2 * NU_SCALE)) + LOG_MID)
        for l in range(layers):
            nu[3 + l] = visc_ref[l] * jnp.exp(prior_ref[place * part + index, l])
        for l in range(1, wide - 1):
            put(buf1, l, adv0[l - 1] + nu[l - 1] * lap0[l - 1], nz)
        src, dst = buf1, buf0
        for sweep in range(1, ITERS):
            low, high = sweep + 1, wide - sweep - 1
            back, centre = src[low - 1, 8 : 8 + nz], src[low, 8 : 8 + nz]
            for l in range(low, high):
                front = src[l + 1, 8 : 8 + nz]
                lap = back + front + neighbours(src, l, centre, nz, ny) - 6.0 * centre
                value = centre + nu[l - 1] * lap - 0.15 * (centre - back) + 0.01
                if sweep == ITERS - 1:
                    out_ref[m, l - ITERS] = value
                else:
                    put(dst, l, value, nz)
                back, centre = centre, front
            src, dst = dst, src
        for s in range(4):
            cell = cells_ref[0, s]
            layer, z = cell // (nz * ny), lax.rem(cell, nz * ny) // ny
            rows[pl.ds(s * 16 + place * part + index, 1), :] = out_ref[m, layer, pl.ds(z, 1), :]
        return carry

    lax.fori_loop(0, group, member, 0)
    if last:

        @pl.when(step == STEPS - 1)
        def _():
            lane = lax.broadcasted_iota(jnp.int32, rows.shape, 1)
            row = lax.broadcasted_iota(jnp.int32, rows.shape, 0)
            y = jnp.zeros(rows.shape, jnp.int32)
            for s in range(4):
                y = jnp.where(row // 16 == s, lax.rem(cells_ref[0, s], ny), y)
            picked = jnp.sum(jnp.where(lane == y, rows[...], 0.0), axis=1, keepdims=True)
            line = jnp.sum(jnp.where(lane == row, picked, 0.0), axis=0, keepdims=True)
            lines_ref[...] = jnp.broadcast_to(line, (devices, ny))


def sweeps(odd, prior, flow, visc, cells, halo, chunk, before, devices):
    _, layers, nz, ny = prior.shape
    part, place = PARTS[chunk]
    wide = layers + 2 * ITERS
    base_shape = (wide - 2, nz, ny)
    args = [odd, cells, prior, flow, visc, *halo]
    scratch = [
        pltpu.VMEM((wide, nz + 16, ny), F32),
        pltpu.VMEM((wide, nz + 16, ny), F32),
        pltpu.VMEM(base_shape, F32),
    ]
    alias = {}
    specs = [SMEM] * 2 + [VMEM] * (len(args) - 2)
    if chunk:
        args += [before[2], before[3], before[1], before[0]]
        specs += [VMEM] * 3 + [pl.BlockSpec(memory_space=pltpu.HBM)]
        alias = {len(args) - 1: 0}
    last = chunk == CHUNKS - 1
    shapes = [prior.shape, (devices, ny) if last else (64, ny)]
    if chunk == 0:
        shapes += [base_shape] * 2
    if last:
        scratch.append(pltpu.VMEM((64, ny), F32))
    out = pl.pallas_call(
        functools.partial(sweep_kernel, chunk, devices),
        grid=(STEPS,),
        in_specs=specs,
        out_specs=[pl.BlockSpec((part // STEPS, layers, nz, ny), lambda i: (place * STEPS + i, 0, 0, 0))] + [VMEM] * (len(shapes) - 1),
        out_shape=[jax.ShapeDtypeStruct(shape, F32) for shape in shapes],
        input_output_aliases=alias,
        scratch_shapes=scratch,
        compiler_params=params(),
        name=f"sweeps{chunk}",
    )(*args)
    return tuple(out) + (tuple(before[2:]) if chunk else ())


def anomaly_kernel(members_all, prior_ref, a_ref, b_ref, *refs):
    out_ref = refs[-1]
    members, _, nz, ny = prior_ref.shape
    flat = prior_ref.reshape(members * nz, ny)
    mean = (a_ref[0] + b_ref[0]) / members_all
    for z in range(nz):
        rows = flat[pl.ds(z, members, stride=nz), :]
        out_ref[z] = (rows - mean[z : z + 1]).astype(BF16)


def anomalies(prior, totals, members_all, *after):
    members, layers, nz, ny = prior.shape
    total = pl.BlockSpec((1, nz, ny), lambda l: (l, 0, 0))
    return pl.pallas_call(
        functools.partial(anomaly_kernel, members_all),
        grid=(layers,),
        in_specs=[pl.BlockSpec((members, 1, nz, ny), lambda l: (0, l, 0, 0))] + [total] * 2 + [pl.BlockSpec(memory_space=pl.ANY)] * len(after),
        out_specs=pl.BlockSpec((nz, members, ny), lambda l: (l, 0, 0)),
        out_shape=jax.ShapeDtypeStruct((layers * nz, members, ny), BF16),
        compiler_params=params(),
        name="anomalies",
    )(prior, *totals, *after)


def slots_kernel(probes, slot_ref, value_ref, var_ref, noise_ref, after, seen_ref, weight_ref, stack):
    members, count = noise_ref.shape
    stack[...] = jnp.zeros_like(stack)
    stack[0:members] = noise_ref[...]
    stack[members : members + 1] = value_ref[...]
    stack[members + 1 : members + 2] = var_ref[...]
    slot = slot_ref[...]
    place = lax.rem(slot, probes) * (count // probes) + slot // probes
    row = lax.broadcasted_iota(jnp.int32, (count, count), 0)
    chosen = jnp.where(row == place, 1.0, 0.0)
    ordered = lax.dot_general(
        chosen, stack[...], (((1,), (1,)), ((), ())), precision=lax.Precision.HIGHEST, preferred_element_type=F32
    )
    value = ordered[:, members : members + 1]
    var = ordered[:, members + 1 : members + 2]
    seen_ref[...] = value + jnp.sqrt(var) * ordered
    weight_ref[...] = jnp.broadcast_to(1.0 / var, weight_ref.shape)


def in_slots(slot, value, var, noise, probes, after):
    count = slot.shape[0]
    shape = jax.ShapeDtypeStruct((count, 128), F32)
    return pl.pallas_call(
        functools.partial(slots_kernel, probes),
        in_specs=[VMEM] * 4 + [pl.BlockSpec(memory_space=pl.ANY)],
        out_specs=[VMEM] * 2,
        out_shape=[shape, shape],
        scratch_shapes=[pltpu.VMEM((128, count), F32)],
        cost_estimate=pl.CostEstimate(flops=0, bytes_accessed=1 << 26, transcendentals=0),
        compiler_params=params(),
        name="slots",
    )(slot[None], value[None], var[None], noise, after)


def dot(a, b, dims):
    return lax.dot_general(a, b, (dims, ((), ())), precision=lax.Precision.HIGHEST, preferred_element_type=F32)


def solve_kernel(members, here, me_ref, vals_ref, seen_ref, weight_ref, beside_any, out_ref, beside_ref, scr, sem):
    fetch = pltpu.make_async_copy(beside_any, beside_ref, sem)
    fetch.start()
    devices, ny = vals_ref.shape
    groups = members // here
    tiles = devices // groups
    probes = 64 // here
    lane = lax.broadcasted_iota(jnp.int32, (tiles, ny), 1)
    parts = [vals_ref[pl.ds(g, tiles, stride=groups), :] for g in range(groups)]
    slabs = []
    for s in range(probes):
        slab = jnp.zeros((tiles, ny), F32)
        for g in range(groups):
            shift = (g - s) * here % ny
            moved = pltpu.roll(parts[g], shift, 1) if shift else parts[g]
            slab = jnp.where((lane >= g * here) & (lane < (g + 1) * here), moved, slab)
        slabs.append(slab)
    predicted = jnp.concatenate(slabs, axis=0)
    lanes = lax.broadcasted_iota(jnp.int32, predicted.shape, 1)
    mean = jnp.sum(predicted, axis=1, keepdims=True) / members
    spread = jnp.where(lanes < members, predicted - mean, 0.0)
    scaled = (spread * weight_ref[...]).T
    gram = dot(scaled, spread, ((1,), (0,)))
    rhs = dot(scaled, seen_ref[...] - predicted, ((1,), (0,)))
    half = 0.5 * jnp.max(jnp.sum(jnp.abs(gram), axis=1))
    alpha = 1.0 / (members - 1.0 + half)
    diagonal = lax.broadcasted_iota(jnp.int32, gram.shape, 0) == lax.broadcasted_iota(jnp.int32, gram.shape, 1)
    error = jnp.where(diagonal, alpha * half, 0.0) - alpha * gram

    def more(state):
        return (state[0] > 1e-9) & (state[1] < 40)

    def double(state):
        size, count, power_of, x = state
        both = dot(power_of, jnp.concatenate([power_of, x], axis=1), ((1,), (0,)))
        return size * size, count + 1, both[:, :ny], x + both[:, ny:]

    x = lax.while_loop(more, double, (half * alpha, 0, error, alpha * rhs))[3]
    me = me_ref[0]
    scr[...] = x
    order = [scr[pl.ds(pl.multiple_of((me ^ g) * here, here), here), :] for g in range(groups)]
    scr[...] = jnp.concatenate(order + [jnp.zeros((ny - members, ny), F32)], axis=0).T
    mine = scr[pl.ds(pl.multiple_of(me * here, here), here), :]
    out_ref[...] = mine[:, :members].astype(BF16)
    fetch.wait()


def solve(vals, seen, weight, me, members, here, beside):
    return pl.pallas_call(
        functools.partial(solve_kernel, members, here),
        in_specs=[SMEM] + [VMEM] * 3 + [pl.BlockSpec(memory_space=pl.ANY)],
        out_specs=[VMEM] * 2,
        out_shape=[jax.ShapeDtypeStruct((here, members), BF16), jax.ShapeDtypeStruct(beside.shape, BF16)],
        scratch_shapes=[pltpu.VMEM((128, 128), F32), pltpu.SemaphoreType.DMA],
        compiler_params=params(),
        name="solve",
    )(me, vals, seen, weight, beside)


def update_kernel(weights_ref, prior_ref, mine_ref, beside_ref, over_ref, far_any, out_hbm, far_ref, out_ref, sems):
    here, layers, nz, ny = prior_ref.shape
    members = weights_ref.shape[1]
    fetch = pltpu.make_async_copy(far_any, far_ref, sems.at[layers])
    fetch.start()
    tall = (here * ROWS, here)
    spread = lax.broadcasted_iota(jnp.int32, tall, 0) // ROWS == lax.broadcasted_iota(jnp.int32, tall, 1)
    wide = (members, members * ROWS)
    column = lax.broadcasted_iota(jnp.int32, wide, 1)
    source = column // (here * ROWS) * here + column % here
    repeat = lax.broadcasted_iota(jnp.int32, wide, 0) == source
    lhs = jnp.dot(jnp.where(spread, 1.0, 0.0).astype(BF16), weights_ref[...], preferred_element_type=F32)
    lhs = jnp.dot(lhs.astype(BF16), jnp.where(repeat, 1.0, 0.0).astype(BF16), preferred_element_type=F32)
    row = lax.broadcasted_iota(jnp.int32, lhs.shape, 0)
    column = lax.broadcasted_iota(jnp.int32, lhs.shape, 1)
    lhs = jnp.where(row % ROWS == column // here % ROWS, lhs, 0.0).astype(BF16)
    places = [(l, z) for l in range(layers) for z in range(0, nz, ROWS)]
    stores = []

    def add(blocks, columns, base, done):
        for p in range(0, len(places), 2):
            pair = places[p : p + 2]
            sides = []
            for l, z in pair:
                first = l * nz + z
                sides.append(jnp.concatenate([b[first : first + ROWS].reshape(ROWS * here, ny) for b in blocks], axis=0))
            update = jnp.dot(columns, jnp.concatenate(sides, axis=1), preferred_element_type=F32)
            for i, (l, z) in enumerate(pair):
                part = update[:, i * ny : (i + 1) * ny]
                for m in range(here):
                    out_ref[m, l, z : z + ROWS] = base[m, l, z : z + ROWS] + part[m * ROWS : (m + 1) * ROWS]
                if done and z + ROWS == nz:
                    stores.append(pltpu.make_async_copy(out_ref.at[:, l], out_hbm.at[:, l], sems.at[l]))
                    stores[-1].start()

    split = 3 * here * ROWS
    add((mine_ref, beside_ref, over_ref), lhs[:, :split], prior_ref, False)
    fetch.wait()
    add((far_ref,), lhs[:, split:], out_ref, True)
    for store in stores:
        store.wait()


def updated(weights, prior, mine, beside, over, far):
    layers = prior.shape[1]
    return pl.pallas_call(
        update_kernel,
        in_specs=[VMEM] * 5 + [pl.BlockSpec(memory_space=pl.ANY)],
        out_specs=pl.BlockSpec(memory_space=pltpu.HBM),
        out_shape=jax.ShapeDtypeStruct(prior.shape, F32),
        scratch_shapes=[
            pltpu.VMEM(mine.shape, BF16),
            pltpu.VMEM(prior.shape, F32),
            pltpu.SemaphoreType.DMA((layers + 1,)),
        ],
        compiler_params=params(),
        name="update",
    )(weights, prior, mine, beside, over, far)


def per_device(prior, base_flow, base_visc, probe_cells, obs_slot, obs_values, obs_var, obs_noise):
    here = prior.shape[0]
    tiles, groups = lax.axis_size("tile"), lax.axis_size("mem")
    members = here * groups
    me = lax.axis_index("mem").astype(jnp.int32).reshape(1)

    odd = (lax.axis_index("tile") & 1).astype(jnp.int32).reshape(1)

    def swap(x, first):
        pairs = [((first + 2 * i) % tiles, (first + 2 * i + 1) % tiles) for i in range(tiles // 2)]
        return lax.ppermute(x, "tile", pairs + [(b, a) for a, b in pairs])

    def across(x, bits):
        return lax.ppermute(x, "mem", [(i, i ^ bits) for i in range(groups)])

    sent = encode(odd, prior, base_flow, base_visc)
    halos = [(swap(sent[2 * c], 0), swap(sent[2 * c + 1], 1)) for c in range(CHUNKS)]
    state, states = None, []
    for chunk in range(CHUNKS):
        state = sweeps(odd, prior, base_flow, base_visc, probe_cells, halos[chunk], chunk, state, tiles * groups)
        states.append(state)
    velocity, payload = state[:2]
    total = total_of(prior, sent[0])
    chip = pair_sum(total, across(total, 1))
    totals = [chip, across(chip, 2)]
    mine = anomalies(prior, totals, float(members), states[0][1], *halos[1])
    beside = across(mine, 1)
    over = across(mine, 2)
    vals = lax.all_to_all(payload, ("tile", "mem"), 0, 0, tiled=True)
    seen, weight = in_slots(obs_slot, obs_values, obs_var, obs_noise, probe_cells.shape[1], payload)
    over = held(over, vals, seen)
    far = across(over, 1)
    weights, beside = solve(vals, seen, weight, me, members, here, beside)
    return velocity, updated(weights, prior, mine, beside, over, far)


def solution(mesh):
    placed = (
        P("mem", "tile", None, None),
        P("tile", None, None),
        P("tile", None, None),
        P("tile", None),
        P(),
        P(),
        P(),
        P(),
    )
    return jax.shard_map(
        per_device,
        mesh=mesh,
        in_specs=placed,
        out_specs=(P("mem", "tile", None, None), P("mem", "tile", None, None)),
        check_vma=False,
    )
```

```python
import functools
import math

import jax
import jax.numpy as jnp
from jax import lax
from jax.experimental import pallas as pl
from jax.experimental.pallas import tpu as pltpu
from jax.sharding import PartitionSpec as P

ITERS = 4
PARTS = ((8, 0), (8, 1))
CHUNKS = len(PARTS)
ROWS = 8
WINDOW = 8
WAYS = 4
STEPS = 1
LOG_MID = 0.5 * (math.log(0.02) + math.log(0.05))
LOG_HALF = 0.5 * (math.log(0.05) - math.log(0.02)) + 1.0
NU_SCALE = 124.0 / LOG_HALF
FLOW_SCALE = 31.0
LN2 = math.log(2.0)
VMEM = pl.BlockSpec(memory_space=pltpu.VMEM)
SMEM = pl.BlockSpec(memory_space=pltpu.SMEM)
F32 = jnp.float32
BF16 = jnp.bfloat16


def params(mib=24):
    return pltpu.CompilerParams(vmem_limit_bytes=mib * 1024 * 1024)


def power(x):
    return jnp.exp(x * LN2)


def log2_of(x):
    return jnp.log(x) * (1.0 / LN2)


def encode_kernel(odd_ref, prior_hbm, flow_hbm, visc_hbm, *refs):
    outs, (prior, flow, visc, base, sems) = refs[: 2 * CHUNKS], refs[2 * CHUNKS :]
    layers = prior.shape[1]
    copies = [
        pltpu.make_async_copy(visc_hbm, visc, sems.at[0]),
        pltpu.make_async_copy(flow_hbm, flow, sems.at[1]),
    ]
    for c, (part, place) in enumerate(PARTS):
        span = pl.ds(place * part, part)
        copies.append(pltpu.make_async_copy(prior_hbm.at[span], prior.at[span], sems.at[2 + c]))
    for copy in copies:
        copy.start()
    copies[0].wait()
    base[...] = jnp.log(visc[...]) * NU_SCALE - LOG_MID * NU_SCALE
    copies[1].wait()
    for l in range(layers):
        code = power(flow[l] * FLOW_SCALE).astype(BF16)
        outs[0][l] = code
        outs[1][l] = code
    for c, (part, place) in enumerate(PARTS):
        copies[2 + c].wait()
        inner_ref, outer_ref = outs[2 * c], outs[2 * c + 1]
        first = layers if c == 0 else 0

        def members(right_ref, left_ref):
            def member(m, carry):
                for l in range(layers):
                    code = power(prior[place * part + m, l] * NU_SCALE + base[l]).astype(BF16)
                    if l >= 1:
                        right_ref[first + m * 3 + l - 1] = code
                    if l < 3:
                        left_ref[first + m * 3 + l] = code
                return carry

            lax.fori_loop(0, part, member, 0)

        @pl.when(odd_ref[0] == 0)
        def _():
            members(inner_ref, outer_ref)

        @pl.when(odd_ref[0] == 1)
        def _():
            members(outer_ref, inner_ref)


def encode(odd, prior, flow, visc):
    members, layers, nz, ny = prior.shape
    shapes = []
    for c, (part, _) in enumerate(PARTS):
        slabs = 3 * part + (layers if c == 0 else 0)
        shapes += [jax.ShapeDtypeStruct((slabs, nz, ny), BF16)] * 2
    return pl.pallas_call(
        encode_kernel,
        in_specs=[SMEM] + [pl.BlockSpec(memory_space=pltpu.HBM)] * 3,
        out_specs=[VMEM] * len(shapes),
        out_shape=shapes,
        scratch_shapes=[
            pltpu.VMEM(prior.shape, F32),
            pltpu.VMEM(flow.shape, F32),
            pltpu.VMEM(visc.shape, F32),
            pltpu.VMEM(visc.shape, F32),
            pltpu.SemaphoreType.DMA((2 + CHUNKS,)),
        ],
        compiler_params=params(),
        name="encode",
    )(odd, *[pltpu.with_memory_space_constraint(x, pltpu.HBM) for x in (prior, flow, visc)])


def total_kernel(prior_ref, after, out_ref):
    out_ref[...] = prior_ref[0]
    for m in range(1, prior_ref.shape[0]):
        out_ref[...] += prior_ref[m]


def total_of(prior, after):
    return pl.pallas_call(
        total_kernel,
        in_specs=[VMEM, pl.BlockSpec(memory_space=pl.ANY)],
        out_specs=VMEM,
        out_shape=jax.ShapeDtypeStruct(prior.shape[1:], F32),
        compiler_params=params(),
        name="total",
    )(prior, after)


def pair_sum_kernel(a_ref, b_ref, out_ref):
    out_ref[...] = a_ref[...] + b_ref[...]


def pair_sum(a, b):
    return pl.pallas_call(
        pair_sum_kernel,
        in_specs=[VMEM] * 2,
        out_specs=VMEM,
        out_shape=jax.ShapeDtypeStruct(a.shape, F32),
        compiler_params=params(),
        name="pair_sum",
    )(a, b)


def hold_kernel(*refs):
    pass


def held(value, *after):
    return pl.pallas_call(
        hold_kernel,
        in_specs=[VMEM] * (1 + len(after)),
        out_specs=VMEM,
        out_shape=jax.ShapeDtypeStruct(value.shape, value.dtype),
        input_output_aliases={0: 0},
        compiler_params=params(),
        name="hold",
    )(value, *after)


def neighbours(buf, l, centre, nz, ny):
    lane = lax.broadcasted_iota(jnp.int32, centre.shape, 1)
    below = jnp.where(lane == 0, 0.0, pltpu.roll(centre, 1, 1))
    above = jnp.where(lane == ny - 1, 0.0, pltpu.roll(centre, ny - 1, 1))
    return (buf[l, 7 : 7 + nz] + buf[l, 9 : 9 + nz]) + (below + above)


def put(buf, l, value, nz):
    buf[l, 8 : 8 + nz] = value
    buf[l, 7:8] = value[nz - 1 : nz]
    buf[l, 8 + nz : 9 + nz] = value[0:1]


def wrap(buf, l, value, nz):
    buf[l, 8 : 8 + nz] = value
    buf[l, 5:8] = value[nz - 3 : nz]
    buf[l, 8 + nz : 12 + nz] = value[0:4]


def viscosity_from(code):
    return jnp.exp(jnp.log(code.astype(F32)) * (1.0 / (LN2 * NU_SCALE)) + LOG_MID)


def probe_kernel(devices, odd_ref, cells_ref, prior_ref, visc_ref, inner_ref, outer_ref, lap0, adv0, rows_in, lines_ref, token_ref, nus, held_rows, rows):
    _, layers, nz, ny = prior_ref.shape
    part, place = PARTS[-1]
    odd = odd_ref[0]
    rows[...] = rows_in[...]
    lane = lax.broadcasted_iota(jnp.int32, (WINDOW, ny), 1)

    def step(slot, back, centre, front, visc):
        held_rows[slot, 4 : 4 + WINDOW] = centre
        sides = held_rows[slot, 3 : 3 + WINDOW] + held_rows[slot, 5 : 5 + WINDOW]
        below = jnp.where(lane == 0, 0.0, pltpu.roll(centre, 1, 1))
        above = jnp.where(lane == ny - 1, 0.0, pltpu.roll(centre, ny - 1, 1))
        lap = back + front + (sides + (below + above)) - 6.0 * centre
        return centre + visc * lap - 0.15 * (centre - back) + 0.01

    def member(m, carry, way):
        nu = nus.at[way]
        for l in range(3):
            for side_ref, ahead in ((inner_ref, 1 - odd), (outer_ref, odd)):
                wrap(nu, ahead * (3 + layers) + l, viscosity_from(side_ref[m * 3 + l]), nz)
        for l in range(layers):
            wrap(nu, 3 + l, visc_ref[l] * jnp.exp(prior_ref[place * part + m, l]), nz)
        for s in range(4):
            cell = cells_ref[0, s]
            layer, z = cell // (nz * ny), lax.rem(cell, nz * ny) // ny
            window = pl.ds(z + 5, WINDOW)
            reach = [layer + j for j in range(2 * ITERS - 1)]
            visc = [nu[l, window] for l in reach]
            speed = [adv0[l, window] + v * lap0[l, window] for l, v in zip(reach, visc)]
            slot = (way * 4 + s) * 9
            for _ in range(1, ITERS):
                visc = visc[1:-1]
                speed = [step(slot + k, *speed[k : k + 3], v) for k, v in enumerate(visc)]
                slot += len(visc)
            rows[pl.ds(s * 16 + place * part + m, 1), :] = speed[0][3:4]
        return carry

    def one_group(i, carry):
        for way in range(WAYS):
            member(i * WAYS + way, carry, way)
        return carry

    lax.fori_loop(0, part // WAYS, one_group, 0)
    lane = lax.broadcasted_iota(jnp.int32, rows.shape, 1)
    row = lax.broadcasted_iota(jnp.int32, rows.shape, 0)
    y = jnp.zeros(rows.shape, jnp.int32)
    for s in range(4):
        y = jnp.where(row // 16 == s, lax.rem(cells_ref[0, s], ny), y)
    picked = jnp.sum(jnp.where(lane == y, rows[...], 0.0), axis=1, keepdims=True)
    line = jnp.sum(jnp.where(lane == row, picked, 0.0), axis=0, keepdims=True)
    lines_ref[...] = jnp.broadcast_to(line, (devices, ny))
    token_ref[...] = rows[0:8]


def probes(odd, prior, visc, cells, halo, first, devices):
    _, layers, nz, ny = prior.shape
    _, rows, lap0, adv0 = first
    return pl.pallas_call(
        functools.partial(probe_kernel, devices),
        in_specs=[SMEM] * 2 + [VMEM] * 7,
        out_specs=[VMEM] * 2,
        out_shape=[jax.ShapeDtypeStruct((devices, ny), F32), jax.ShapeDtypeStruct((8, ny), F32)],
        scratch_shapes=[
            pltpu.VMEM((WAYS,) + lap0.shape, F32),
            pltpu.VMEM((36 * WAYS, WINDOW + 8, ny), F32),
            pltpu.VMEM(rows.shape, F32),
        ],
        compiler_params=params(),
        name="probes",
    )(odd, cells, prior, visc, *halo, lap0, adv0, rows)


def sweep_kernel(chunk, odd_ref, cells_ref, prior_ref, flow_ref, visc_ref, inner_ref, outer_ref, *rest):
    _, layers, nz, ny = prior_ref.shape
    part, place = PARTS[chunk]
    group = part // STEPS
    step = pl.program_id(0)
    wide = layers + 2 * ITERS
    odd = odd_ref[0]
    partners = ((inner_ref, 1 - odd), (outer_ref, odd))
    if chunk == 0:
        _, out_ref, rows, lap0, adv0, buf0, buf1, nu = rest
        prior, offset = prior_ref, place * part

        @pl.when(step == 0)
        def _():
            for l in range(ITERS):
                for side_ref, ahead in partners:
                    flow = log2_of(side_ref[l].astype(F32)) * (1.0 / FLOW_SCALE)
                    put(buf0, ahead * (ITERS + layers) + l, flow, nz)
            for l in range(layers):
                put(buf0, ITERS + l, flow_ref[l], nz)
            for l in range(1, wide - 1):
                centre, back = buf0[l, 8 : 8 + nz], buf0[l - 1, 8 : 8 + nz]
                sides = back + buf0[l + 1, 8 : 8 + nz] + neighbours(buf0, l, centre, nz, ny)
                wrap(lap0, l - 1, sides - 6.0 * centre, nz)
                wrap(adv0, l - 1, centre - 0.15 * (centre - back) + 0.01, nz)
            rows[...] = jnp.zeros_like(rows)

    else:
        sources, (_, _, out_ref, token_ref, buf0, buf1, nu), (lap0, adv0, *sides, prior, sems) = rest[:2], rest[2:9], rest[9:]
        copies = [
            pltpu.make_async_copy(source, target, sems.at[i])
            for i, (source, target) in enumerate(
                zip(
                    (prior_ref.at[pl.ds(place * part, part)], inner_ref, outer_ref) + tuple(sources),
                    (prior, *sides, lap0, adv0),
                )
            )
        ]
        for copy in copies:
            copy.start()
        for copy in copies:
            copy.wait()
        partners = ((sides[0], 1 - odd), (sides[1], odd))
        offset = 0
        token_ref[...] = jnp.zeros_like(token_ref)

    base_slabs = layers if chunk == 0 else 0

    def member(m, carry):
        index = step * group + m
        first = base_slabs + index * 3
        for l in range(3):
            for side_ref, ahead in partners:
                code = side_ref[first + l]
                nu[ahead * (3 + layers) + l] = viscosity_from(code)
        for l in range(layers):
            nu[3 + l] = visc_ref[l] * jnp.exp(prior[offset + index, l])
        for l in range(1, wide - 1):
            put(buf1, l, adv0[l - 1, 8 : 8 + nz] + nu[l - 1] * lap0[l - 1, 8 : 8 + nz], nz)
        src, dst = buf1, buf0
        for sweep in range(1, ITERS):
            low, high = sweep + 1, wide - sweep - 1
            back, centre = src[low - 1, 8 : 8 + nz], src[low, 8 : 8 + nz]
            for l in range(low, high):
                front = src[l + 1, 8 : 8 + nz]
                lap = back + front + neighbours(src, l, centre, nz, ny) - 6.0 * centre
                value = centre + nu[l - 1] * lap - 0.15 * (centre - back) + 0.01
                if sweep == ITERS - 1:
                    out_ref[m, l - ITERS] = value
                else:
                    put(dst, l, value, nz)
                back, centre = centre, front
            src, dst = dst, src
        if chunk == 0:
            for s in range(4):
                cell = cells_ref[0, s]
                layer, z = cell // (nz * ny), lax.rem(cell, nz * ny) // ny
                rows[pl.ds(s * 16 + place * part + index, 1), :] = out_ref[m, layer, pl.ds(z, 1), :]
        return carry

    lax.fori_loop(0, group, member, 0)


def sweeps(odd, prior, flow, visc, cells, halo, chunk, before=None, after=None):
    _, layers, nz, ny = prior.shape
    part, place = PARTS[chunk]
    wide = layers + 2 * ITERS
    padded = (wide - 2, nz + 16, ny)
    anywhere = pl.BlockSpec(memory_space=pl.ANY)
    hbm = pl.BlockSpec(memory_space=pltpu.HBM)
    args = [odd, cells, prior, flow, visc]
    specs = [SMEM] * 2 + [VMEM] * 3
    scratch = [
        pltpu.VMEM((wide, nz + 16, ny), F32),
        pltpu.VMEM((wide, nz + 16, ny), F32),
        pltpu.VMEM((wide - 2, nz, ny), F32),
    ]
    alias = {}
    shapes = [prior.shape]
    if chunk:
        velocity, _, lap0, adv0 = before
        args += [pltpu.with_memory_space_constraint(x, pltpu.HBM) for x in (*halo, lap0, adv0)] + [after, velocity]
        specs += [hbm] * 4 + [anywhere, hbm]
        args[2:4] = [pltpu.with_memory_space_constraint(x, pltpu.HBM) for x in (prior, flow)]
        specs[2:4] = [hbm, hbm]
        alias = {len(args) - 1: 0}
        scratch += [pltpu.VMEM(padded, F32)] * 2 + [pltpu.VMEM(halo[0].shape, BF16)] * 2
        scratch += [pltpu.VMEM((part, layers, nz, ny), F32), pltpu.SemaphoreType.DMA((5,))]
        shapes += [(8, ny)]
    else:
        args += [*halo, after]
        specs += [VMEM] * 2 + [anywhere]
        shapes += [(64, ny), padded, padded]
    return pl.pallas_call(
        functools.partial(sweep_kernel, chunk),
        grid=(STEPS,),
        in_specs=specs,
        out_specs=[pl.BlockSpec((part // STEPS, layers, nz, ny), lambda i: (place * STEPS + i, 0, 0, 0))] + [VMEM] * (len(shapes) - 1),
        out_shape=[jax.ShapeDtypeStruct(shape, F32) for shape in shapes],
        input_output_aliases=alias,
        scratch_shapes=scratch,
        compiler_params=params(),
        name=f"sweeps{chunk}",
    )(*args)


def anomaly_kernel(members_all, prior_ref, a_ref, b_ref, *refs):
    out_ref = refs[-1]
    members, _, nz, ny = prior_ref.shape
    flat = prior_ref.reshape(members * nz, ny)
    mean = (a_ref[0] + b_ref[0]) / members_all
    for z in range(nz):
        rows = flat[pl.ds(z, members, stride=nz), :]
        out_ref[z] = (rows - mean[z : z + 1]).astype(BF16)


def anomalies(prior, totals, members_all, *after):
    members, layers, nz, ny = prior.shape
    total = pl.BlockSpec((1, nz, ny), lambda l: (l, 0, 0))
    return pl.pallas_call(
        functools.partial(anomaly_kernel, members_all),
        grid=(layers,),
        in_specs=[pl.BlockSpec((members, 1, nz, ny), lambda l: (0, l, 0, 0))] + [total] * 2 + [pl.BlockSpec(memory_space=pl.ANY)] * len(after),
        out_specs=pl.BlockSpec((nz, members, ny), lambda l: (l, 0, 0)),
        out_shape=jax.ShapeDtypeStruct((layers * nz, members, ny), BF16),
        compiler_params=params(),
        name="anomalies",
    )(prior, *totals, *after)


def slots_kernel(probes, slot_ref, value_ref, var_ref, noise_ref, after, seen_ref, weight_ref, stack):
    members, count = noise_ref.shape
    stack[...] = jnp.zeros_like(stack)
    stack[0:members] = noise_ref[...]
    stack[members : members + 1] = value_ref[...]
    stack[members + 1 : members + 2] = var_ref[...]
    slot = slot_ref[...]
    place = lax.rem(slot, probes) * (count // probes) + slot // probes
    row = lax.broadcasted_iota(jnp.int32, (count, count), 0)
    chosen = jnp.where(row == place, 1.0, 0.0)
    ordered = lax.dot_general(
        chosen, stack[...], (((1,), (1,)), ((), ())), precision=lax.Precision.HIGHEST, preferred_element_type=F32
    )
    value = ordered[:, members : members + 1]
    var = ordered[:, members + 1 : members + 2]
    seen_ref[...] = value + jnp.sqrt(var) * ordered
    weight_ref[...] = jnp.broadcast_to(1.0 / var, weight_ref.shape)


def in_slots(slot, value, var, noise, probes, after):
    count = slot.shape[0]
    shape = jax.ShapeDtypeStruct((count, 128), F32)
    return pl.pallas_call(
        functools.partial(slots_kernel, probes),
        in_specs=[VMEM] * 4 + [pl.BlockSpec(memory_space=pl.ANY)],
        out_specs=[VMEM] * 2,
        out_shape=[shape, shape],
        scratch_shapes=[pltpu.VMEM((128, count), F32)],
        cost_estimate=pl.CostEstimate(flops=0, bytes_accessed=1 << 26, transcendentals=0),
        compiler_params=params(),
        name="slots",
    )(slot[None], value[None], var[None], noise, after)


def dot(a, b, dims):
    return lax.dot_general(a, b, (dims, ((), ())), precision=lax.Precision.HIGHEST, preferred_element_type=F32)


def solve_kernel(members, here, me_ref, vals_ref, seen_ref, weight_ref, beside_any, prior_hbm, out_ref, beside_ref, prior_ref, scr, sems):
    fetches = [
        pltpu.make_async_copy(beside_any, beside_ref, sems.at[0]),
        pltpu.make_async_copy(prior_hbm, prior_ref, sems.at[1]),
    ]
    for fetch in fetches:
        fetch.start()
    devices, ny = vals_ref.shape
    groups = members // here
    tiles = devices // groups
    probes = 64 // here
    lane = lax.broadcasted_iota(jnp.int32, (tiles, ny), 1)
    parts = [vals_ref[pl.ds(g, tiles, stride=groups), :] for g in range(groups)]
    slabs = []
    for s in range(probes):
        slab = jnp.zeros((tiles, ny), F32)
        for g in range(groups):
            shift = (g - s) * here % ny
            moved = pltpu.roll(parts[g], shift, 1) if shift else parts[g]
            slab = jnp.where((lane >= g * here) & (lane < (g + 1) * here), moved, slab)
        slabs.append(slab)
    predicted = jnp.concatenate(slabs, axis=0)
    lanes = lax.broadcasted_iota(jnp.int32, predicted.shape, 1)
    mean = jnp.sum(predicted, axis=1, keepdims=True) / members
    spread = jnp.where(lanes < members, predicted - mean, 0.0)
    scaled = (spread * weight_ref[...]).T
    gram = dot(scaled, spread, ((1,), (0,)))
    rhs = dot(scaled, seen_ref[...] - predicted, ((1,), (0,)))
    half = 0.5 * jnp.max(jnp.sum(jnp.abs(gram), axis=1))
    alpha = 1.0 / (members - 1.0 + half)
    diagonal = lax.broadcasted_iota(jnp.int32, gram.shape, 0) == lax.broadcasted_iota(jnp.int32, gram.shape, 1)
    error = jnp.where(diagonal, alpha * half, 0.0) - alpha * gram

    def more(state):
        return (state[0] > 1e-9) & (state[1] < 40)

    def double(state):
        size, count, power_of, x = state
        both = dot(power_of, jnp.concatenate([power_of, x], axis=1), ((1,), (0,)))
        return size * size, count + 1, both[:, :ny], x + both[:, ny:]

    x = lax.while_loop(more, double, (half * alpha, 0, error, alpha * rhs))[3]
    me = me_ref[0]
    scr[...] = x
    order = [scr[pl.ds(pl.multiple_of((me ^ g) * here, here), here), :] for g in range(groups)]
    scr[...] = jnp.concatenate(order + [jnp.zeros((ny - members, ny), F32)], axis=0).T
    mine = scr[pl.ds(pl.multiple_of(me * here, here), here), :]
    out_ref[...] = mine[:, :members].astype(BF16)
    for fetch in fetches:
        fetch.wait()


def solve(vals, seen, weight, me, members, here, beside, prior):
    return pl.pallas_call(
        functools.partial(solve_kernel, members, here),
        in_specs=[SMEM] + [VMEM] * 3 + [pl.BlockSpec(memory_space=pl.ANY), pl.BlockSpec(memory_space=pltpu.HBM)],
        out_specs=[VMEM] * 3,
        out_shape=[
            jax.ShapeDtypeStruct((here, members), BF16),
            jax.ShapeDtypeStruct(beside.shape, BF16),
            jax.ShapeDtypeStruct(prior.shape, F32),
        ],
        scratch_shapes=[pltpu.VMEM((128, 128), F32), pltpu.SemaphoreType.DMA((2,))],
        compiler_params=params(),
        name="solve",
    )(me, vals, seen, weight, beside, pltpu.with_memory_space_constraint(prior, pltpu.HBM))


def update_kernel(weights_ref, prior_ref, mine_ref, beside_ref, over_ref, far_any, out_hbm, far_ref, out_ref, sems):
    here, layers, nz, ny = prior_ref.shape
    members = weights_ref.shape[1]
    fetch = pltpu.make_async_copy(far_any, far_ref, sems.at[layers])
    fetch.start()
    tall = (here * ROWS, here)
    spread = lax.broadcasted_iota(jnp.int32, tall, 0) // ROWS == lax.broadcasted_iota(jnp.int32, tall, 1)
    wide = (members, members * ROWS)
    column = lax.broadcasted_iota(jnp.int32, wide, 1)
    source = column // (here * ROWS) * here + column % here
    repeat = lax.broadcasted_iota(jnp.int32, wide, 0) == source
    lhs = jnp.dot(jnp.where(spread, 1.0, 0.0).astype(BF16), weights_ref[...], preferred_element_type=F32)
    lhs = jnp.dot(lhs.astype(BF16), jnp.where(repeat, 1.0, 0.0).astype(BF16), preferred_element_type=F32)
    row = lax.broadcasted_iota(jnp.int32, lhs.shape, 0)
    column = lax.broadcasted_iota(jnp.int32, lhs.shape, 1)
    lhs = jnp.where(row % ROWS == column // here % ROWS, lhs, 0.0).astype(BF16)
    places = [(l, z) for l in range(layers) for z in range(0, nz, ROWS)]
    stores = []

    def add(blocks, columns, base, done):
        for p in range(0, len(places), 2):
            pair = places[p : p + 2]
            sides = []
            for l, z in pair:
                first = l * nz + z
                sides.append(jnp.concatenate([b[first : first + ROWS].reshape(ROWS * here, ny) for b in blocks], axis=0))
            update = jnp.dot(columns, jnp.concatenate(sides, axis=1), preferred_element_type=F32)
            for i, (l, z) in enumerate(pair):
                part = update[:, i * ny : (i + 1) * ny]
                for m in range(here):
                    out_ref[m, l, z : z + ROWS] = base[m, l, z : z + ROWS] + part[m * ROWS : (m + 1) * ROWS]
                if done and z + ROWS == nz:
                    stores.append(pltpu.make_async_copy(out_ref.at[:, l], out_hbm.at[:, l], sems.at[l]))
                    stores[-1].start()

    split = 3 * here * ROWS
    add((mine_ref, beside_ref, over_ref), lhs[:, :split], prior_ref, False)
    fetch.wait()
    add((far_ref,), lhs[:, split:], out_ref, True)
    for store in stores:
        store.wait()


def updated(weights, prior, mine, beside, over, far):
    layers = prior.shape[1]
    return pl.pallas_call(
        update_kernel,
        in_specs=[VMEM] * 5 + [pl.BlockSpec(memory_space=pl.ANY)],
        out_specs=pl.BlockSpec(memory_space=pltpu.HBM),
        out_shape=jax.ShapeDtypeStruct(prior.shape, F32),
        scratch_shapes=[
            pltpu.VMEM(mine.shape, BF16),
            pltpu.VMEM(prior.shape, F32),
            pltpu.SemaphoreType.DMA((layers + 1,)),
        ],
        compiler_params=params(),
        name="update",
    )(weights, prior, mine, beside, over, far)


def per_device(prior, base_flow, base_visc, probe_cells, obs_slot, obs_values, obs_var, obs_noise):
    here = prior.shape[0]
    tiles, groups = lax.axis_size("tile"), lax.axis_size("mem")
    members = here * groups
    me = lax.axis_index("mem").astype(jnp.int32).reshape(1)

    odd = (lax.axis_index("tile") & 1).astype(jnp.int32).reshape(1)

    def swap(x, first):
        pairs = [((first + 2 * i) % tiles, (first + 2 * i + 1) % tiles) for i in range(tiles // 2)]
        return lax.ppermute(x, "tile", pairs + [(b, a) for a, b in pairs])

    def across(x, bits):
        return lax.ppermute(x, "mem", [(i, i ^ bits) for i in range(groups)])

    sent = encode(odd, prior, base_flow, base_visc)
    halos = [(swap(sent[2 * c], 0), swap(sent[2 * c + 1], 1)) for c in range(CHUNKS)]
    fields = (odd, prior, base_flow, base_visc, probe_cells)
    seen, weight = in_slots(obs_slot, obs_values, obs_var, obs_noise, probe_cells.shape[1], sent[0])
    first = sweeps(*fields, halos[0], 0, after=seen)
    payload, token = probes(odd, prior, base_visc, probe_cells, halos[1], first, tiles * groups)
    velocity, done = sweeps(*fields, halos[1], 1, first, token)
    total = total_of(prior, sent[0])
    chip = pair_sum(total, across(total, 1))
    totals = [chip, across(chip, 2)]
    mine = anomalies(prior, totals, float(members), first[1], *halos[1])
    beside = across(mine, 1)
    over = across(mine, 2)
    vals = lax.all_to_all(payload, ("tile", "mem"), 0, 0, tiled=True)
    over = held(over, vals, done)
    far = across(over, 1)
    weights, beside, near_prior = solve(vals, seen, weight, me, members, here, beside, prior)
    return velocity, updated(weights, near_prior, mine, beside, over, far)


def solution(mesh):
    placed = (
        P("mem", "tile", None, None),
        P("tile", None, None),
        P("tile", None, None),
        P("tile", None),
        P(),
        P(),
        P(),
        P(),
    )
    return jax.shard_map(
        per_device,
        mesh=mesh,
        in_specs=placed,
        out_specs=(P("mem", "tile", None, None), P("mem", "tile", None, None)),
        check_vma=False,
    )
```

```python
import functools
import math

import jax
import jax.numpy as jnp
from jax import lax
from jax.experimental import pallas as pl
from jax.experimental.pallas import tpu as pltpu
from jax.sharding import PartitionSpec as P

ITERS = 4
PARTS = ((8, 0), (8, 1))
CHUNKS = len(PARTS)
ROWS = 8
WINDOW = 8
WAYS = 2
STEPS = 1
LOG_MID = 0.5 * (math.log(0.02) + math.log(0.05))
LOG_HALF = 0.5 * (math.log(0.05) - math.log(0.02)) + 1.0
NU_SCALE = 124.0 / LOG_HALF
FLOW_SCALE = 31.0
LN2 = math.log(2.0)
VMEM = pl.BlockSpec(memory_space=pltpu.VMEM)
SMEM = pl.BlockSpec(memory_space=pltpu.SMEM)
F32 = jnp.float32
BF16 = jnp.bfloat16


def params(mib=24):
    return pltpu.CompilerParams(vmem_limit_bytes=mib * 1024 * 1024)


def power(x):
    return jnp.exp(x * LN2)


def log2_of(x):
    return jnp.log(x) * (1.0 / LN2)


def encode_kernel(odd_ref, prior_hbm, flow_hbm, visc_hbm, *refs):
    outs, (prior, flow, visc, base, sems) = refs[: 2 * CHUNKS], refs[2 * CHUNKS :]
    layers = prior.shape[1]
    copies = [
        pltpu.make_async_copy(visc_hbm, visc, sems.at[0]),
        pltpu.make_async_copy(flow_hbm, flow, sems.at[1]),
    ]
    for c, (part, place) in enumerate(PARTS):
        span = pl.ds(place * part, part)
        copies.append(pltpu.make_async_copy(prior_hbm.at[span], prior.at[span], sems.at[2 + c]))
    for copy in copies:
        copy.start()
    copies[0].wait()
    base[...] = jnp.log(visc[...]) * NU_SCALE - LOG_MID * NU_SCALE
    copies[1].wait()
    for l in range(layers):
        code = power(flow[l] * FLOW_SCALE).astype(BF16)
        outs[0][l] = code
        outs[1][l] = code
    for c, (part, place) in enumerate(PARTS):
        copies[2 + c].wait()
        inner_ref, outer_ref = outs[2 * c], outs[2 * c + 1]
        first = layers if c == 0 else 0

        def members(right_ref, left_ref):
            def member(m, carry):
                for l in range(layers):
                    code = power(prior[place * part + m, l] * NU_SCALE + base[l]).astype(BF16)
                    if l >= 1:
                        right_ref[first + m * 3 + l - 1] = code
                    if l < 3:
                        left_ref[first + m * 3 + l] = code
                return carry

            lax.fori_loop(0, part, member, 0)

        @pl.when(odd_ref[0] == 0)
        def _():
            members(inner_ref, outer_ref)

        @pl.when(odd_ref[0] == 1)
        def _():
            members(outer_ref, inner_ref)


def encode(odd, prior, flow, visc):
    members, layers, nz, ny = prior.shape
    shapes = []
    for c, (part, _) in enumerate(PARTS):
        slabs = 3 * part + (layers if c == 0 else 0)
        shapes += [jax.ShapeDtypeStruct((slabs, nz, ny), BF16)] * 2
    return pl.pallas_call(
        encode_kernel,
        in_specs=[SMEM] + [pl.BlockSpec(memory_space=pltpu.HBM)] * 3,
        out_specs=[VMEM] * len(shapes),
        out_shape=shapes,
        scratch_shapes=[
            pltpu.VMEM(prior.shape, F32),
            pltpu.VMEM(flow.shape, F32),
            pltpu.VMEM(visc.shape, F32),
            pltpu.VMEM(visc.shape, F32),
            pltpu.SemaphoreType.DMA((2 + CHUNKS,)),
        ],
        compiler_params=params(),
        name="encode",
    )(odd, *[pltpu.with_memory_space_constraint(x, pltpu.HBM) for x in (prior, flow, visc)])


def total_kernel(prior_ref, after, out_ref):
    out_ref[...] = prior_ref[0]
    for m in range(1, prior_ref.shape[0]):
        out_ref[...] += prior_ref[m]


def total_of(prior, after):
    return pl.pallas_call(
        total_kernel,
        in_specs=[VMEM, pl.BlockSpec(memory_space=pl.ANY)],
        out_specs=VMEM,
        out_shape=jax.ShapeDtypeStruct(prior.shape[1:], F32),
        compiler_params=params(),
        name="total",
    )(prior, after)


def pair_sum_kernel(a_ref, b_ref, out_ref):
    out_ref[...] = a_ref[...] + b_ref[...]


def pair_sum(a, b):
    return pl.pallas_call(
        pair_sum_kernel,
        in_specs=[VMEM] * 2,
        out_specs=VMEM,
        out_shape=jax.ShapeDtypeStruct(a.shape, F32),
        compiler_params=params(),
        name="pair_sum",
    )(a, b)


def hold_kernel(*refs):
    pass


def held(value, *after):
    return pl.pallas_call(
        hold_kernel,
        in_specs=[VMEM] * (1 + len(after)),
        out_specs=VMEM,
        out_shape=jax.ShapeDtypeStruct(value.shape, value.dtype),
        input_output_aliases={0: 0},
        compiler_params=params(),
        name="hold",
    )(value, *after)


def neighbours(buf, l, centre, nz, ny):
    lane = lax.broadcasted_iota(jnp.int32, centre.shape, 1)
    below = jnp.where(lane == 0, 0.0, pltpu.roll(centre, 1, 1))
    above = jnp.where(lane == ny - 1, 0.0, pltpu.roll(centre, ny - 1, 1))
    return (buf[l, 7 : 7 + nz] + buf[l, 9 : 9 + nz]) + (below + above)


def put(buf, l, value, nz):
    buf[l, 8 : 8 + nz] = value
    buf[l, 7:8] = value[nz - 1 : nz]
    buf[l, 8 + nz : 9 + nz] = value[0:1]


def wrap(buf, l, value, nz):
    buf[l, 8 : 8 + nz] = value
    buf[l, 5:8] = value[nz - 3 : nz]
    buf[l, 8 + nz : 12 + nz] = value[0:4]


def viscosity_from(code):
    return jnp.exp(jnp.log(code.astype(F32)) * (1.0 / (LN2 * NU_SCALE)) + LOG_MID)


def probe_kernel(devices, odd_ref, cells_ref, prior_ref, visc_ref, inner_ref, outer_ref, lap0, adv0, rows_in, lines_ref, token_ref, nus, held_rows, rows):
    _, layers, nz, ny = prior_ref.shape
    part, place = PARTS[-1]
    odd = odd_ref[0]
    rows[...] = rows_in[...]
    lane = lax.broadcasted_iota(jnp.int32, (WINDOW, ny), 1)

    def step(slot, back, centre, front, visc):
        held_rows[slot, 4 : 4 + WINDOW] = centre
        sides = held_rows[slot, 3 : 3 + WINDOW] + held_rows[slot, 5 : 5 + WINDOW]
        below = jnp.where(lane == 0, 0.0, pltpu.roll(centre, 1, 1))
        above = jnp.where(lane == ny - 1, 0.0, pltpu.roll(centre, ny - 1, 1))
        lap = back + front + (sides + (below + above)) - 6.0 * centre
        return centre + visc * lap - 0.15 * (centre - back) + 0.01

    def member(m, carry, way):
        nu = nus.at[way]
        for l in range(3):
            for side_ref, ahead in ((inner_ref, 1 - odd), (outer_ref, odd)):
                wrap(nu, ahead * (3 + layers) + l, viscosity_from(side_ref[m * 3 + l]), nz)
        for l in range(layers):
            wrap(nu, 3 + l, visc_ref[l] * jnp.exp(prior_ref[place * part + m, l]), nz)
        for s in range(4):
            cell = cells_ref[0, s]
            layer, z = cell // (nz * ny), lax.rem(cell, nz * ny) // ny
            window = pl.ds(z + 5, WINDOW)
            reach = [layer + j for j in range(2 * ITERS - 1)]
            visc = [nu[l, window] for l in reach]
            speed = [adv0[l, window] + v * lap0[l, window] for l, v in zip(reach, visc)]
            slot = (way * 4 + s) * 9
            for _ in range(1, ITERS):
                visc = visc[1:-1]
                speed = [step(slot + k, *speed[k : k + 3], v) for k, v in enumerate(visc)]
                slot += len(visc)
            rows[pl.ds(s * 16 + place * part + m, 1), :] = speed[0][3:4]
        return carry

    def one_group(i, carry):
        for way in range(WAYS):
            member(i * WAYS + way, carry, way)
        return carry

    lax.fori_loop(0, part // WAYS, one_group, 0)
    lane = lax.broadcasted_iota(jnp.int32, rows.shape, 1)
    row = lax.broadcasted_iota(jnp.int32, rows.shape, 0)
    y = jnp.zeros(rows.shape, jnp.int32)
    for s in range(4):
        y = jnp.where(row // 16 == s, lax.rem(cells_ref[0, s], ny), y)
    picked = jnp.sum(jnp.where(lane == y, rows[...], 0.0), axis=1, keepdims=True)
    line = jnp.sum(jnp.where(lane == row, picked, 0.0), axis=0, keepdims=True)
    lines_ref[...] = jnp.broadcast_to(line, (devices, ny))
    token_ref[...] = rows[0:8]


def probes(odd, prior, visc, cells, halo, first, devices):
    _, layers, nz, ny = prior.shape
    _, rows, lap0, adv0 = first
    return pl.pallas_call(
        functools.partial(probe_kernel, devices),
        in_specs=[SMEM] * 2 + [VMEM] * 7,
        out_specs=[VMEM] * 2,
        out_shape=[jax.ShapeDtypeStruct((devices, ny), F32), jax.ShapeDtypeStruct((8, ny), F32)],
        scratch_shapes=[
            pltpu.VMEM((WAYS,) + lap0.shape, F32),
            pltpu.VMEM((36 * WAYS, WINDOW + 8, ny), F32),
            pltpu.VMEM(rows.shape, F32),
        ],
        compiler_params=params(),
        name="probes",
    )(odd, cells, prior, visc, *halo, lap0, adv0, rows)


def sweep_kernel(chunk, odd_ref, cells_ref, prior_ref, flow_ref, visc_ref, inner_ref, outer_ref, *rest):
    _, layers, nz, ny = prior_ref.shape
    part, place = PARTS[chunk]
    group = part // STEPS
    step = pl.program_id(0)
    wide = layers + 2 * ITERS
    odd = odd_ref[0]
    partners = ((inner_ref, 1 - odd), (outer_ref, odd))
    if chunk == 0:
        _, out_ref, rows, lap0, adv0, buf0, buf1, nu = rest
        prior, offset = prior_ref, place * part

        @pl.when(step == 0)
        def _():
            for l in range(ITERS):
                for side_ref, ahead in partners:
                    flow = log2_of(side_ref[l].astype(F32)) * (1.0 / FLOW_SCALE)
                    put(buf0, ahead * (ITERS + layers) + l, flow, nz)
            for l in range(layers):
                put(buf0, ITERS + l, flow_ref[l], nz)
            for l in range(1, wide - 1):
                centre, back = buf0[l, 8 : 8 + nz], buf0[l - 1, 8 : 8 + nz]
                sides = back + buf0[l + 1, 8 : 8 + nz] + neighbours(buf0, l, centre, nz, ny)
                wrap(lap0, l - 1, sides - 6.0 * centre, nz)
                wrap(adv0, l - 1, centre - 0.15 * (centre - back) + 0.01, nz)
            rows[...] = jnp.zeros_like(rows)

    else:
        sources, (_, _, out_ref, token_ref, buf0, buf1, nu), (lap0, adv0, *sides, prior, sems) = rest[:2], rest[2:9], rest[9:]
        copies = [
            pltpu.make_async_copy(source, target, sems.at[i])
            for i, (source, target) in enumerate(
                zip(
                    (prior_ref.at[pl.ds(place * part, part)], inner_ref, outer_ref) + tuple(sources),
                    (prior, *sides, lap0, adv0),
                )
            )
        ]
        for copy in copies:
            copy.start()
        for copy in copies:
            copy.wait()
        partners = ((sides[0], 1 - odd), (sides[1], odd))
        offset = 0
        token_ref[...] = jnp.zeros_like(token_ref)

    base_slabs = layers if chunk == 0 else 0

    def member(m, carry):
        index = step * group + m
        first = base_slabs + index * 3
        for l in range(3):
            for side_ref, ahead in partners:
                code = side_ref[first + l]
                nu[ahead * (3 + layers) + l] = viscosity_from(code)
        for l in range(layers):
            nu[3 + l] = visc_ref[l] * jnp.exp(prior[offset + index, l])
        for l in range(1, wide - 1):
            put(buf1, l, adv0[l - 1, 8 : 8 + nz] + nu[l - 1] * lap0[l - 1, 8 : 8 + nz], nz)
        src, dst = buf1, buf0
        for sweep in range(1, ITERS):
            low, high = sweep + 1, wide - sweep - 1
            back, centre = src[low - 1, 8 : 8 + nz], src[low, 8 : 8 + nz]
            for l in range(low, high):
                front = src[l + 1, 8 : 8 + nz]
                lap = back + front + neighbours(src, l, centre, nz, ny) - 6.0 * centre
                value = centre + nu[l - 1] * lap - 0.15 * (centre - back) + 0.01
                if sweep == ITERS - 1:
                    out_ref[m, l - ITERS] = value
                else:
                    put(dst, l, value, nz)
                back, centre = centre, front
            src, dst = dst, src
        if chunk == 0:
            for s in range(4):
                cell = cells_ref[0, s]
                layer, z = cell // (nz * ny), lax.rem(cell, nz * ny) // ny
                rows[pl.ds(s * 16 + place * part + index, 1), :] = out_ref[m, layer, pl.ds(z, 1), :]
        return carry

    lax.fori_loop(0, group, member, 0)


def sweeps(odd, prior, flow, visc, cells, halo, chunk, before=None, after=None):
    _, layers, nz, ny = prior.shape
    part, place = PARTS[chunk]
    wide = layers + 2 * ITERS
    padded = (wide - 2, nz + 16, ny)
    anywhere = pl.BlockSpec(memory_space=pl.ANY)
    hbm = pl.BlockSpec(memory_space=pltpu.HBM)
    args = [odd, cells, prior, flow, visc]
    specs = [SMEM] * 2 + [VMEM] * 3
    scratch = [
        pltpu.VMEM((wide, nz + 16, ny), F32),
        pltpu.VMEM((wide, nz + 16, ny), F32),
        pltpu.VMEM((wide - 2, nz, ny), F32),
    ]
    alias = {}
    shapes = [prior.shape]
    if chunk:
        velocity, _, lap0, adv0 = before
        args += [pltpu.with_memory_space_constraint(x, pltpu.HBM) for x in (*halo, lap0, adv0)] + [after, velocity]
        specs += [hbm] * 4 + [anywhere, hbm]
        args[2:4] = [pltpu.with_memory_space_constraint(x, pltpu.HBM) for x in (prior, flow)]
        specs[2:4] = [hbm, hbm]
        alias = {len(args) - 1: 0}
        scratch += [pltpu.VMEM(padded, F32)] * 2 + [pltpu.VMEM(halo[0].shape, BF16)] * 2
        scratch += [pltpu.VMEM((part, layers, nz, ny), F32), pltpu.SemaphoreType.DMA((5,))]
        shapes += [(8, ny)]
    else:
        args += [*halo, after]
        specs += [VMEM] * 2 + [anywhere]
        shapes += [(64, ny), padded, padded]
    return pl.pallas_call(
        functools.partial(sweep_kernel, chunk),
        grid=(STEPS,),
        in_specs=specs,
        out_specs=[pl.BlockSpec((part // STEPS, layers, nz, ny), lambda i: (place * STEPS + i, 0, 0, 0))] + [VMEM] * (len(shapes) - 1),
        out_shape=[jax.ShapeDtypeStruct(shape, F32) for shape in shapes],
        input_output_aliases=alias,
        scratch_shapes=scratch,
        compiler_params=params(),
        name=f"sweeps{chunk}",
    )(*args)


def anomaly_kernel(members_all, prior_ref, a_ref, b_ref, *refs):
    out_ref = refs[-1]
    members, _, nz, ny = prior_ref.shape
    flat = prior_ref.reshape(members * nz, ny)
    mean = (a_ref[0] + b_ref[0]) / members_all
    for z in range(nz):
        rows = flat[pl.ds(z, members, stride=nz), :]
        out_ref[z] = (rows - mean[z : z + 1]).astype(BF16)


def anomalies(prior, totals, members_all, *after):
    members, layers, nz, ny = prior.shape
    total = pl.BlockSpec((1, nz, ny), lambda l: (l, 0, 0))
    return pl.pallas_call(
        functools.partial(anomaly_kernel, members_all),
        grid=(layers,),
        in_specs=[pl.BlockSpec((members, 1, nz, ny), lambda l: (0, l, 0, 0))] + [total] * 2 + [pl.BlockSpec(memory_space=pl.ANY)] * len(after),
        out_specs=pl.BlockSpec((nz, members, ny), lambda l: (l, 0, 0)),
        out_shape=jax.ShapeDtypeStruct((layers * nz, members, ny), BF16),
        compiler_params=params(),
        name="anomalies",
    )(prior, *totals, *after)


def slots_kernel(probes, slot_ref, value_ref, var_ref, noise_ref, after, seen_ref, weight_ref, stack):
    members, count = noise_ref.shape
    stack[...] = jnp.zeros_like(stack)
    stack[0:members] = noise_ref[...]
    stack[members : members + 1] = value_ref[...]
    stack[members + 1 : members + 2] = var_ref[...]
    slot = slot_ref[...]
    place = lax.rem(slot, probes) * (count // probes) + slot // probes
    row = lax.broadcasted_iota(jnp.int32, (count, count), 0)
    chosen = jnp.where(row == place, 1.0, 0.0)
    ordered = lax.dot_general(
        chosen, stack[...], (((1,), (1,)), ((), ())), precision=lax.Precision.HIGHEST, preferred_element_type=F32
    )
    value = ordered[:, members : members + 1]
    var = ordered[:, members + 1 : members + 2]
    seen_ref[...] = value + jnp.sqrt(var) * ordered
    weight_ref[...] = jnp.broadcast_to(1.0 / var, weight_ref.shape)


def in_slots(slot, value, var, noise, probes, after):
    count = slot.shape[0]
    shape = jax.ShapeDtypeStruct((count, 128), F32)
    return pl.pallas_call(
        functools.partial(slots_kernel, probes),
        in_specs=[VMEM] * 4 + [pl.BlockSpec(memory_space=pl.ANY)],
        out_specs=[VMEM] * 2,
        out_shape=[shape, shape],
        scratch_shapes=[pltpu.VMEM((128, count), F32)],
        cost_estimate=pl.CostEstimate(flops=0, bytes_accessed=1 << 26, transcendentals=0),
        compiler_params=params(),
        name="slots",
    )(slot[None], value[None], var[None], noise, after)


def dot(a, b, dims):
    return lax.dot_general(a, b, (dims, ((), ())), precision=lax.Precision.HIGHEST, preferred_element_type=F32)


def solve_kernel(members, here, me_ref, vals_ref, seen_ref, weight_ref, beside_any, prior_hbm, out_ref, beside_ref, prior_ref, scr, sems):
    fetches = [
        pltpu.make_async_copy(beside_any, beside_ref, sems.at[0]),
        pltpu.make_async_copy(prior_hbm, prior_ref, sems.at[1]),
    ]
    for fetch in fetches:
        fetch.start()
    devices, ny = vals_ref.shape
    groups = members // here
    tiles = devices // groups
    probes = 64 // here
    lane = lax.broadcasted_iota(jnp.int32, (tiles, ny), 1)
    parts = [vals_ref[pl.ds(g, tiles, stride=groups), :] for g in range(groups)]
    slabs = []
    for s in range(probes):
        slab = jnp.zeros((tiles, ny), F32)
        for g in range(groups):
            shift = (g - s) * here % ny
            moved = pltpu.roll(parts[g], shift, 1) if shift else parts[g]
            slab = jnp.where((lane >= g * here) & (lane < (g + 1) * here), moved, slab)
        slabs.append(slab)
    predicted = jnp.concatenate(slabs, axis=0)
    lanes = lax.broadcasted_iota(jnp.int32, predicted.shape, 1)
    mean = jnp.sum(predicted, axis=1, keepdims=True) / members
    spread = jnp.where(lanes < members, predicted - mean, 0.0)
    scaled = (spread * weight_ref[...]).T
    gram = dot(scaled, spread, ((1,), (0,)))
    rhs = dot(scaled, seen_ref[...] - predicted, ((1,), (0,)))
    half = 0.5 * jnp.max(jnp.sum(jnp.abs(gram), axis=1))
    alpha = 1.0 / (members - 1.0 + half)
    diagonal = lax.broadcasted_iota(jnp.int32, gram.shape, 0) == lax.broadcasted_iota(jnp.int32, gram.shape, 1)
    error = jnp.where(diagonal, alpha * half, 0.0) - alpha * gram

    def more(state):
        return (state[0] > 2e-6) & (state[1] < 40)

    def double(state):
        size, count, power_of, x = state
        both = dot(power_of, jnp.concatenate([power_of, x], axis=1), ((1,), (0,)))
        return size * size, count + 1, both[:, :ny], x + both[:, ny:]

    x = lax.while_loop(more, double, (half * alpha, 0, error, alpha * rhs))[3]
    me = me_ref[0]
    scr[...] = x
    order = [scr[pl.ds(pl.multiple_of((me ^ g) * here, here), here), :] for g in range(groups)]
    scr[...] = jnp.concatenate(order + [jnp.zeros((ny - members, ny), F32)], axis=0).T
    mine = scr[pl.ds(pl.multiple_of(me * here, here), here), :]
    out_ref[...] = mine[:, :members].astype(BF16)
    for fetch in fetches:
        fetch.wait()


def solve(vals, seen, weight, me, members, here, beside, prior):
    return pl.pallas_call(
        functools.partial(solve_kernel, members, here),
        in_specs=[SMEM] + [VMEM] * 3 + [pl.BlockSpec(memory_space=pl.ANY), pl.BlockSpec(memory_space=pltpu.HBM)],
        out_specs=[VMEM] * 3,
        out_shape=[
            jax.ShapeDtypeStruct((here, members), BF16),
            jax.ShapeDtypeStruct(beside.shape, BF16),
            jax.ShapeDtypeStruct(prior.shape, F32),
        ],
        scratch_shapes=[pltpu.VMEM((128, 128), F32), pltpu.SemaphoreType.DMA((2,))],
        compiler_params=params(),
        name="solve",
    )(me, vals, seen, weight, beside, pltpu.with_memory_space_constraint(prior, pltpu.HBM))


def update_kernel(weights_ref, prior_ref, *refs):
    blocks, (out_hbm, out_ref, sems) = refs[:4], refs[4:]
    here, layers, nz, ny = prior_ref.shape
    members = weights_ref.shape[1]
    tall = (here * ROWS, here)
    spread = lax.broadcasted_iota(jnp.int32, tall, 0) // ROWS == lax.broadcasted_iota(jnp.int32, tall, 1)
    wide = (members, members * ROWS)
    column = lax.broadcasted_iota(jnp.int32, wide, 1)
    source = column // (here * ROWS) * here + column % here
    repeat = lax.broadcasted_iota(jnp.int32, wide, 0) == source
    lhs = jnp.dot(jnp.where(spread, 1.0, 0.0).astype(BF16), weights_ref[...], preferred_element_type=F32)
    lhs = jnp.dot(lhs.astype(BF16), jnp.where(repeat, 1.0, 0.0).astype(BF16), preferred_element_type=F32)
    row = lax.broadcasted_iota(jnp.int32, lhs.shape, 0)
    column = lax.broadcasted_iota(jnp.int32, lhs.shape, 1)
    lhs = jnp.where(row % ROWS == column // here % ROWS, lhs, 0.0).astype(BF16)
    places = [(l, z) for l in range(layers) for z in range(0, nz, ROWS)]
    stores = []
    for p in range(0, len(places), 2):
        pair = places[p : p + 2]
        sides = []
        for l, z in pair:
            first = l * nz + z
            sides.append(jnp.concatenate([b[first : first + ROWS].reshape(ROWS * here, ny) for b in blocks], axis=0))
        update = jnp.dot(lhs, jnp.concatenate(sides, axis=1), preferred_element_type=F32)
        for i, (l, z) in enumerate(pair):
            part = update[:, i * ny : (i + 1) * ny]
            for m in range(here):
                out_ref[m, l, z : z + ROWS] = prior_ref[m, l, z : z + ROWS] + part[m * ROWS : (m + 1) * ROWS]
            if z + ROWS == nz:
                stores.append(pltpu.make_async_copy(out_ref.at[:, l], out_hbm.at[:, l], sems.at[l]))
                stores[-1].start()
    for store in stores:
        store.wait()


def updated(weights, prior, mine, beside, over, far):
    layers = prior.shape[1]
    return pl.pallas_call(
        update_kernel,
        in_specs=[VMEM] * 6,
        out_specs=pl.BlockSpec(memory_space=pltpu.HBM),
        out_shape=jax.ShapeDtypeStruct(prior.shape, F32),
        scratch_shapes=[pltpu.VMEM(prior.shape, F32), pltpu.SemaphoreType.DMA((layers,))],
        compiler_params=params(),
        name="update",
    )(weights, prior, mine, beside, over, far)


def per_device(prior, base_flow, base_visc, probe_cells, obs_slot, obs_values, obs_var, obs_noise):
    here = prior.shape[0]
    tiles, groups = lax.axis_size("tile"), lax.axis_size("mem")
    members = here * groups
    me = lax.axis_index("mem").astype(jnp.int32).reshape(1)

    odd = (lax.axis_index("tile") & 1).astype(jnp.int32).reshape(1)

    def swap(x, first):
        pairs = [((first + 2 * i) % tiles, (first + 2 * i + 1) % tiles) for i in range(tiles // 2)]
        return lax.ppermute(x, "tile", pairs + [(b, a) for a, b in pairs])

    def across(x, bits):
        return lax.ppermute(x, "mem", [(i, i ^ bits) for i in range(groups)])

    sent = encode(odd, prior, base_flow, base_visc)
    halos = [(swap(sent[2 * c], 0), swap(sent[2 * c + 1], 1)) for c in range(CHUNKS)]
    fields = (odd, prior, base_flow, base_visc, probe_cells)
    seen, weight = in_slots(obs_slot, obs_values, obs_var, obs_noise, probe_cells.shape[1], sent[0])
    first = sweeps(*fields, halos[0], 0, after=seen)
    payload, token = probes(odd, prior, base_visc, probe_cells, halos[1], first, tiles * groups)
    velocity, done = sweeps(*fields, halos[1], 1, first, token)
    total = total_of(prior, sent[0])
    chip = pair_sum(total, across(total, 1))
    totals = [chip, across(chip, 2)]
    mine = anomalies(prior, totals, float(members), first[1], *halos[1])
    beside = across(mine, 1)
    over = across(mine, 2)
    vals = lax.all_to_all(payload, ("tile", "mem"), 0, 0, tiled=True)
    over = held(over, vals, done)
    far = across(over, 1)
    weights, beside, near_prior = solve(vals, seen, weight, me, members, here, beside, prior)
    return velocity, updated(weights, near_prior, mine, beside, over, far)


def solution(mesh):
    placed = (
        P("mem", "tile", None, None),
        P("tile", None, None),
        P("tile", None, None),
        P("tile", None),
        P(),
        P(),
        P(),
        P(),
    )
    return jax.shard_map(
        per_device,
        mesh=mesh,
        in_specs=placed,
        out_specs=(P("mem", "tile", None, None), P("mem", "tile", None, None)),
        check_vma=False,
    )
```

```python
import functools
import math

import jax
import jax.numpy as jnp
from jax import lax
from jax.experimental import pallas as pl
from jax.experimental.pallas import tpu as pltpu
from jax.sharding import PartitionSpec as P

ITERS = 4
PARTS = ((8, 0), (8, 1))
CHUNKS = len(PARTS)
ROWS = 8
WINDOW = 8
WAYS = 2
STEPS = 1
LOG_MID = 0.5 * (math.log(0.02) + math.log(0.05))
LOG_HALF = 0.5 * (math.log(0.05) - math.log(0.02)) + 1.0
NU_SCALE = 124.0 / LOG_HALF
FLOW_SCALE = 31.0
LN2 = math.log(2.0)
VMEM = pl.BlockSpec(memory_space=pltpu.VMEM)
SMEM = pl.BlockSpec(memory_space=pltpu.SMEM)
F32 = jnp.float32
BF16 = jnp.bfloat16


def params(mib=24):
    return pltpu.CompilerParams(vmem_limit_bytes=mib * 1024 * 1024)


def power(x):
    return jnp.exp(x * LN2)


def log2_of(x):
    return jnp.log(x) * (1.0 / LN2)


def encode_kernel(odd_ref, prior_hbm, flow_hbm, visc_hbm, *refs):
    outs, (prior, flow, visc, base, sems) = refs[: 2 * CHUNKS], refs[2 * CHUNKS :]
    layers = prior.shape[1]
    copies = [
        pltpu.make_async_copy(visc_hbm, visc, sems.at[0]),
        pltpu.make_async_copy(flow_hbm, flow, sems.at[1]),
    ]
    for c, (part, place) in enumerate(PARTS):
        span = pl.ds(place * part, part)
        copies.append(pltpu.make_async_copy(prior_hbm.at[span], prior.at[span], sems.at[2 + c]))
    for copy in copies:
        copy.start()
    copies[0].wait()
    base[...] = jnp.log(visc[...]) * NU_SCALE - LOG_MID * NU_SCALE
    copies[1].wait()
    for l in range(layers):
        code = power(flow[l] * FLOW_SCALE).astype(BF16)
        outs[0][l] = code
        outs[1][l] = code
    for c, (part, place) in enumerate(PARTS):
        copies[2 + c].wait()
        inner_ref, outer_ref = outs[2 * c], outs[2 * c + 1]
        first = layers if c == 0 else 0

        def members(right_ref, left_ref):
            def member(m, carry):
                for l in range(layers):
                    code = power(prior[place * part + m, l] * NU_SCALE + base[l]).astype(BF16)
                    if l >= 1:
                        right_ref[first + m * 3 + l - 1] = code
                    if l < 3:
                        left_ref[first + m * 3 + l] = code
                return carry

            lax.fori_loop(0, part, member, 0)

        @pl.when(odd_ref[0] == 0)
        def _():
            members(inner_ref, outer_ref)

        @pl.when(odd_ref[0] == 1)
        def _():
            members(outer_ref, inner_ref)


def encode(odd, prior, flow, visc):
    members, layers, nz, ny = prior.shape
    shapes = []
    for c, (part, _) in enumerate(PARTS):
        slabs = 3 * part + (layers if c == 0 else 0)
        shapes += [jax.ShapeDtypeStruct((slabs, nz, ny), BF16)] * 2
    return pl.pallas_call(
        encode_kernel,
        in_specs=[SMEM] + [pl.BlockSpec(memory_space=pltpu.HBM)] * 3,
        out_specs=[VMEM] * len(shapes),
        out_shape=shapes,
        scratch_shapes=[
            pltpu.VMEM(prior.shape, F32),
            pltpu.VMEM(flow.shape, F32),
            pltpu.VMEM(visc.shape, F32),
            pltpu.VMEM(visc.shape, F32),
            pltpu.SemaphoreType.DMA((2 + CHUNKS,)),
        ],
        compiler_params=params(),
        name="encode",
    )(odd, *[pltpu.with_memory_space_constraint(x, pltpu.HBM) for x in (prior, flow, visc)])


def total_kernel(prior_ref, after, out_ref):
    out_ref[...] = prior_ref[0]
    for m in range(1, prior_ref.shape[0]):
        out_ref[...] += prior_ref[m]


def total_of(prior, after):
    return pl.pallas_call(
        total_kernel,
        in_specs=[VMEM, pl.BlockSpec(memory_space=pl.ANY)],
        out_specs=VMEM,
        out_shape=jax.ShapeDtypeStruct(prior.shape[1:], F32),
        compiler_params=params(),
        name="total",
    )(prior, after)


def pair_sum_kernel(a_ref, b_ref, out_ref):
    out_ref[...] = a_ref[...] + b_ref[...]


def pair_sum(a, b):
    return pl.pallas_call(
        pair_sum_kernel,
        in_specs=[VMEM] * 2,
        out_specs=VMEM,
        out_shape=jax.ShapeDtypeStruct(a.shape, F32),
        compiler_params=params(),
        name="pair_sum",
    )(a, b)


def hold_kernel(*refs):
    pass


def held(value, *after):
    return pl.pallas_call(
        hold_kernel,
        in_specs=[VMEM] * (1 + len(after)),
        out_specs=VMEM,
        out_shape=jax.ShapeDtypeStruct(value.shape, value.dtype),
        input_output_aliases={0: 0},
        compiler_params=params(),
        name="hold",
    )(value, *after)


def neighbours(buf, l, centre, nz, ny):
    lane = lax.broadcasted_iota(jnp.int32, centre.shape, 1)
    below = jnp.where(lane == 0, 0.0, pltpu.roll(centre, 1, 1))
    above = jnp.where(lane == ny - 1, 0.0, pltpu.roll(centre, ny - 1, 1))
    return (buf[l, 7 : 7 + nz] + buf[l, 9 : 9 + nz]) + (below + above)


def put(buf, l, value, nz):
    buf[l, 8 : 8 + nz] = value
    buf[l, 7:8] = value[nz - 1 : nz]
    buf[l, 8 + nz : 9 + nz] = value[0:1]


def wrap(buf, l, value, nz):
    buf[l, 8 : 8 + nz] = value
    buf[l, 5:8] = value[nz - 3 : nz]
    buf[l, 8 + nz : 12 + nz] = value[0:4]


def viscosity_from(code):
    return jnp.exp(jnp.log(code.astype(F32)) * (1.0 / (LN2 * NU_SCALE)) + LOG_MID)


def probe_kernel(devices, odd_ref, cells_ref, prior_ref, visc_ref, inner_ref, outer_ref, lap0, adv0, rows_in, lines_ref, token_ref, nus, held_rows, rows):
    _, layers, nz, ny = prior_ref.shape
    part, place = PARTS[-1]
    odd = odd_ref[0]
    rows[...] = rows_in[...]
    lane = lax.broadcasted_iota(jnp.int32, (WINDOW, ny), 1)

    def step(slot, back, centre, front, visc):
        held_rows[slot, 4 : 4 + WINDOW] = centre
        sides = held_rows[slot, 3 : 3 + WINDOW] + held_rows[slot, 5 : 5 + WINDOW]
        below = jnp.where(lane == 0, 0.0, pltpu.roll(centre, 1, 1))
        above = jnp.where(lane == ny - 1, 0.0, pltpu.roll(centre, ny - 1, 1))
        lap = back + front + (sides + (below + above)) - 6.0 * centre
        return centre + visc * lap - 0.15 * (centre - back) + 0.01

    def member(m, carry, way):
        nu = nus.at[way]
        for l in range(3):
            for side_ref, ahead in ((inner_ref, 1 - odd), (outer_ref, odd)):
                wrap(nu, ahead * (3 + layers) + l, viscosity_from(side_ref[m * 3 + l]), nz)
        for l in range(layers):
            wrap(nu, 3 + l, visc_ref[l] * jnp.exp(prior_ref[place * part + m, l]), nz)
        for s in range(4):
            cell = cells_ref[0, s]
            layer, z = cell // (nz * ny), lax.rem(cell, nz * ny) // ny
            window = pl.ds(z + 5, WINDOW)
            reach = [layer + j for j in range(2 * ITERS - 1)]
            visc = [nu[l, window] for l in reach]
            speed = [adv0[l, window] + v * lap0[l, window] for l, v in zip(reach, visc)]
            slot = (way * 4 + s) * 9
            for _ in range(1, ITERS):
                visc = visc[1:-1]
                speed = [step(slot + k, *speed[k : k + 3], v) for k, v in enumerate(visc)]
                slot += len(visc)
            rows[pl.ds(s * 16 + place * part + m, 1), :] = speed[0][3:4]
        return carry

    def one_group(i, carry):
        for way in range(WAYS):
            member(i * WAYS + way, carry, way)
        return carry

    lax.fori_loop(0, part // WAYS, one_group, 0)
    lane = lax.broadcasted_iota(jnp.int32, rows.shape, 1)
    row = lax.broadcasted_iota(jnp.int32, rows.shape, 0)
    y = jnp.zeros(rows.shape, jnp.int32)
    for s in range(4):
        y = jnp.where(row // 16 == s, lax.rem(cells_ref[0, s], ny), y)
    picked = jnp.sum(jnp.where(lane == y, rows[...], 0.0), axis=1, keepdims=True)
    line = jnp.sum(jnp.where(lane == row, picked, 0.0), axis=0, keepdims=True)
    lines_ref[...] = jnp.broadcast_to(line, (devices, ny))
    token_ref[...] = rows[0:8]


def probes(odd, prior, visc, cells, halo, first, devices):
    _, layers, nz, ny = prior.shape
    _, rows, lap0, adv0 = first
    return pl.pallas_call(
        functools.partial(probe_kernel, devices),
        in_specs=[SMEM] * 2 + [VMEM] * 7,
        out_specs=[VMEM] * 2,
        out_shape=[jax.ShapeDtypeStruct((devices, ny), F32), jax.ShapeDtypeStruct((8, ny), F32)],
        scratch_shapes=[
            pltpu.VMEM((WAYS,) + lap0.shape, F32),
            pltpu.VMEM((36 * WAYS, WINDOW + 8, ny), F32),
            pltpu.VMEM(rows.shape, F32),
        ],
        compiler_params=params(),
        name="probes",
    )(odd, cells, prior, visc, *halo, lap0, adv0, rows)


def sweep_kernel(chunk, odd_ref, cells_ref, prior_ref, flow_ref, visc_ref, inner_ref, outer_ref, *rest):
    _, layers, nz, ny = prior_ref.shape
    part, place = PARTS[chunk]
    group = part // STEPS
    step = pl.program_id(0)
    wide = layers + 2 * ITERS
    odd = odd_ref[0]
    partners = ((inner_ref, 1 - odd), (outer_ref, odd))
    if chunk == 0:
        _, out_ref, rows, lap0, adv0, buf0, buf1, nu = rest
        prior, offset = prior_ref, place * part

        @pl.when(step == 0)
        def _():
            for l in range(ITERS):
                for side_ref, ahead in partners:
                    flow = log2_of(side_ref[l].astype(F32)) * (1.0 / FLOW_SCALE)
                    put(buf0, ahead * (ITERS + layers) + l, flow, nz)
            for l in range(layers):
                put(buf0, ITERS + l, flow_ref[l], nz)
            for l in range(1, wide - 1):
                centre, back = buf0[l, 8 : 8 + nz], buf0[l - 1, 8 : 8 + nz]
                sides = back + buf0[l + 1, 8 : 8 + nz] + neighbours(buf0, l, centre, nz, ny)
                wrap(lap0, l - 1, sides - 6.0 * centre, nz)
                wrap(adv0, l - 1, centre - 0.15 * (centre - back) + 0.01, nz)
            rows[...] = jnp.zeros_like(rows)

    else:
        sources, (_, _, out_ref, token_ref, buf0, buf1, nu), (lap0, adv0, *sides, prior, sems) = rest[:2], rest[2:9], rest[9:]
        copies = [
            pltpu.make_async_copy(source, target, sems.at[i])
            for i, (source, target) in enumerate(
                zip(
                    (prior_ref.at[pl.ds(place * part, part)], inner_ref, outer_ref) + tuple(sources),
                    (prior, *sides, lap0, adv0),
                )
            )
        ]
        for copy in copies:
            copy.start()
        for copy in copies:
            copy.wait()
        partners = ((sides[0], 1 - odd), (sides[1], odd))
        offset = 0
        token_ref[...] = jnp.zeros_like(token_ref)

    base_slabs = layers if chunk == 0 else 0

    def member(m, carry):
        index = step * group + m
        first = base_slabs + index * 3
        for l in range(3):
            for side_ref, ahead in partners:
                code = side_ref[first + l]
                nu[ahead * (3 + layers) + l] = viscosity_from(code)
        for l in range(layers):
            nu[3 + l] = visc_ref[l] * jnp.exp(prior[offset + index, l])
        for l in range(1, wide - 1):
            put(buf1, l, adv0[l - 1, 8 : 8 + nz] + nu[l - 1] * lap0[l - 1, 8 : 8 + nz], nz)
        src, dst = buf1, buf0
        for sweep in range(1, ITERS):
            low, high = sweep + 1, wide - sweep - 1
            back, centre = src[low - 1, 8 : 8 + nz], src[low, 8 : 8 + nz]
            for l in range(low, high):
                front = src[l + 1, 8 : 8 + nz]
                lap = back + front + neighbours(src, l, centre, nz, ny) - 6.0 * centre
                value = centre + nu[l - 1] * lap - 0.15 * (centre - back) + 0.01
                if sweep == ITERS - 1:
                    out_ref[m, l - ITERS] = value
                else:
                    put(dst, l, value, nz)
                back, centre = centre, front
            src, dst = dst, src
        if chunk == 0:
            for s in range(4):
                cell = cells_ref[0, s]
                layer, z = cell // (nz * ny), lax.rem(cell, nz * ny) // ny
                rows[pl.ds(s * 16 + place * part + index, 1), :] = out_ref[m, layer, pl.ds(z, 1), :]
        return carry

    lax.fori_loop(0, group, member, 0)


def sweeps(odd, prior, flow, visc, cells, halo, chunk, before=None, after=None):
    _, layers, nz, ny = prior.shape
    part, place = PARTS[chunk]
    wide = layers + 2 * ITERS
    padded = (wide - 2, nz + 16, ny)
    anywhere = pl.BlockSpec(memory_space=pl.ANY)
    hbm = pl.BlockSpec(memory_space=pltpu.HBM)
    args = [odd, cells, prior, flow, visc]
    specs = [SMEM] * 2 + [VMEM] * 3
    scratch = [
        pltpu.VMEM((wide, nz + 16, ny), F32),
        pltpu.VMEM((wide, nz + 16, ny), F32),
        pltpu.VMEM((wide - 2, nz, ny), F32),
    ]
    alias = {}
    shapes = [prior.shape]
    if chunk:
        velocity, _, lap0, adv0 = before
        args += [pltpu.with_memory_space_constraint(x, pltpu.HBM) for x in (*halo, lap0, adv0)] + [after, velocity]
        specs += [hbm] * 4 + [anywhere, hbm]
        args[2:4] = [pltpu.with_memory_space_constraint(x, pltpu.HBM) for x in (prior, flow)]
        specs[2:4] = [hbm, hbm]
        alias = {len(args) - 1: 0}
        scratch += [pltpu.VMEM(padded, F32)] * 2 + [pltpu.VMEM(halo[0].shape, BF16)] * 2
        scratch += [pltpu.VMEM((part, layers, nz, ny), F32), pltpu.SemaphoreType.DMA((5,))]
        shapes += [(8, ny)]
    else:
        args += [*halo, after]
        specs += [VMEM] * 2 + [anywhere]
        shapes += [(64, ny), padded, padded]
    return pl.pallas_call(
        functools.partial(sweep_kernel, chunk),
        grid=(STEPS,),
        in_specs=specs,
        out_specs=[pl.BlockSpec((part // STEPS, layers, nz, ny), lambda i: (place * STEPS + i, 0, 0, 0))] + [VMEM] * (len(shapes) - 1),
        out_shape=[jax.ShapeDtypeStruct(shape, F32) for shape in shapes],
        input_output_aliases=alias,
        scratch_shapes=scratch,
        compiler_params=params(),
        name=f"sweeps{chunk}",
    )(*args)


def anomaly_kernel(members_all, prior_ref, a_ref, b_ref, *refs):
    out_ref = refs[-1]
    members, _, nz, ny = prior_ref.shape
    flat = prior_ref.reshape(members * nz, ny)
    mean = (a_ref[0] + b_ref[0]) / members_all
    for z in range(nz):
        rows = flat[pl.ds(z, members, stride=nz), :]
        out_ref[z] = (rows - mean[z : z + 1]).astype(BF16)


def anomalies(prior, totals, members_all, *after):
    members, layers, nz, ny = prior.shape
    total = pl.BlockSpec((1, nz, ny), lambda l: (l, 0, 0))
    return pl.pallas_call(
        functools.partial(anomaly_kernel, members_all),
        grid=(layers,),
        in_specs=[pl.BlockSpec((members, 1, nz, ny), lambda l: (0, l, 0, 0))] + [total] * 2 + [pl.BlockSpec(memory_space=pl.ANY)] * len(after),
        out_specs=pl.BlockSpec((nz, members, ny), lambda l: (l, 0, 0)),
        out_shape=jax.ShapeDtypeStruct((layers * nz, members, ny), BF16),
        compiler_params=params(),
        name="anomalies",
    )(prior, *totals, *after)


def slots_kernel(probes, slot_ref, value_ref, var_ref, noise_ref, after, seen_ref, weight_ref, stack):
    members, count = noise_ref.shape
    stack[...] = jnp.zeros_like(stack)
    stack[0:members] = noise_ref[...]
    stack[members : members + 1] = value_ref[...]
    stack[members + 1 : members + 2] = var_ref[...]
    slot = slot_ref[...]
    place = lax.rem(slot, probes) * (count // probes) + slot // probes
    row = lax.broadcasted_iota(jnp.int32, (count, count), 0)
    chosen = jnp.where(row == place, 1.0, 0.0)
    ordered = lax.dot_general(
        chosen, stack[...], (((1,), (1,)), ((), ())), precision=lax.Precision.HIGHEST, preferred_element_type=F32
    )
    value = ordered[:, members : members + 1]
    var = ordered[:, members + 1 : members + 2]
    seen_ref[...] = value + jnp.sqrt(var) * ordered
    weight_ref[...] = jnp.broadcast_to(1.0 / var, weight_ref.shape)


def in_slots(slot, value, var, noise, probes, after):
    count = slot.shape[0]
    shape = jax.ShapeDtypeStruct((count, 128), F32)
    return pl.pallas_call(
        functools.partial(slots_kernel, probes),
        in_specs=[VMEM] * 4 + [pl.BlockSpec(memory_space=pl.ANY)],
        out_specs=[VMEM] * 2,
        out_shape=[shape, shape],
        scratch_shapes=[pltpu.VMEM((128, count), F32)],
        cost_estimate=pl.CostEstimate(flops=0, bytes_accessed=1 << 26, transcendentals=0),
        compiler_params=params(),
        name="slots",
    )(slot[None], value[None], var[None], noise, after)


def dot(a, b, dims):
    return lax.dot_general(a, b, (dims, ((), ())), precision=lax.Precision.HIGHEST, preferred_element_type=F32)


def solve_kernel(members, here, me_ref, vals_ref, seen_ref, weight_ref, beside_any, prior_hbm, out_ref, beside_ref, prior_ref, scr, sems):
    fetches = [
        pltpu.make_async_copy(beside_any, beside_ref, sems.at[0]),
        pltpu.make_async_copy(prior_hbm, prior_ref, sems.at[1]),
    ]
    for fetch in fetches:
        fetch.start()
    devices, ny = vals_ref.shape
    groups = members // here
    tiles = devices // groups
    probes = 64 // here
    lane = lax.broadcasted_iota(jnp.int32, (tiles, ny), 1)
    parts = [vals_ref[pl.ds(g, tiles, stride=groups), :] for g in range(groups)]
    slabs = []
    for s in range(probes):
        slab = jnp.zeros((tiles, ny), F32)
        for g in range(groups):
            shift = (g - s) * here % ny
            moved = pltpu.roll(parts[g], shift, 1) if shift else parts[g]
            slab = jnp.where((lane >= g * here) & (lane < (g + 1) * here), moved, slab)
        slabs.append(slab)
    predicted = jnp.concatenate(slabs, axis=0)
    lanes = lax.broadcasted_iota(jnp.int32, predicted.shape, 1)
    mean = jnp.sum(predicted, axis=1, keepdims=True) / members
    spread = jnp.where(lanes < members, predicted - mean, 0.0)
    scaled = (spread * weight_ref[...]).T
    gram = dot(scaled, spread, ((1,), (0,)))
    rhs = dot(scaled, seen_ref[...] - predicted, ((1,), (0,)))
    half = 0.5 * jnp.max(jnp.sum(jnp.abs(gram), axis=1))
    alpha = 1.0 / (members - 1.0 + half)
    diagonal = lax.broadcasted_iota(jnp.int32, gram.shape, 0) == lax.broadcasted_iota(jnp.int32, gram.shape, 1)
    error = (jnp.where(diagonal, alpha * half, 0.0) - alpha * gram)[:members]
    rest = jnp.zeros((ny - members, 2 * ny), F32)

    def more(state):
        return (state[0] > 2e-6) & (state[1] < 40)

    def double(state):
        size, count, power_of, x = state
        right = jnp.concatenate([jnp.concatenate([power_of, x], axis=1), rest], axis=0)
        both = dot(power_of, right, ((1,), (0,)))
        return size * size, count + 1, both[:, :ny], x + both[:, ny:]

    x = lax.while_loop(more, double, (half * alpha, 0, error, alpha * rhs[:members]))[3]
    me = me_ref[0]
    scr[0:members] = x
    order = [scr[pl.ds(pl.multiple_of((me ^ g) * here, here), here), :] for g in range(groups)]
    scr[...] = jnp.concatenate(order + [jnp.zeros((ny - members, ny), F32)], axis=0).T
    mine = scr[pl.ds(pl.multiple_of(me * here, here), here), :]
    out_ref[...] = mine[:, :members].astype(BF16)
    for fetch in fetches:
        fetch.wait()


def solve(vals, seen, weight, me, members, here, beside, prior):
    return pl.pallas_call(
        functools.partial(solve_kernel, members, here),
        in_specs=[SMEM] + [VMEM] * 3 + [pl.BlockSpec(memory_space=pl.ANY), pl.BlockSpec(memory_space=pltpu.HBM)],
        out_specs=[VMEM] * 3,
        out_shape=[
            jax.ShapeDtypeStruct((here, members), BF16),
            jax.ShapeDtypeStruct(beside.shape, BF16),
            jax.ShapeDtypeStruct(prior.shape, F32),
        ],
        scratch_shapes=[pltpu.VMEM((128, 128), F32), pltpu.SemaphoreType.DMA((2,))],
        compiler_params=params(),
        name="solve",
    )(me, vals, seen, weight, beside, pltpu.with_memory_space_constraint(prior, pltpu.HBM))


def update_kernel(weights_ref, prior_ref, *refs):
    blocks, (out_hbm, out_ref, sems) = refs[:4], refs[4:]
    here, layers, nz, ny = prior_ref.shape
    members = weights_ref.shape[1]
    tall = (here * ROWS, here)
    spread = lax.broadcasted_iota(jnp.int32, tall, 0) // ROWS == lax.broadcasted_iota(jnp.int32, tall, 1)
    wide = (members, members * ROWS)
    column = lax.broadcasted_iota(jnp.int32, wide, 1)
    source = column // (here * ROWS) * here + column % here
    repeat = lax.broadcasted_iota(jnp.int32, wide, 0) == source
    lhs = jnp.dot(jnp.where(spread, 1.0, 0.0).astype(BF16), weights_ref[...], preferred_element_type=F32)
    lhs = jnp.dot(lhs.astype(BF16), jnp.where(repeat, 1.0, 0.0).astype(BF16), preferred_element_type=F32)
    row = lax.broadcasted_iota(jnp.int32, lhs.shape, 0)
    column = lax.broadcasted_iota(jnp.int32, lhs.shape, 1)
    lhs = jnp.where(row % ROWS == column // here % ROWS, lhs, 0.0).astype(BF16)
    places = [(l, z) for l in range(layers) for z in range(0, nz, ROWS)]
    stores = []
    for p in range(0, len(places), 2):
        pair = places[p : p + 2]
        sides = []
        for l, z in pair:
            first = l * nz + z
            sides.append(jnp.concatenate([b[first : first + ROWS].reshape(ROWS * here, ny) for b in blocks], axis=0))
        update = jnp.dot(lhs, jnp.concatenate(sides, axis=1), preferred_element_type=F32)
        for i, (l, z) in enumerate(pair):
            part = update[:, i * ny : (i + 1) * ny]
            for m in range(here):
                out_ref[m, l, z : z + ROWS] = prior_ref[m, l, z : z + ROWS] + part[m * ROWS : (m + 1) * ROWS]
            if z + ROWS == nz:
                stores.append(pltpu.make_async_copy(out_ref.at[:, l], out_hbm.at[:, l], sems.at[l]))
                stores[-1].start()
    for store in stores:
        store.wait()


def updated(weights, prior, mine, beside, over, far):
    layers = prior.shape[1]
    return pl.pallas_call(
        update_kernel,
        in_specs=[VMEM] * 6,
        out_specs=pl.BlockSpec(memory_space=pltpu.HBM),
        out_shape=jax.ShapeDtypeStruct(prior.shape, F32),
        scratch_shapes=[pltpu.VMEM(prior.shape, F32), pltpu.SemaphoreType.DMA((layers,))],
        compiler_params=params(),
        name="update",
    )(weights, prior, mine, beside, over, far)


def per_device(prior, base_flow, base_visc, probe_cells, obs_slot, obs_values, obs_var, obs_noise):
    here = prior.shape[0]
    tiles, groups = lax.axis_size("tile"), lax.axis_size("mem")
    members = here * groups
    me = lax.axis_index("mem").astype(jnp.int32).reshape(1)

    odd = (lax.axis_index("tile") & 1).astype(jnp.int32).reshape(1)

    def swap(x, first):
        pairs = [((first + 2 * i) % tiles, (first + 2 * i + 1) % tiles) for i in range(tiles // 2)]
        return lax.ppermute(x, "tile", pairs + [(b, a) for a, b in pairs])

    def across(x, bits):
        return lax.ppermute(x, "mem", [(i, i ^ bits) for i in range(groups)])

    sent = encode(odd, prior, base_flow, base_visc)
    halos = [(swap(sent[2 * c], 0), swap(sent[2 * c + 1], 1)) for c in range(CHUNKS)]
    fields = (odd, prior, base_flow, base_visc, probe_cells)
    seen, weight = in_slots(obs_slot, obs_values, obs_var, obs_noise, probe_cells.shape[1], sent[0])
    first = sweeps(*fields, halos[0], 0, after=seen)
    payload, token = probes(odd, prior, base_visc, probe_cells, halos[1], first, tiles * groups)
    velocity, done = sweeps(*fields, halos[1], 1, first, token)
    total = total_of(prior, sent[0])
    chip = pair_sum(total, across(total, 1))
    totals = [chip, across(chip, 2)]
    mine = anomalies(prior, totals, float(members), first[1], *halos[1])
    beside = across(mine, 1)
    over = across(mine, 2)
    vals = lax.all_to_all(payload, ("tile", "mem"), 0, 0, tiled=True)
    over = held(over, vals, done)
    far = across(over, 1)
    weights, beside, near_prior = solve(vals, seen, weight, me, members, here, beside, prior)
    return velocity, updated(weights, near_prior, mine, beside, over, far)


def solution(mesh):
    placed = (
        P("mem", "tile", None, None),
        P("tile", None, None),
        P("tile", None, None),
        P("tile", None),
        P(),
        P(),
        P(),
        P(),
    )
    return jax.shard_map(
        per_device,
        mesh=mesh,
        in_specs=placed,
        out_specs=(P("mem", "tile", None, None), P("mem", "tile", None, None)),
        check_vma=False,
    )
```

```python
import functools
import math

import jax
import jax.numpy as jnp
from jax import lax
from jax.experimental import pallas as pl
from jax.experimental.pallas import tpu as pltpu
from jax.sharding import PartitionSpec as P

ITERS = 4
PARTS = ((8, 0), (8, 1))
CHUNKS = len(PARTS)
ROWS = 8
WINDOW = 8
WAYS = 2
STEPS = 1
LOG_MID = 0.5 * (math.log(0.02) + math.log(0.05))
LOG_HALF = 0.5 * (math.log(0.05) - math.log(0.02)) + 1.0
NU_SCALE = 124.0 / LOG_HALF
FLOW_SCALE = 31.0
LN2 = math.log(2.0)
VMEM = pl.BlockSpec(memory_space=pltpu.VMEM)
SMEM = pl.BlockSpec(memory_space=pltpu.SMEM)
F32 = jnp.float32
BF16 = jnp.bfloat16


def params(mib=24):
    return pltpu.CompilerParams(vmem_limit_bytes=mib * 1024 * 1024)


def power(x):
    return jnp.exp(x * LN2)


def log2_of(x):
    return jnp.log(x) * (1.0 / LN2)


def encode_kernel(odd_ref, prior_hbm, flow_hbm, visc_hbm, *refs):
    outs, (prior, flow, visc, base, sems) = refs[: 2 * CHUNKS], refs[2 * CHUNKS :]
    layers = prior.shape[1]
    copies = [
        pltpu.make_async_copy(visc_hbm, visc, sems.at[0]),
        pltpu.make_async_copy(flow_hbm, flow, sems.at[1]),
    ]
    for c, (part, place) in enumerate(PARTS):
        span = pl.ds(place * part, part)
        copies.append(pltpu.make_async_copy(prior_hbm.at[span], prior.at[span], sems.at[2 + c]))
    for copy in copies:
        copy.start()
    copies[0].wait()
    base[...] = jnp.log(visc[...]) * NU_SCALE - LOG_MID * NU_SCALE
    copies[1].wait()
    for l in range(layers):
        code = power(flow[l] * FLOW_SCALE).astype(BF16)
        outs[0][l] = code
        outs[1][l] = code
    for c, (part, place) in enumerate(PARTS):
        copies[2 + c].wait()
        inner_ref, outer_ref = outs[2 * c], outs[2 * c + 1]
        first = layers if c == 0 else 0

        def members(right_ref, left_ref):
            def member(m, carry):
                for l in range(layers):
                    code = power(prior[place * part + m, l] * NU_SCALE + base[l]).astype(BF16)
                    if l >= 1:
                        right_ref[first + m * 3 + l - 1] = code
                    if l < 3:
                        left_ref[first + m * 3 + l] = code
                return carry

            lax.fori_loop(0, part, member, 0)

        @pl.when(odd_ref[0] == 0)
        def _():
            members(inner_ref, outer_ref)

        @pl.when(odd_ref[0] == 1)
        def _():
            members(outer_ref, inner_ref)


def encode(odd, prior, flow, visc):
    members, layers, nz, ny = prior.shape
    shapes = []
    for c, (part, _) in enumerate(PARTS):
        slabs = 3 * part + (layers if c == 0 else 0)
        shapes += [jax.ShapeDtypeStruct((slabs, nz, ny), BF16)] * 2
    return pl.pallas_call(
        encode_kernel,
        in_specs=[SMEM] + [pl.BlockSpec(memory_space=pltpu.HBM)] * 3,
        out_specs=[VMEM] * len(shapes),
        out_shape=shapes,
        scratch_shapes=[
            pltpu.VMEM(prior.shape, F32),
            pltpu.VMEM(flow.shape, F32),
            pltpu.VMEM(visc.shape, F32),
            pltpu.VMEM(visc.shape, F32),
            pltpu.SemaphoreType.DMA((2 + CHUNKS,)),
        ],
        compiler_params=params(),
        name="encode",
    )(odd, *[pltpu.with_memory_space_constraint(x, pltpu.HBM) for x in (prior, flow, visc)])


def total_kernel(prior_ref, after, out_ref):
    out_ref[...] = prior_ref[0]
    for m in range(1, prior_ref.shape[0]):
        out_ref[...] += prior_ref[m]


def total_of(prior, after):
    return pl.pallas_call(
        total_kernel,
        in_specs=[VMEM, pl.BlockSpec(memory_space=pl.ANY)],
        out_specs=VMEM,
        out_shape=jax.ShapeDtypeStruct(prior.shape[1:], F32),
        compiler_params=params(),
        name="total",
    )(prior, after)


def pair_sum_kernel(a_ref, b_ref, out_ref):
    out_ref[...] = a_ref[...] + b_ref[...]


def pair_sum(a, b):
    return pl.pallas_call(
        pair_sum_kernel,
        in_specs=[VMEM] * 2,
        out_specs=VMEM,
        out_shape=jax.ShapeDtypeStruct(a.shape, F32),
        compiler_params=params(),
        name="pair_sum",
    )(a, b)


def hold_kernel(*refs):
    pass


def held(value, *after):
    return pl.pallas_call(
        hold_kernel,
        in_specs=[VMEM] * (1 + len(after)),
        out_specs=VMEM,
        out_shape=jax.ShapeDtypeStruct(value.shape, value.dtype),
        input_output_aliases={0: 0},
        compiler_params=params(),
        name="hold",
    )(value, *after)


def neighbours(buf, l, centre, nz, ny):
    lane = lax.broadcasted_iota(jnp.int32, centre.shape, 1)
    below = jnp.where(lane == 0, 0.0, pltpu.roll(centre, 1, 1))
    above = jnp.where(lane == ny - 1, 0.0, pltpu.roll(centre, ny - 1, 1))
    return (buf[l, 7 : 7 + nz] + buf[l, 9 : 9 + nz]) + (below + above)


def put(buf, l, value, nz):
    buf[l, 8 : 8 + nz] = value
    buf[l, 7:8] = value[nz - 1 : nz]
    buf[l, 8 + nz : 9 + nz] = value[0:1]


def wrap(buf, l, value, nz):
    buf[l, 8 : 8 + nz] = value
    buf[l, 5:8] = value[nz - 3 : nz]
    buf[l, 8 + nz : 12 + nz] = value[0:4]


def viscosity_from(code):
    return jnp.exp(jnp.log(code.astype(F32)) * (1.0 / (LN2 * NU_SCALE)) + LOG_MID)


def probe_kernel(devices, odd_ref, cells_ref, prior_ref, visc_ref, inner_ref, outer_ref, lap0, adv0, rows_in, lines_ref, token_ref, nus, held_rows, rows):
    _, layers, nz, ny = prior_ref.shape
    part, place = PARTS[-1]
    odd = odd_ref[0]
    rows[...] = rows_in[...]
    lane = lax.broadcasted_iota(jnp.int32, (WINDOW, ny), 1)

    def step(slot, back, centre, front, visc):
        held_rows[slot, 4 : 4 + WINDOW] = centre
        sides = held_rows[slot, 3 : 3 + WINDOW] + held_rows[slot, 5 : 5 + WINDOW]
        below = jnp.where(lane == 0, 0.0, pltpu.roll(centre, 1, 1))
        above = jnp.where(lane == ny - 1, 0.0, pltpu.roll(centre, ny - 1, 1))
        lap = back + front + (sides + (below + above)) - 6.0 * centre
        return centre + visc * lap - 0.15 * (centre - back) + 0.01

    def member(m, carry, way):
        nu = nus.at[way]
        for l in range(3):
            for side_ref, ahead in ((inner_ref, 1 - odd), (outer_ref, odd)):
                wrap(nu, ahead * (3 + layers) + l, viscosity_from(side_ref[m * 3 + l]), nz)
        for l in range(layers):
            wrap(nu, 3 + l, visc_ref[l] * jnp.exp(prior_ref[place * part + m, l]), nz)
        for s in range(4):
            cell = cells_ref[0, s]
            layer, z = cell // (nz * ny), lax.rem(cell, nz * ny) // ny
            window = pl.ds(z + 5, WINDOW)
            reach = [layer + j for j in range(2 * ITERS - 1)]
            visc = [nu[l, window] for l in reach]
            speed = [adv0[l, window] + v * lap0[l, window] for l, v in zip(reach, visc)]
            slot = (way * 4 + s) * 9
            for _ in range(1, ITERS):
                visc = visc[1:-1]
                speed = [step(slot + k, *speed[k : k + 3], v) for k, v in enumerate(visc)]
                slot += len(visc)
            rows[pl.ds(s * 16 + place * part + m, 1), :] = speed[0][3:4]
        return carry

    def one_group(i, carry):
        for way in range(WAYS):
            member(i * WAYS + way, carry, way)
        return carry

    lax.fori_loop(0, part // WAYS, one_group, 0)
    lane = lax.broadcasted_iota(jnp.int32, rows.shape, 1)
    row = lax.broadcasted_iota(jnp.int32, rows.shape, 0)
    y = jnp.zeros(rows.shape, jnp.int32)
    for s in range(4):
        y = jnp.where(row // 16 == s, lax.rem(cells_ref[0, s], ny), y)
    picked = jnp.sum(jnp.where(lane == y, rows[...], 0.0), axis=1, keepdims=True)
    line = jnp.sum(jnp.where(lane == row, picked, 0.0), axis=0, keepdims=True)
    lines_ref[...] = jnp.broadcast_to(line, (devices, ny))
    token_ref[...] = rows[0:8]


def probes(odd, prior, visc, cells, halo, first, devices):
    _, layers, nz, ny = prior.shape
    _, rows, lap0, adv0 = first
    return pl.pallas_call(
        functools.partial(probe_kernel, devices),
        in_specs=[SMEM] * 2 + [VMEM] * 7,
        out_specs=[VMEM] * 2,
        out_shape=[jax.ShapeDtypeStruct((devices, ny), F32), jax.ShapeDtypeStruct((8, ny), F32)],
        scratch_shapes=[
            pltpu.VMEM((WAYS,) + lap0.shape, F32),
            pltpu.VMEM((36 * WAYS, WINDOW + 8, ny), F32),
            pltpu.VMEM(rows.shape, F32),
        ],
        compiler_params=params(),
        name="probes",
    )(odd, cells, prior, visc, *halo, lap0, adv0, rows)


def sweep_kernel(chunk, odd_ref, cells_ref, prior_ref, flow_ref, visc_ref, inner_ref, outer_ref, *rest):
    _, layers, nz, ny = prior_ref.shape
    part, place = PARTS[chunk]
    group = part // STEPS
    step = pl.program_id(0)
    wide = layers + 2 * ITERS
    odd = odd_ref[0]
    partners = ((inner_ref, 1 - odd), (outer_ref, odd))
    if chunk == 0:
        _, out_ref, rows, lap0, adv0, buf0, buf1, nu = rest
        prior, offset = prior_ref, place * part

        @pl.when(step == 0)
        def _():
            for l in range(ITERS):
                for side_ref, ahead in partners:
                    flow = log2_of(side_ref[l].astype(F32)) * (1.0 / FLOW_SCALE)
                    put(buf0, ahead * (ITERS + layers) + l, flow, nz)
            for l in range(layers):
                put(buf0, ITERS + l, flow_ref[l], nz)
            for l in range(1, wide - 1):
                centre, back = buf0[l, 8 : 8 + nz], buf0[l - 1, 8 : 8 + nz]
                sides = back + buf0[l + 1, 8 : 8 + nz] + neighbours(buf0, l, centre, nz, ny)
                wrap(lap0, l - 1, sides - 6.0 * centre, nz)
                wrap(adv0, l - 1, centre - 0.15 * (centre - back) + 0.01, nz)
            rows[...] = jnp.zeros_like(rows)

    else:
        sources, (_, _, out_ref, token_ref, buf0, buf1, nu), (lap0, adv0, *sides, prior, sems) = rest[:2], rest[2:9], rest[9:]
        copies = [
            pltpu.make_async_copy(source, target, sems.at[i])
            for i, (source, target) in enumerate(
                zip(
                    (prior_ref.at[pl.ds(place * part, part)], inner_ref, outer_ref) + tuple(sources),
                    (prior, *sides, lap0, adv0),
                )
            )
        ]
        for copy in copies:
            copy.start()
        for copy in copies:
            copy.wait()
        partners = ((sides[0], 1 - odd), (sides[1], odd))
        offset = 0
        token_ref[...] = jnp.zeros_like(token_ref)

    base_slabs = layers if chunk == 0 else 0

    def member(m, carry):
        index = step * group + m
        first = base_slabs + index * 3
        for l in range(3):
            for side_ref, ahead in partners:
                code = side_ref[first + l]
                nu[ahead * (3 + layers) + l] = viscosity_from(code)
        for l in range(layers):
            nu[3 + l] = visc_ref[l] * jnp.exp(prior[offset + index, l])
        for l in range(1, wide - 1):
            put(buf1, l, adv0[l - 1, 8 : 8 + nz] + nu[l - 1] * lap0[l - 1, 8 : 8 + nz], nz)
        src, dst = buf1, buf0
        for sweep in range(1, ITERS):
            low, high = sweep + 1, wide - sweep - 1
            back, centre = src[low - 1, 8 : 8 + nz], src[low, 8 : 8 + nz]
            for l in range(low, high):
                front = src[l + 1, 8 : 8 + nz]
                lap = back + front + neighbours(src, l, centre, nz, ny) - 6.0 * centre
                value = centre + nu[l - 1] * lap - 0.15 * (centre - back) + 0.01
                if sweep == ITERS - 1:
                    out_ref[m, l - ITERS] = value
                else:
                    put(dst, l, value, nz)
                back, centre = centre, front
            src, dst = dst, src
        if chunk == 0:
            for s in range(4):
                cell = cells_ref[0, s]
                layer, z = cell // (nz * ny), lax.rem(cell, nz * ny) // ny
                rows[pl.ds(s * 16 + place * part + index, 1), :] = out_ref[m, layer, pl.ds(z, 1), :]
        return carry

    lax.fori_loop(0, group, member, 0)


def sweeps(odd, prior, flow, visc, cells, halo, chunk, before=None, after=None):
    _, layers, nz, ny = prior.shape
    part, place = PARTS[chunk]
    wide = layers + 2 * ITERS
    padded = (wide - 2, nz + 16, ny)
    anywhere = pl.BlockSpec(memory_space=pl.ANY)
    hbm = pl.BlockSpec(memory_space=pltpu.HBM)
    args = [odd, cells, prior, flow, visc]
    specs = [SMEM] * 2 + [VMEM] * 3
    scratch = [
        pltpu.VMEM((wide, nz + 16, ny), F32),
        pltpu.VMEM((wide, nz + 16, ny), F32),
        pltpu.VMEM((wide - 2, nz, ny), F32),
    ]
    alias = {}
    shapes = [prior.shape]
    if chunk:
        velocity, _, lap0, adv0 = before
        args += [pltpu.with_memory_space_constraint(x, pltpu.HBM) for x in (*halo, lap0, adv0)] + [after, velocity]
        specs += [hbm] * 4 + [anywhere, hbm]
        args[2:4] = [pltpu.with_memory_space_constraint(x, pltpu.HBM) for x in (prior, flow)]
        specs[2:4] = [hbm, hbm]
        alias = {len(args) - 1: 0}
        scratch += [pltpu.VMEM(padded, F32)] * 2 + [pltpu.VMEM(halo[0].shape, BF16)] * 2
        scratch += [pltpu.VMEM((part, layers, nz, ny), F32), pltpu.SemaphoreType.DMA((5,))]
        shapes += [(8, ny)]
    else:
        args += [*halo, after]
        specs += [VMEM] * 2 + [anywhere]
        shapes += [(64, ny), padded, padded]
    return pl.pallas_call(
        functools.partial(sweep_kernel, chunk),
        grid=(STEPS,),
        in_specs=specs,
        out_specs=[pl.BlockSpec((part // STEPS, layers, nz, ny), lambda i: (place * STEPS + i, 0, 0, 0))] + [VMEM] * (len(shapes) - 1),
        out_shape=[jax.ShapeDtypeStruct(shape, F32) for shape in shapes],
        input_output_aliases=alias,
        scratch_shapes=scratch,
        compiler_params=params(),
        name=f"sweeps{chunk}",
    )(*args)


def anomaly_kernel(members_all, prior_ref, a_ref, b_ref, *refs):
    out_ref = refs[-1]
    members, _, nz, ny = prior_ref.shape
    flat = prior_ref.reshape(members * nz, ny)
    mean = (a_ref[0] + b_ref[0]) / members_all
    for z in range(nz):
        rows = flat[pl.ds(z, members, stride=nz), :]
        out_ref[z] = (rows - mean[z : z + 1]).astype(BF16)


def anomalies(prior, totals, members_all, *after):
    members, layers, nz, ny = prior.shape
    total = pl.BlockSpec((1, nz, ny), lambda l: (l, 0, 0))
    return pl.pallas_call(
        functools.partial(anomaly_kernel, members_all),
        grid=(layers,),
        in_specs=[pl.BlockSpec((members, 1, nz, ny), lambda l: (0, l, 0, 0))] + [total] * 2 + [pl.BlockSpec(memory_space=pl.ANY)] * len(after),
        out_specs=pl.BlockSpec((nz, members, ny), lambda l: (l, 0, 0)),
        out_shape=jax.ShapeDtypeStruct((layers * nz, members, ny), BF16),
        compiler_params=params(),
        name="anomalies",
    )(prior, *totals, *after)


def slots_kernel(probes, slot_ref, value_ref, var_ref, noise_ref, after, seen_ref, weight_ref, stack):
    members, count = noise_ref.shape
    stack[...] = jnp.zeros_like(stack)
    stack[0:members] = noise_ref[...]
    stack[members : members + 1] = value_ref[...]
    stack[members + 1 : members + 2] = var_ref[...]
    slot = slot_ref[...]
    place = lax.rem(slot, probes) * (count // probes) + slot // probes
    row = lax.broadcasted_iota(jnp.int32, (count, count), 0)
    chosen = jnp.where(row == place, 1.0, 0.0)
    ordered = lax.dot_general(
        chosen, stack[...], (((1,), (1,)), ((), ())), precision=lax.Precision.HIGHEST, preferred_element_type=F32
    )
    value = ordered[:, members : members + 1]
    var = ordered[:, members + 1 : members + 2]
    seen_ref[...] = value + jnp.sqrt(var) * ordered
    weight_ref[...] = jnp.broadcast_to(1.0 / var, weight_ref.shape)


def in_slots(slot, value, var, noise, probes, after):
    count = slot.shape[0]
    shape = jax.ShapeDtypeStruct((count, 128), F32)
    return pl.pallas_call(
        functools.partial(slots_kernel, probes),
        in_specs=[VMEM] * 4 + [pl.BlockSpec(memory_space=pl.ANY)],
        out_specs=[VMEM] * 2,
        out_shape=[shape, shape],
        scratch_shapes=[pltpu.VMEM((128, count), F32)],
        cost_estimate=pl.CostEstimate(flops=0, bytes_accessed=1 << 26, transcendentals=0),
        compiler_params=params(),
        name="slots",
    )(slot[None], value[None], var[None], noise, after)


def dot(a, b, dims):
    return lax.dot_general(a, b, (dims, ((), ())), precision=lax.Precision.HIGHEST, preferred_element_type=F32)


def solve_kernel(members, here, me_ref, vals_ref, seen_ref, weight_ref, beside_any, prior_hbm, out_ref, beside_ref, prior_ref, scr, sems):
    fetches = [
        pltpu.make_async_copy(beside_any, beside_ref, sems.at[0]),
        pltpu.make_async_copy(prior_hbm, prior_ref, sems.at[1]),
    ]
    for fetch in fetches:
        fetch.start()
    devices, ny = vals_ref.shape
    groups = members // here
    tiles = devices // groups
    probes = 64 // here
    lane = lax.broadcasted_iota(jnp.int32, (tiles, ny), 1)
    parts = [vals_ref[pl.ds(g, tiles, stride=groups), :] for g in range(groups)]
    slabs = []
    for s in range(probes):
        slab = jnp.zeros((tiles, ny), F32)
        for g in range(groups):
            shift = (g - s) * here % ny
            moved = pltpu.roll(parts[g], shift, 1) if shift else parts[g]
            slab = jnp.where((lane >= g * here) & (lane < (g + 1) * here), moved, slab)
        slabs.append(slab)
    predicted = jnp.concatenate(slabs, axis=0)
    lanes = lax.broadcasted_iota(jnp.int32, predicted.shape, 1)
    mean = jnp.sum(predicted, axis=1, keepdims=True) / members
    spread = jnp.where(lanes < members, predicted - mean, 0.0)
    scaled = (spread * weight_ref[...]).T
    gram = dot(scaled, spread, ((1,), (0,)))
    rhs = dot(scaled, seen_ref[...] - predicted, ((1,), (0,)))
    half = 0.5 * jnp.max(jnp.sum(jnp.abs(gram), axis=1))
    alpha = 1.0 / (members - 1.0 + half)
    diagonal = lax.broadcasted_iota(jnp.int32, gram.shape, 0) == lax.broadcasted_iota(jnp.int32, gram.shape, 1)
    error = (jnp.where(diagonal, alpha * half, 0.0) - alpha * gram)[:members]
    rest = jnp.zeros((ny - members, 2 * ny), F32)

    def more(state):
        return (state[0] > 2e-6) & (state[1] < 40)

    def double(state):
        size, count, power_of, x = state
        right = jnp.concatenate([jnp.concatenate([power_of, x], axis=1), rest], axis=0)
        both = dot(power_of, right, ((1,), (0,)))
        return size * size, count + 1, both[:, :ny], x + both[:, ny:]

    x = lax.while_loop(more, double, (half * alpha, 0, error, alpha * rhs[:members]))[3]
    me = me_ref[0]
    scr[0:members] = x
    order = [scr[pl.ds(pl.multiple_of((me ^ g) * here, here), here), :] for g in range(groups)]
    scr[...] = jnp.concatenate(order + [jnp.zeros((ny - members, ny), F32)], axis=0).T
    mine = scr[pl.ds(pl.multiple_of(me * here, here), here), :]
    out_ref[...] = mine[:, :members].astype(BF16)
    for fetch in fetches:
        fetch.wait()


def solve(vals, seen, weight, me, members, here, beside, prior):
    return pl.pallas_call(
        functools.partial(solve_kernel, members, here),
        in_specs=[SMEM] + [VMEM] * 3 + [pl.BlockSpec(memory_space=pl.ANY), pl.BlockSpec(memory_space=pltpu.HBM)],
        out_specs=[VMEM] * 3,
        out_shape=[
            jax.ShapeDtypeStruct((here, members), BF16),
            jax.ShapeDtypeStruct(beside.shape, BF16),
            jax.ShapeDtypeStruct(prior.shape, F32),
        ],
        scratch_shapes=[pltpu.VMEM((128, 128), F32), pltpu.SemaphoreType.DMA((2,))],
        compiler_params=params(),
        name="solve",
    )(me, vals, seen, weight, beside, pltpu.with_memory_space_constraint(prior, pltpu.HBM))


def update_kernel(weights_ref, prior_ref, *refs):
    blocks, (out_hbm, out_ref, sems) = refs[:4], refs[4:]
    here, layers, nz, ny = prior_ref.shape
    members = weights_ref.shape[1]
    tall = (here * ROWS, here)
    spread = lax.broadcasted_iota(jnp.int32, tall, 0) // ROWS == lax.broadcasted_iota(jnp.int32, tall, 1)
    wide = (members, members * ROWS)
    column = lax.broadcasted_iota(jnp.int32, wide, 1)
    source = column // (here * ROWS) * here + column % here
    repeat = lax.broadcasted_iota(jnp.int32, wide, 0) == source
    lhs = jnp.dot(jnp.where(spread, 1.0, 0.0).astype(BF16), weights_ref[...], preferred_element_type=F32)
    lhs = jnp.dot(lhs.astype(BF16), jnp.where(repeat, 1.0, 0.0).astype(BF16), preferred_element_type=F32)
    row = lax.broadcasted_iota(jnp.int32, lhs.shape, 0)
    column = lax.broadcasted_iota(jnp.int32, lhs.shape, 1)
    lhs = jnp.where(row % ROWS == column // here % ROWS, lhs, 0.0).astype(BF16)
    places = [(l, z) for l in range(layers) for z in range(0, nz, ROWS)]
    stores = []
    for p in range(0, len(places), 2):
        pair = places[p : p + 2]
        sides = []
        for l, z in pair:
            first = l * nz + z
            sides.append(jnp.concatenate([b[first : first + ROWS].reshape(ROWS * here, ny) for b in blocks], axis=0))
        update = jnp.dot(lhs, jnp.concatenate(sides, axis=1), preferred_element_type=F32)
        for i, (l, z) in enumerate(pair):
            part = update[:, i * ny : (i + 1) * ny]
            for m in range(here):
                out_ref[m, l, z : z + ROWS] = prior_ref[m, l, z : z + ROWS] + part[m * ROWS : (m + 1) * ROWS]
            if z + ROWS == nz:
                stores.append(pltpu.make_async_copy(out_ref.at[:, l], out_hbm.at[:, l], sems.at[l]))
                stores[-1].start()
    for store in stores:
        store.wait()


def updated(weights, prior, mine, beside, over, far):
    layers = prior.shape[1]
    return pl.pallas_call(
        update_kernel,
        in_specs=[VMEM] * 6,
        out_specs=pl.BlockSpec(memory_space=pltpu.HBM),
        out_shape=jax.ShapeDtypeStruct(prior.shape, F32),
        scratch_shapes=[pltpu.VMEM(prior.shape, F32), pltpu.SemaphoreType.DMA((layers,))],
        compiler_params=params(),
        name="update",
    )(weights, prior, mine, beside, over, far)


def per_device(prior, base_flow, base_visc, probe_cells, obs_slot, obs_values, obs_var, obs_noise):
    here = prior.shape[0]
    tiles, groups = lax.axis_size("tile"), lax.axis_size("mem")
    members = here * groups
    me = lax.axis_index("mem").astype(jnp.int32).reshape(1)

    odd = (lax.axis_index("tile") & 1).astype(jnp.int32).reshape(1)

    def swap(x, first):
        pairs = [((first + 2 * i) % tiles, (first + 2 * i + 1) % tiles) for i in range(tiles // 2)]
        return lax.ppermute(x, "tile", pairs + [(b, a) for a, b in pairs])

    def across(x, bits):
        return lax.ppermute(x, "mem", [(i, i ^ bits) for i in range(groups)])

    sent = encode(odd, prior, base_flow, base_visc)
    halos = [(swap(sent[2 * c], 0), swap(sent[2 * c + 1], 1)) for c in range(CHUNKS)]
    fields = (odd, prior, base_flow, base_visc, probe_cells)
    seen, weight = in_slots(obs_slot, obs_values, obs_var, obs_noise, probe_cells.shape[1], sent[0])
    first = sweeps(*fields, halos[0], 0, after=seen)
    payload, token = probes(odd, prior, base_visc, probe_cells, halos[1], first, tiles * groups)
    velocity, done = sweeps(*fields, halos[1], 1, first, token)
    total = total_of(prior, sent[0])
    chip = pair_sum(total, across(total, 1))
    totals = [chip, across(chip, 2)]
    mine = anomalies(prior, totals, float(members), token, *halos[1])
    beside = across(mine, 1)
    over = across(mine, 2)
    vals = lax.all_to_all(payload, ("tile", "mem"), 0, 0, tiled=True)
    over = held(over, vals, done)
    far = across(over, 1)
    weights, beside, near_prior = solve(vals, seen, weight, me, members, here, beside, prior)
    return velocity, updated(weights, near_prior, mine, beside, over, far)


def solution(mesh):
    placed = (
        P("mem", "tile", None, None),
        P("tile", None, None),
        P("tile", None, None),
        P("tile", None),
        P(),
        P(),
        P(),
        P(),
    )
    return jax.shard_map(
        per_device,
        mesh=mesh,
        in_specs=placed,
        out_specs=(P("mem", "tile", None, None), P("mem", "tile", None, None)),
        check_vma=False,
    )
```

```python
import functools
import math

import jax
import jax.numpy as jnp
from jax import lax
from jax.experimental import pallas as pl
from jax.experimental.pallas import tpu as pltpu
from jax.sharding import PartitionSpec as P

ITERS = 4
PARTS = ((8, 0), (8, 1))
CHUNKS = len(PARTS)
ROWS = 8
WINDOW = 8
WAYS = 2
STEPS = 1
LOG_MID = 0.5 * (math.log(0.02) + math.log(0.05))
LOG_HALF = 0.5 * (math.log(0.05) - math.log(0.02)) + 1.0
NU_SCALE = 124.0 / LOG_HALF
FLOW_SCALE = 31.0
LN2 = math.log(2.0)
VMEM = pl.BlockSpec(memory_space=pltpu.VMEM)
SMEM = pl.BlockSpec(memory_space=pltpu.SMEM)
F32 = jnp.float32
BF16 = jnp.bfloat16


def params(mib=24):
    return pltpu.CompilerParams(vmem_limit_bytes=mib * 1024 * 1024)


def power(x):
    return jnp.exp(x * LN2)


def log2_of(x):
    return jnp.log(x) * (1.0 / LN2)


def encode_kernel(odd_ref, prior_hbm, flow_hbm, visc_hbm, *refs):
    outs, (prior, flow, visc, base, sems) = refs[: 2 * CHUNKS], refs[2 * CHUNKS :]
    layers = prior.shape[1]
    copies = [
        pltpu.make_async_copy(visc_hbm, visc, sems.at[0]),
        pltpu.make_async_copy(flow_hbm, flow, sems.at[1]),
    ]
    for c, (part, place) in enumerate(PARTS):
        span = pl.ds(place * part, part)
        copies.append(pltpu.make_async_copy(prior_hbm.at[span], prior.at[span], sems.at[2 + c]))
    for copy in copies:
        copy.start()
    copies[0].wait()
    base[...] = jnp.log(visc[...]) * NU_SCALE - LOG_MID * NU_SCALE
    copies[1].wait()
    for l in range(layers):
        code = power(flow[l] * FLOW_SCALE).astype(BF16)
        outs[0][l] = code
        outs[1][l] = code
    for c, (part, place) in enumerate(PARTS):
        copies[2 + c].wait()
        inner_ref, outer_ref = outs[2 * c], outs[2 * c + 1]
        first = layers if c == 0 else 0

        def members(right_ref, left_ref):
            def member(m, carry):
                for l in range(layers):
                    code = power(prior[place * part + m, l] * NU_SCALE + base[l]).astype(BF16)
                    if l >= 1:
                        right_ref[first + m * 3 + l - 1] = code
                    if l < 3:
                        left_ref[first + m * 3 + l] = code
                return carry

            lax.fori_loop(0, part, member, 0)

        @pl.when(odd_ref[0] == 0)
        def _():
            members(inner_ref, outer_ref)

        @pl.when(odd_ref[0] == 1)
        def _():
            members(outer_ref, inner_ref)


def encode(odd, prior, flow, visc):
    members, layers, nz, ny = prior.shape
    shapes = []
    for c, (part, _) in enumerate(PARTS):
        slabs = 3 * part + (layers if c == 0 else 0)
        shapes += [jax.ShapeDtypeStruct((slabs, nz, ny), BF16)] * 2
    shapes.append(jax.ShapeDtypeStruct(prior.shape, F32))
    return pl.pallas_call(
        encode_kernel,
        in_specs=[SMEM] + [pl.BlockSpec(memory_space=pltpu.HBM)] * 3,
        out_specs=[VMEM] * len(shapes),
        out_shape=shapes,
        scratch_shapes=[
            pltpu.VMEM(flow.shape, F32),
            pltpu.VMEM(visc.shape, F32),
            pltpu.VMEM(visc.shape, F32),
            pltpu.SemaphoreType.DMA((2 + CHUNKS,)),
        ],
        compiler_params=params(),
        name="encode",
    )(odd, *[pltpu.with_memory_space_constraint(x, pltpu.HBM) for x in (prior, flow, visc)])


def total_kernel(prior_ref, after, out_ref):
    out_ref[...] = prior_ref[0]
    for m in range(1, prior_ref.shape[0]):
        out_ref[...] += prior_ref[m]


def total_of(prior, after):
    return pl.pallas_call(
        total_kernel,
        in_specs=[VMEM, pl.BlockSpec(memory_space=pl.ANY)],
        out_specs=VMEM,
        out_shape=jax.ShapeDtypeStruct(prior.shape[1:], F32),
        compiler_params=params(),
        name="total",
    )(prior, after)


def pair_sum_kernel(a_ref, b_ref, out_ref):
    out_ref[...] = a_ref[...] + b_ref[...]


def pair_sum(a, b):
    return pl.pallas_call(
        pair_sum_kernel,
        in_specs=[VMEM] * 2,
        out_specs=VMEM,
        out_shape=jax.ShapeDtypeStruct(a.shape, F32),
        compiler_params=params(),
        name="pair_sum",
    )(a, b)


def hold_kernel(*refs):
    pass


def held(value, *after):
    return pl.pallas_call(
        hold_kernel,
        in_specs=[VMEM] * (1 + len(after)),
        out_specs=VMEM,
        out_shape=jax.ShapeDtypeStruct(value.shape, value.dtype),
        input_output_aliases={0: 0},
        compiler_params=params(),
        name="hold",
    )(value, *after)


def neighbours(buf, l, centre, nz, ny):
    lane = lax.broadcasted_iota(jnp.int32, centre.shape, 1)
    below = jnp.where(lane == 0, 0.0, pltpu.roll(centre, 1, 1))
    above = jnp.where(lane == ny - 1, 0.0, pltpu.roll(centre, ny - 1, 1))
    return (buf[l, 7 : 7 + nz] + buf[l, 9 : 9 + nz]) + (below + above)


def put(buf, l, value, nz):
    buf[l, 8 : 8 + nz] = value
    buf[l, 7:8] = value[nz - 1 : nz]
    buf[l, 8 + nz : 9 + nz] = value[0:1]


def wrap(buf, l, value, nz):
    buf[l, 8 : 8 + nz] = value
    buf[l, 5:8] = value[nz - 3 : nz]
    buf[l, 8 + nz : 12 + nz] = value[0:4]


def viscosity_from(code):
    return jnp.exp(jnp.log(code.astype(F32)) * (1.0 / (LN2 * NU_SCALE)) + LOG_MID)


def probe_kernel(devices, odd_ref, cells_ref, prior_ref, visc_ref, inner_ref, outer_ref, lap0, adv0, rows_in, lines_ref, token_ref, nus, held_rows, rows):
    _, layers, nz, ny = prior_ref.shape
    part, place = PARTS[-1]
    odd = odd_ref[0]
    rows[...] = rows_in[...]
    lane = lax.broadcasted_iota(jnp.int32, (WINDOW, ny), 1)

    def step(slot, back, centre, front, visc):
        held_rows[slot, 4 : 4 + WINDOW] = centre
        sides = held_rows[slot, 3 : 3 + WINDOW] + held_rows[slot, 5 : 5 + WINDOW]
        below = jnp.where(lane == 0, 0.0, pltpu.roll(centre, 1, 1))
        above = jnp.where(lane == ny - 1, 0.0, pltpu.roll(centre, ny - 1, 1))
        lap = back + front + (sides + (below + above)) - 6.0 * centre
        return centre + visc * lap - 0.15 * (centre - back) + 0.01

    def member(m, carry, way):
        nu = nus.at[way]
        for l in range(3):
            for side_ref, ahead in ((inner_ref, 1 - odd), (outer_ref, odd)):
                wrap(nu, ahead * (3 + layers) + l, viscosity_from(side_ref[m * 3 + l]), nz)
        for l in range(layers):
            wrap(nu, 3 + l, visc_ref[l] * jnp.exp(prior_ref[place * part + m, l]), nz)
        for s in range(4):
            cell = cells_ref[0, s]
            layer, z = cell // (nz * ny), lax.rem(cell, nz * ny) // ny
            window = pl.ds(z + 5, WINDOW)
            reach = [layer + j for j in range(2 * ITERS - 1)]
            visc = [nu[l, window] for l in reach]
            speed = [adv0[l, window] + v * lap0[l, window] for l, v in zip(reach, visc)]
            slot = (way * 4 + s) * 9
            for _ in range(1, ITERS):
                visc = visc[1:-1]
                speed = [step(slot + k, *speed[k : k + 3], v) for k, v in enumerate(visc)]
                slot += len(visc)
            rows[pl.ds(s * 16 + place * part + m, 1), :] = speed[0][3:4]
        return carry

    def one_group(i, carry):
        for way in range(WAYS):
            member(i * WAYS + way, carry, way)
        return carry

    lax.fori_loop(0, part // WAYS, one_group, 0)
    lane = lax.broadcasted_iota(jnp.int32, rows.shape, 1)
    row = lax.broadcasted_iota(jnp.int32, rows.shape, 0)
    y = jnp.zeros(rows.shape, jnp.int32)
    for s in range(4):
        y = jnp.where(row // 16 == s, lax.rem(cells_ref[0, s], ny), y)
    picked = jnp.sum(jnp.where(lane == y, rows[...], 0.0), axis=1, keepdims=True)
    line = jnp.sum(jnp.where(lane == row, picked, 0.0), axis=0, keepdims=True)
    lines_ref[...] = jnp.broadcast_to(line, (devices, ny))
    token_ref[...] = rows[0:8]


def probes(odd, prior, visc, cells, halo, first, devices):
    _, layers, nz, ny = prior.shape
    _, rows, lap0, adv0 = first
    return pl.pallas_call(
        functools.partial(probe_kernel, devices),
        in_specs=[SMEM] * 2 + [VMEM] * 7,
        out_specs=[VMEM] * 2,
        out_shape=[jax.ShapeDtypeStruct((devices, ny), F32), jax.ShapeDtypeStruct((8, ny), F32)],
        scratch_shapes=[
            pltpu.VMEM((WAYS,) + lap0.shape, F32),
            pltpu.VMEM((36 * WAYS, WINDOW + 8, ny), F32),
            pltpu.VMEM(rows.shape, F32),
        ],
        compiler_params=params(),
        name="probes",
    )(odd, cells, prior, visc, *halo, lap0, adv0, rows)


def sweep_kernel(chunk, odd_ref, cells_ref, prior_ref, flow_ref, visc_ref, inner_ref, outer_ref, *rest):
    _, layers, nz, ny = prior_ref.shape
    part, place = PARTS[chunk]
    group = part // STEPS
    step = pl.program_id(0)
    wide = layers + 2 * ITERS
    odd = odd_ref[0]
    partners = ((inner_ref, 1 - odd), (outer_ref, odd))
    if chunk == 0:
        _, out_ref, rows, lap0, adv0, buf0, buf1, nu = rest
        prior, offset = prior_ref, place * part

        @pl.when(step == 0)
        def _():
            for l in range(ITERS):
                for side_ref, ahead in partners:
                    flow = log2_of(side_ref[l].astype(F32)) * (1.0 / FLOW_SCALE)
                    put(buf0, ahead * (ITERS + layers) + l, flow, nz)
            for l in range(layers):
                put(buf0, ITERS + l, flow_ref[l], nz)
            for l in range(1, wide - 1):
                centre, back = buf0[l, 8 : 8 + nz], buf0[l - 1, 8 : 8 + nz]
                sides = back + buf0[l + 1, 8 : 8 + nz] + neighbours(buf0, l, centre, nz, ny)
                wrap(lap0, l - 1, sides - 6.0 * centre, nz)
                wrap(adv0, l - 1, centre - 0.15 * (centre - back) + 0.01, nz)
            rows[...] = jnp.zeros_like(rows)

    else:
        sources, (_, _, out_ref, token_ref, buf0, buf1, nu), (lap0, adv0, *sides, prior, sems) = rest[:2], rest[2:9], rest[9:]
        copies = [
            pltpu.make_async_copy(source, target, sems.at[i])
            for i, (source, target) in enumerate(
                zip(
                    (prior_ref.at[pl.ds(place * part, part)], inner_ref, outer_ref) + tuple(sources),
                    (prior, *sides, lap0, adv0),
                )
            )
        ]
        for copy in copies:
            copy.start()
        for copy in copies:
            copy.wait()
        partners = ((sides[0], 1 - odd), (sides[1], odd))
        offset = 0
        token_ref[...] = jnp.zeros_like(token_ref)

    base_slabs = layers if chunk == 0 else 0

    def member(m, carry):
        index = step * group + m
        first = base_slabs + index * 3
        for l in range(3):
            for side_ref, ahead in partners:
                code = side_ref[first + l]
                nu[ahead * (3 + layers) + l] = viscosity_from(code)
        for l in range(layers):
            nu[3 + l] = visc_ref[l] * jnp.exp(prior[offset + index, l])
        for l in range(1, wide - 1):
            put(buf1, l, adv0[l - 1, 8 : 8 + nz] + nu[l - 1] * lap0[l - 1, 8 : 8 + nz], nz)
        src, dst = buf1, buf0
        for sweep in range(1, ITERS):
            low, high = sweep + 1, wide - sweep - 1
            back, centre = src[low - 1, 8 : 8 + nz], src[low, 8 : 8 + nz]
            for l in range(low, high):
                front = src[l + 1, 8 : 8 + nz]
                lap = back + front + neighbours(src, l, centre, nz, ny) - 6.0 * centre
                value = centre + nu[l - 1] * lap - 0.15 * (centre - back) + 0.01
                if sweep == ITERS - 1:
                    out_ref[m, l - ITERS] = value
                else:
                    put(dst, l, value, nz)
                back, centre = centre, front
            src, dst = dst, src
        if chunk == 0:
            for s in range(4):
                cell = cells_ref[0, s]
                layer, z = cell // (nz * ny), lax.rem(cell, nz * ny) // ny
                rows[pl.ds(s * 16 + place * part + index, 1), :] = out_ref[m, layer, pl.ds(z, 1), :]
        return carry

    lax.fori_loop(0, group, member, 0)


def sweeps(odd, prior, flow, visc, cells, halo, chunk, before=None, after=None):
    _, layers, nz, ny = prior.shape
    part, place = PARTS[chunk]
    wide = layers + 2 * ITERS
    padded = (wide - 2, nz + 16, ny)
    anywhere = pl.BlockSpec(memory_space=pl.ANY)
    hbm = pl.BlockSpec(memory_space=pltpu.HBM)
    args = [odd, cells, prior, flow, visc]
    specs = [SMEM] * 2 + [VMEM] * 3
    scratch = [
        pltpu.VMEM((wide, nz + 16, ny), F32),
        pltpu.VMEM((wide, nz + 16, ny), F32),
        pltpu.VMEM((wide - 2, nz, ny), F32),
    ]
    alias = {}
    shapes = [prior.shape]
    if chunk:
        velocity, _, lap0, adv0 = before
        args += [pltpu.with_memory_space_constraint(x, pltpu.HBM) for x in (*halo, lap0, adv0)] + [after, velocity]
        specs += [hbm] * 4 + [anywhere, hbm]
        args[2:4] = [pltpu.with_memory_space_constraint(x, pltpu.HBM) for x in (prior, flow)]
        specs[2:4] = [hbm, hbm]
        alias = {len(args) - 1: 0}
        scratch += [pltpu.VMEM(padded, F32)] * 2 + [pltpu.VMEM(halo[0].shape, BF16)] * 2
        scratch += [pltpu.VMEM((part, layers, nz, ny), F32), pltpu.SemaphoreType.DMA((5,))]
        shapes += [(8, ny)]
    else:
        args += [*halo, after]
        specs += [VMEM] * 2 + [anywhere]
        shapes += [(64, ny), padded, padded]
    return pl.pallas_call(
        functools.partial(sweep_kernel, chunk),
        grid=(STEPS,),
        in_specs=specs,
        out_specs=[pl.BlockSpec((part // STEPS, layers, nz, ny), lambda i: (place * STEPS + i, 0, 0, 0))] + [VMEM] * (len(shapes) - 1),
        out_shape=[jax.ShapeDtypeStruct(shape, F32) for shape in shapes],
        input_output_aliases=alias,
        scratch_shapes=scratch,
        compiler_params=params(),
        name=f"sweeps{chunk}",
    )(*args)


def anomaly_kernel(members_all, prior_ref, a_ref, b_ref, *refs):
    out_ref = refs[-1]
    members, _, nz, ny = prior_ref.shape
    flat = prior_ref.reshape(members * nz, ny)
    mean = (a_ref[0] + b_ref[0]) / members_all
    for z in range(nz):
        rows = flat[pl.ds(z, members, stride=nz), :]
        out_ref[z] = (rows - mean[z : z + 1]).astype(BF16)


def anomalies(prior, totals, members_all, *after):
    members, layers, nz, ny = prior.shape
    total = pl.BlockSpec((1, nz, ny), lambda l: (l, 0, 0))
    return pl.pallas_call(
        functools.partial(anomaly_kernel, members_all),
        grid=(layers,),
        in_specs=[pl.BlockSpec((members, 1, nz, ny), lambda l: (0, l, 0, 0))] + [total] * 2 + [pl.BlockSpec(memory_space=pl.ANY)] * len(after),
        out_specs=pl.BlockSpec((nz, members, ny), lambda l: (l, 0, 0)),
        out_shape=jax.ShapeDtypeStruct((layers * nz, members, ny), BF16),
        compiler_params=params(),
        name="anomalies",
    )(prior, *totals, *after)


def slots_kernel(probes, slot_ref, value_ref, var_ref, noise_ref, after, seen_ref, weight_ref, stack):
    members, count = noise_ref.shape
    stack[...] = jnp.zeros_like(stack)
    stack[0:members] = noise_ref[...]
    stack[members : members + 1] = value_ref[...]
    stack[members + 1 : members + 2] = var_ref[...]
    slot = slot_ref[...]
    place = lax.rem(slot, probes) * (count // probes) + slot // probes
    row = lax.broadcasted_iota(jnp.int32, (count, count), 0)
    chosen = jnp.where(row == place, 1.0, 0.0)
    ordered = lax.dot_general(
        chosen, stack[...], (((1,), (1,)), ((), ())), precision=lax.Precision.HIGHEST, preferred_element_type=F32
    )
    value = ordered[:, members : members + 1]
    var = ordered[:, members + 1 : members + 2]
    seen_ref[...] = value + jnp.sqrt(var) * ordered
    weight_ref[...] = jnp.broadcast_to(1.0 / var, weight_ref.shape)


def in_slots(slot, value, var, noise, probes, after):
    count = slot.shape[0]
    shape = jax.ShapeDtypeStruct((count, 128), F32)
    return pl.pallas_call(
        functools.partial(slots_kernel, probes),
        in_specs=[VMEM] * 4 + [pl.BlockSpec(memory_space=pl.ANY)],
        out_specs=[VMEM] * 2,
        out_shape=[shape, shape],
        scratch_shapes=[pltpu.VMEM((128, count), F32)],
        cost_estimate=pl.CostEstimate(flops=0, bytes_accessed=1 << 26, transcendentals=0),
        compiler_params=params(),
        name="slots",
    )(slot[None], value[None], var[None], noise, after)


def dot(a, b, dims):
    return lax.dot_general(a, b, (dims, ((), ())), precision=lax.Precision.HIGHEST, preferred_element_type=F32)


def solve_kernel(members, here, me_ref, vals_ref, seen_ref, weight_ref, beside_any, prior_hbm, out_ref, beside_ref, prior_ref, scr, sems):
    fetches = [
        pltpu.make_async_copy(beside_any, beside_ref, sems.at[0]),
        pltpu.make_async_copy(prior_hbm, prior_ref, sems.at[1]),
    ]
    for fetch in fetches:
        fetch.start()
    devices, ny = vals_ref.shape
    groups = members // here
    tiles = devices // groups
    probes = 64 // here
    lane = lax.broadcasted_iota(jnp.int32, (tiles, ny), 1)
    parts = [vals_ref[pl.ds(g, tiles, stride=groups), :] for g in range(groups)]
    slabs = []
    for s in range(probes):
        slab = jnp.zeros((tiles, ny), F32)
        for g in range(groups):
            shift = (g - s) * here % ny
            moved = pltpu.roll(parts[g], shift, 1) if shift else parts[g]
            slab = jnp.where((lane >= g * here) & (lane < (g + 1) * here), moved, slab)
        slabs.append(slab)
    predicted = jnp.concatenate(slabs, axis=0)
    lanes = lax.broadcasted_iota(jnp.int32, predicted.shape, 1)
    mean = jnp.sum(predicted, axis=1, keepdims=True) / members
    spread = jnp.where(lanes < members, predicted - mean, 0.0)
    scaled = (spread * weight_ref[...]).T
    gram = dot(scaled, spread, ((1,), (0,)))
    rhs = dot(scaled, seen_ref[...] - predicted, ((1,), (0,)))
    half = 0.5 * jnp.max(jnp.sum(jnp.abs(gram), axis=1))
    alpha = 1.0 / (members - 1.0 + half)
    diagonal = lax.broadcasted_iota(jnp.int32, gram.shape, 0) == lax.broadcasted_iota(jnp.int32, gram.shape, 1)
    error = (jnp.where(diagonal, alpha * half, 0.0) - alpha * gram)[:members]
    rest = jnp.zeros((ny - members, 2 * ny), F32)

    def more(state):
        return (state[0] > 2e-6) & (state[1] < 40)

    def double(state):
        size, count, power_of, x = state
        right = jnp.concatenate([jnp.concatenate([power_of, x], axis=1), rest], axis=0)
        both = dot(power_of, right, ((1,), (0,)))
        return size * size, count + 1, both[:, :ny], x + both[:, ny:]

    x = lax.while_loop(more, double, (half * alpha, 0, error, alpha * rhs[:members]))[3]
    me = me_ref[0]
    scr[0:members] = x
    order = [scr[pl.ds(pl.multiple_of((me ^ g) * here, here), here), :] for g in range(groups)]
    scr[...] = jnp.concatenate(order + [jnp.zeros((ny - members, ny), F32)], axis=0).T
    mine = scr[pl.ds(pl.multiple_of(me * here, here), here), :]
    out_ref[...] = mine[:, :members].astype(BF16)
    for fetch in fetches:
        fetch.wait()


def solve(vals, seen, weight, me, members, here, beside, prior):
    return pl.pallas_call(
        functools.partial(solve_kernel, members, here),
        in_specs=[SMEM] + [VMEM] * 3 + [pl.BlockSpec(memory_space=pl.ANY), pl.BlockSpec(memory_space=pltpu.HBM)],
        out_specs=[VMEM] * 3,
        out_shape=[
            jax.ShapeDtypeStruct((here, members), BF16),
            jax.ShapeDtypeStruct(beside.shape, BF16),
            jax.ShapeDtypeStruct(prior.shape, F32),
        ],
        scratch_shapes=[pltpu.VMEM((128, 128), F32), pltpu.SemaphoreType.DMA((2,))],
        compiler_params=params(),
        name="solve",
    )(me, vals, seen, weight, beside, pltpu.with_memory_space_constraint(prior, pltpu.HBM))


def update_kernel(weights_ref, prior_ref, *refs):
    blocks, (out_hbm, out_ref, sems) = refs[:4], refs[4:]
    here, layers, nz, ny = prior_ref.shape
    members = weights_ref.shape[1]
    tall = (here * ROWS, here)
    spread = lax.broadcasted_iota(jnp.int32, tall, 0) // ROWS == lax.broadcasted_iota(jnp.int32, tall, 1)
    wide = (members, members * ROWS)
    column = lax.broadcasted_iota(jnp.int32, wide, 1)
    source = column // (here * ROWS) * here + column % here
    repeat = lax.broadcasted_iota(jnp.int32, wide, 0) == source
    lhs = jnp.dot(jnp.where(spread, 1.0, 0.0).astype(BF16), weights_ref[...], preferred_element_type=F32)
    lhs = jnp.dot(lhs.astype(BF16), jnp.where(repeat, 1.0, 0.0).astype(BF16), preferred_element_type=F32)
    row = lax.broadcasted_iota(jnp.int32, lhs.shape, 0)
    column = lax.broadcasted_iota(jnp.int32, lhs.shape, 1)
    lhs = jnp.where(row % ROWS == column // here % ROWS, lhs, 0.0).astype(BF16)
    places = [(l, z) for l in range(layers) for z in range(0, nz, ROWS)]
    stores = []
    for p in range(0, len(places), 2):
        pair = places[p : p + 2]
        sides = []
        for l, z in pair:
            first = l * nz + z
            sides.append(jnp.concatenate([b[first : first + ROWS].reshape(ROWS * here, ny) for b in blocks], axis=0))
        update = jnp.dot(lhs, jnp.concatenate(sides, axis=1), preferred_element_type=F32)
        for i, (l, z) in enumerate(pair):
            part = update[:, i * ny : (i + 1) * ny]
            for m in range(here):
                out_ref[m, l, z : z + ROWS] = prior_ref[m, l, z : z + ROWS] + part[m * ROWS : (m + 1) * ROWS]
            if z + ROWS == nz:
                stores.append(pltpu.make_async_copy(out_ref.at[:, l], out_hbm.at[:, l], sems.at[l]))
                stores[-1].start()
    for store in stores:
        store.wait()


def updated(weights, prior, mine, beside, over, far):
    layers = prior.shape[1]
    return pl.pallas_call(
        update_kernel,
        in_specs=[VMEM] * 6,
        out_specs=pl.BlockSpec(memory_space=pltpu.HBM),
        out_shape=jax.ShapeDtypeStruct(prior.shape, F32),
        scratch_shapes=[pltpu.VMEM(prior.shape, F32), pltpu.SemaphoreType.DMA((layers,))],
        compiler_params=params(),
        name="update",
    )(weights, prior, mine, beside, over, far)


def per_device(prior, base_flow, base_visc, probe_cells, obs_slot, obs_values, obs_var, obs_noise):
    here = prior.shape[0]
    tiles, groups = lax.axis_size("tile"), lax.axis_size("mem")
    members = here * groups
    me = lax.axis_index("mem").astype(jnp.int32).reshape(1)

    odd = (lax.axis_index("tile") & 1).astype(jnp.int32).reshape(1)

    def swap(x, first):
        pairs = [((first + 2 * i) % tiles, (first + 2 * i + 1) % tiles) for i in range(tiles // 2)]
        return lax.ppermute(x, "tile", pairs + [(b, a) for a, b in pairs])

    def across(x, bits):
        return lax.ppermute(x, "mem", [(i, i ^ bits) for i in range(groups)])

    *sent, near = encode(odd, prior, base_flow, base_visc)
    halos = [(swap(sent[2 * c], 0), swap(sent[2 * c + 1], 1)) for c in range(CHUNKS)]
    fields = (odd, near, base_flow, base_visc, probe_cells)
    seen, weight = in_slots(obs_slot, obs_values, obs_var, obs_noise, probe_cells.shape[1], sent[0])
    first = sweeps(*fields, halos[0], 0, after=seen)
    payload, token = probes(odd, near, base_visc, probe_cells, halos[1], first, tiles * groups)
    velocity, done = sweeps(odd, prior, *fields[2:], halos[1], 1, first, token)
    total = total_of(near, sent[0])
    chip = pair_sum(total, across(total, 1))
    totals = [chip, across(chip, 2)]
    mine = anomalies(near, totals, float(members), first[1], *halos[1])
    beside = across(mine, 1)
    over = across(mine, 2)
    vals = lax.all_to_all(payload, ("tile", "mem"), 0, 0, tiled=True)
    over = held(over, vals, done)
    far = across(over, 1)
    weights, beside, near_prior = solve(vals, seen, weight, me, members, here, beside, prior)
    return velocity, updated(weights, near_prior, mine, beside, over, far)


def solution(mesh):
    placed = (
        P("mem", "tile", None, None),
        P("tile", None, None),
        P("tile", None, None),
        P("tile", None),
        P(),
        P(),
        P(),
        P(),
    )
    return jax.shard_map(
        per_device,
        mesh=mesh,
        in_specs=placed,
        out_specs=(P("mem", "tile", None, None), P("mem", "tile", None, None)),
        check_vma=False,
    )
```
